128 devices in a mesh: band: 4 (over x_hi, core), dom: 32 (over z, y, x_lo).
Axes of the slice: x: 4 (x_hi: 2, x_lo: 2; x = x_hi * 2 + x_lo), y: 4, z: 4, core: 2. Of those that a mesh axis runs over, the one named last changes fastest.
Arguments:
- orbitals: float32 [128, 32, 48, 512], P('dom', None, None, 'band'), may hold values from -6 to 6
- potential: float32 [128, 32, 48], P('dom'), may hold values from -1 to 2
- projectors: float32 [256, 4, 4608], P('dom'), may hold values from -0.09375 to 0.09375
- coupling: float32 [256, 4, 4], P('dom'), may hold values from -4 to 4
- atom_plane: int32 [256], P('dom'), may hold values from 0 to 127, as said below
- projector_count: int32 [256], P('dom'), may hold values from 1 to 4
Outputs:
- filtered: float32 [128, 32, 48, 512], P('dom', None, None, 'band')
- gram: float32 [512, 512], replicated
The draws below stay inside these ranges and needn't reach their ends.
Inputs may be any that keep to these rules, and one draw needn't show every extreme that they name: `atom_plane`: atom a's first plane lies among the 4 planes of dom index a // 8, that is from (a // 8) * 4 to (a // 8) * 4 + 3; the last atom of each dom index starts on that index's last plane.
All inputs are finite; a program needn't handle non-finite values.
Results may differ from the reference program's by a relative error of at most 0.0003.
Values sent between devices are 32-bit elements; how exact they have to be, the bound alone decides.
A program may use at most 192 MiB of HBM per device.

```python
import jax
import jax.numpy as jnp
from jax import lax

NORB = 512
CX = 4
NY = 32
NZ = 48
SPAN = 3
MAXPROJ = 4
ATOM_DEV = 8
ATOMS = 256
NX = 128


def draw_atom_plane(key, part):
    key = jax.random.fold_in(key, 11)
    atom_ids = jnp.arange(ATOMS, dtype=jnp.int32)
    owners = atom_ids // ATOM_DEV
    offsets = jax.random.randint(key, (ATOMS,), 0, CX, dtype=jnp.int32)
    is_last = atom_ids % ATOM_DEV == ATOM_DEV - 1
    offsets = jnp.where(is_last, CX - 1, offsets)
    offsets = offsets.at[0].set(0)
    return owners * CX + offsets


def draw_projector_count(key, part):
    key = jax.random.fold_in(key, 23)
    counts = jax.random.randint(key, (ATOMS,), 1, MAXPROJ + 1, dtype=jnp.int32)
    return counts.at[0].set(MAXPROJ).at[1].set(1)


def block_levels(key, extent, cuts, smallest, top_value):
    factor_of, own = 1.0, jax.random.fold_in(key, 6)
    for axis_at, parts in cuts:
        heights = jnp.exp(jax.random.uniform(jax.random.fold_in(own, axis_at), (parts,), jnp.float32, smallest / len(cuts), top_value / len(cuts)))
        factor_of = factor_of * jnp.repeat(heights, extent[axis_at] // parts).reshape([-1 if axis == axis_at else 1 for axis in range(len(extent))])
    return factor_of


def centred(stream_key, extent, scale, bound, pieces=(), kind=jnp.bfloat16):
    result = scale * jax.random.normal(stream_key, extent, jnp.float32)
    if pieces:
        result = result * block_levels(stream_key, extent, pieces, -0.22, 0.18)
    return jnp.clip(result, -bound, bound).astype(kind)


def setup_inputs(seed: int = 0) -> dict:
    streams_of = jax.random.split(jax.random.key(seed), 7)
    return {
        "orbitals": centred(streams_of[0], (NX, NY, NZ, NORB), 1.0, 6.0, ((0, 32), (3, 4)), jnp.float32),
        "potential": jnp.clip(-1.0 + 3.0 * jax.random.uniform(streams_of[1], (NX, NY, NZ), jnp.float32) ** block_levels(streams_of[1], (NX, NY, NZ), ((0, 32),), -0.2, 0.2), -1.0, 2.0),
        "projectors": centred(streams_of[2], (ATOMS, MAXPROJ, SPAN * NY * NZ), (SPAN * NY * NZ) ** -0.5, 0.09375, ((0, 32),), jnp.float32),
        "coupling": centred(streams_of[3], (ATOMS, MAXPROJ, MAXPROJ), 1.0, 4.0, ((0, 32),), jnp.float32),
        "atom_plane": draw_atom_plane(jax.random.fold_in(streams_of[6], 71), 0),
        "projector_count": draw_projector_count(jax.random.fold_in(streams_of[6], 71), 0),
    }


center_weight = -205.0 / 72.0
side_weights = (8.0 / 5.0, -1.0 / 5.0, 8.0 / 315.0, -1.0 / 560.0)
HIGH = lax.Precision.HIGHEST

def laplacian(orbital_field):
    total = 3.0 * center_weight * orbital_field
    for offset in range(1, 5):
        weight = side_weights[offset - 1]
        for axis_number in range(3):
            total = total + weight * (jnp.roll(orbital_field, offset, axis_number) + jnp.roll(orbital_field, -offset, axis_number))
    return total

def nonlocal_term(orbital_field, projectors, coupling, atom_plane, projector_count):
    padded = jnp.concatenate([orbital_field, orbital_field[:SPAN - 1]], axis=0)
    slots = jnp.arange(MAXPROJ, dtype=jnp.int32)

    def one_atom(accumulated, inputs):
        beta, couple, first_plane, count = inputs
        live_mask = (slots < count).astype(jnp.float32)
        window_cells = lax.dynamic_slice_in_dim(padded, first_plane.astype(jnp.int32), SPAN, 0).reshape(SPAN * NY * NZ, NORB)
        correlations = jnp.dot(beta.astype(jnp.float32), window_cells.astype(jnp.float32), precision=HIGH, preferred_element_type=jnp.float32) * live_mask[:, None]
        sym_coupling = 0.5 * (couple + couple.T)
        weighted = jnp.dot(sym_coupling.astype(jnp.float32), correlations.astype(jnp.float32), precision=HIGH, preferred_element_type=jnp.float32) * live_mask[:, None]
        added = jnp.dot(beta.T.astype(jnp.float32), weighted.astype(jnp.float32), precision=HIGH, preferred_element_type=jnp.float32).reshape(SPAN, NY, NZ, NORB)
        current = lax.dynamic_slice_in_dim(accumulated, first_plane.astype(jnp.int32), SPAN, 0)
        accumulated = lax.dynamic_update_slice_in_dim(accumulated, current + added, first_plane.astype(jnp.int32), 0)
        return (accumulated, None)
    accumulated, _ = lax.scan(one_atom, jnp.zeros_like(padded), (projectors, coupling, atom_plane, projector_count))
    head = accumulated[:SPAN - 1] + accumulated[NX:]
    return jnp.concatenate([head, accumulated[SPAN - 1:NX]], axis=0)

def hamiltonian(orbital_field, potential, projectors, coupling, atom_plane, projector_count):
    return -0.5 * laplacian(orbital_field) + potential[:, :, :, None] * orbital_field + nonlocal_term(orbital_field, projectors, coupling, atom_plane, projector_count)

def reference(orbitals, potential, projectors, coupling, atom_plane, projector_count):
    extra = (potential, projectors, coupling, atom_plane, projector_count)
    first = (hamiltonian(orbitals, *extra) - 7.0 * orbitals) / 6.0
    second = 2.0 * (hamiltonian(first, *extra) - 7.0 * first) / 6.0 - orbitals
    flat = second.reshape(NX * NY * NZ, NORB)
    gram = jnp.dot(flat.T.astype(jnp.float32), flat.astype(jnp.float32), precision=HIGH, preferred_element_type=jnp.float32) * (1.0 / (NX * NY * NZ))
    lower = jnp.linalg.cholesky(gram)
    inverse = jax.scipy.linalg.solve_triangular(lower, jnp.eye(NORB, dtype=jnp.float32), lower=True)
    filtered = jnp.dot(flat.astype(jnp.float32), inverse.T.astype(jnp.float32), precision=HIGH, preferred_element_type=jnp.float32)
    return (filtered.reshape(NX, NY, NZ, NORB), gram)
```

```python
import functools

import jax
import jax.numpy as jnp
from jax import lax
from jax.experimental import pallas as pl
from jax.experimental.pallas import tpu as pltpu
from jax.sharding import PartitionSpec as P

NORB = 512
HALO = 4
SPAN = 3
MAXPROJ = 4


center_weight = -205.0 / 72.0
side_weights = (8.0 / 5.0, -1.0 / 5.0, 8.0 / 315.0, -1.0 / 560.0)
HIGH = lax.Precision.HIGHEST


B = 128
HIGHEST = lax.Precision.HIGHEST


def dot_f32(a, b, dims):
    return lax.dot_general(a, b, (dims, ((), ())), precision=HIGHEST, preferred_element_type=jnp.float32)


def block_inverse(tiles):
    count = len(tiles)
    tiles = list(tiles)
    shape = tiles[0].shape
    lane = lax.broadcasted_iota(jnp.int32, shape, 1)
    sub = lax.broadcasted_iota(jnp.int32, shape, 0)
    done = []
    for j in range(count):
        base = 8 * j
        cols = [
            [jnp.broadcast_to(tiles[t][:, base + k : base + k + 1], shape) for k in range(8)]
            for t in range(j, count)
        ]
        inside = (lane >= base) & (lane < base + 8)
        unit = jnp.where(lane == sub + base, 1.0, 0.0)
        own = jnp.where(inside, unit, tiles[j])
        rows = [jnp.broadcast_to(own[k : k + 1, :], shape) for k in range(8)]
        splat = [
            [jnp.broadcast_to(cols[0][k][i : i + 1, :], shape) if i >= k else None for k in range(8)]
            for i in range(8)
        ]
        rest = [jnp.where(inside, 0.0, tiles[t]) for t in range(j + 1, count)]
        result = jnp.zeros(shape, jnp.float32)
        for k in range(8):
            scale = lax.rsqrt(splat[k][k])
            rows[k] = rows[k] * scale
            for i in range(k + 1, 8):
                splat[i][k] = splat[i][k] * scale
            for i in range(k + 1, 8):
                for m in range(k + 1, i + 1):
                    splat[i][m] = splat[i][m] - splat[i][k] * splat[m][k]
                rows[i] = rows[i] - splat[i][k] * rows[k]
            for t in range(len(rest)):
                below = cols[t + 1]
                below[k] = below[k] * scale
                for m in range(k + 1, 8):
                    below[m] = below[m] - below[k] * splat[m][k]
                rest[t] = rest[t] - below[k] * rows[k]
            result = jnp.where(sub == k, rows[k], result)
        done.append(jnp.where(lane <= sub + base, result, 0.0))
        tiles[j + 1 :] = rest
    return done


def factor_kernel(gram_ref, inverse_ref, work):
    size = work.shape[0]
    work[...] = gram_ref[...]

    def step(k, carry):
        at = pl.ds(pl.multiple_of(k * B, B), B)
        tiles = [work[pl.ds(pl.multiple_of(k * B + 8 * t, 8), 8), at] for t in range(B // 8)]
        corner = jnp.concatenate(block_inverse(tiles), axis=0)
        row_id = lax.broadcasted_iota(jnp.int32, (size, B), 0)
        column = jnp.where(row_id >= (k + 1) * B, work[:, at], 0.0)
        unit = lax.broadcasted_iota(jnp.int32, (B, B), 0) == lax.broadcasted_iota(jnp.int32, (B, B), 1)
        work[at, at] = jnp.where(unit, 1.0, 0.0)
        below = dot_f32(column, corner, ((1,), (1,)))
        scaled = dot_f32(corner, work[at, :], ((1,), (0,)))
        block = work[:, at]
        work[:, at] = jnp.where(row_id >= (k + 1) * B, 0.0, block)
        work[...] = work[...] - dot_f32(below, scaled, ((1,), (0,)))
        work[at, :] = scaled
        return carry

    lax.fori_loop(0, size // B, step, 0)
    row_id = lax.broadcasted_iota(jnp.int32, (size, size), 0)
    col_id = lax.broadcasted_iota(jnp.int32, (size, size), 1)
    inverse_ref[...] = jnp.where(col_id <= row_id, work[...], 0.0)


def inverse_factor(gram):
    size = gram.shape[0]
    return pl.pallas_call(
        factor_kernel,
        out_shape=jax.ShapeDtypeStruct((size, size), jnp.float32),
        in_specs=[pl.BlockSpec(memory_space=pltpu.VMEM)],
        out_specs=pl.BlockSpec(memory_space=pltpu.VMEM),
        scratch_shapes=[pltpu.VMEM((size, size), jnp.float32)],
        compiler_params=pltpu.CompilerParams(vmem_limit_bytes=32 * 2**20),
    )(gram)


MESH = pl.DeviceIdType.MESH
B = 128
NEAR = 8
FAR = 16
SUMMERS = 10


def tri_blocks(size):
    return [(i, j) for i in range(size // B) for j in range(i + 1)]


def sum_kernel(factor, part_ref, gram_ref, pack, near, mine, far, total, near_s, near_r, far_s, far_r, out_s, out_r, end_s, end_r):
    band, dom = lax.axis_index("band"), lax.axis_index("dom")
    pair, half = dom // 2, dom % 2
    rank = half * 4 + band
    blocks = tri_blocks(part_ref.shape[0])
    share = len(blocks) * B // NEAR
    piece = share // SUMMERS

    def near_peer(step):
        other = (rank + step) % NEAR
        return other, (other % 4, pair * 2 + other // 4)

    def far_peer(step):
        other = (pair + step) % FAR
        return other, (band, other * 2 + half)

    barrier = pltpu.get_barrier_semaphore()
    for step in range(1, NEAR):
        pl.semaphore_signal(barrier, inc=1, device_id=near_peer(step)[1], device_id_type=MESH)
    for step in range(1, FAR):
        pl.semaphore_signal(barrier, inc=1, device_id=far_peer(step)[1], device_id_type=MESH)
    for n, (i, j) in enumerate(blocks):
        pack[n * B : (n + 1) * B, :] = part_ref[i * B : (i + 1) * B, j * B : (j + 1) * B]
    pl.semaphore_wait(barrier, NEAR + FAR - 2)

    def rows(index, count):
        return pl.ds(pl.multiple_of(index * count, 8), count)

    def near_copy(step):
        other, device = near_peer(step)
        return pltpu.make_async_remote_copy(
            src_ref=pack.at[rows(other, share)], dst_ref=near.at[rank],
            send_sem=near_s.at[step], recv_sem=near_r.at[rank], device_id=device, device_id_type=MESH)

    def near_arrival(step):
        other, device = near_peer(step)
        return pltpu.make_async_remote_copy(
            src_ref=pack.at[rows(other, share)], dst_ref=near.at[other],
            send_sem=near_s.at[step], recv_sem=near_r.at[other], device_id=device, device_id_type=MESH)

    for step in range(1, NEAR):
        near_copy(step).start()
    near[rank] = pack[rows(rank, share), :]
    for step in range(1, NEAR):
        near_arrival(step).wait_recv()
    acc = near[0]
    for n in range(1, NEAR):
        acc = acc + near[n]
    mine[...] = acc

    def far_copy(step, slot):
        other, device = far_peer(step)
        return other, pltpu.make_async_remote_copy(
            src_ref=mine.at[rows(other % SUMMERS, piece)], dst_ref=far.at[pair if slot is None else other],
            send_sem=far_s.at[step], recv_sem=far_r.at[pair if slot is None else other],
            device_id=device, device_id_type=MESH)

    for step in range(1, FAR):
        other, copy = far_copy(step, None)
        pl.when(other < SUMMERS)(copy.start)

    place = rank * share

    def out_rows(index):
        return pl.ds(pl.multiple_of(place + (index % SUMMERS) * piece, 8), piece)

    def out_copy(step):
        other, device = far_peer(step)
        return pltpu.make_async_remote_copy(
            src_ref=total.at[out_rows(pair)], dst_ref=total.at[out_rows(pair)],
            send_sem=out_s.at[step], recv_sem=out_r.at[pair], device_id=device, device_id_type=MESH)

    def out_arrival(step):
        other, device = far_peer(step)
        return other, pltpu.make_async_remote_copy(
            src_ref=total.at[out_rows(other)], dst_ref=total.at[out_rows(other)],
            send_sem=out_s.at[step], recv_sem=out_r.at[other], device_id=device, device_id_type=MESH)

    @pl.when(pair < SUMMERS)
    def _():
        far[pair] = mine[rows(pair % SUMMERS, piece), :]
        for step in range(1, FAR):
            far_copy(step, 1)[1].wait_recv()
        acc = far[0]
        for n in range(1, FAR):
            acc = acc + far[n]
        total[out_rows(pair), :] = acc * factor
        for step in range(1, FAR):
            out_copy(step).start()

    for step in range(1, FAR):
        other, copy = out_arrival(step)
        pl.when(other < SUMMERS)(copy.wait_recv)

    def end_copy(step, slot):
        other, device = near_peer(step)
        at = rows(rank if slot is None else other, share)
        return pltpu.make_async_remote_copy(
            src_ref=total.at[at], dst_ref=total.at[at],
            send_sem=end_s.at[step], recv_sem=end_r.at[rank if slot is None else other],
            device_id=device, device_id_type=MESH)

    for step in range(1, NEAR):
        end_copy(step, None).start()
    for step in range(1, NEAR):
        end_copy(step, 1).wait_recv()
    for n, (i, j) in enumerate(blocks):
        block = total[n * B : (n + 1) * B, :]
        gram_ref[i * B : (i + 1) * B, j * B : (j + 1) * B] = block
        if i != j:
            gram_ref[j * B : (j + 1) * B, i * B : (i + 1) * B] = block.T

    for step in range(1, NEAR):
        near_copy(step).wait_send()
        end_copy(step, None).wait_send()
    for step in range(1, FAR):
        other, copy = far_copy(step, None)
        pl.when(other < SUMMERS)(copy.wait_send)

    @pl.when(pair < SUMMERS)
    def _():
        for step in range(1, FAR):
            out_copy(step).wait_send()


def sum_gram(part, factor):
    size = part.shape[0]
    packed = len(tri_blocks(size)) * B
    share = packed // NEAR
    dma = pltpu.SemaphoreType.DMA
    return pl.pallas_call(
        functools.partial(sum_kernel, factor),
        out_shape=jax.ShapeDtypeStruct((size, size), jnp.float32),
        in_specs=[pl.BlockSpec(memory_space=pltpu.VMEM)],
        out_specs=pl.BlockSpec(memory_space=pltpu.VMEM),
        scratch_shapes=[
            pltpu.VMEM((packed, B), jnp.float32),
            pltpu.VMEM((NEAR, share, B), jnp.float32),
            pltpu.VMEM((share, B), jnp.float32),
            pltpu.VMEM((FAR, share // SUMMERS, B), jnp.float32),
            pltpu.VMEM((packed, B), jnp.float32),
            dma((NEAR,)), dma((NEAR,)), dma((FAR,)), dma((FAR,)),
            dma((FAR,)), dma((FAR,)), dma((NEAR,)), dma((NEAR,)),
        ],
        compiler_params=pltpu.CompilerParams(collective_id=1, has_side_effects=True, vmem_limit_bytes=32 * 2**20),
    )(part)


def with_halo(value, sides, width):
    for axis, dim in sides:
        peers, length = (lax.axis_size(axis), value.shape[dim])
        up = [(i, (i + 1) % peers) for i in range(peers)]
        down = [(j, i) for i, j in up]
        last = lax.slice_in_dim(value, length - width, length, axis=dim)
        first = lax.slice_in_dim(value, 0, width, axis=dim)
        before = lax.ppermute(last, axis, up)
        after = lax.ppermute(first, axis, down)
        value = jnp.concatenate([before, value, after], axis=dim)
    return value


def passed_along(value, axis, steps):
    count = lax.axis_size(axis)
    pairs = [(source, (source + steps) % count) for source in range(count)]
    return lax.ppermute(value, axis, pairs)


def laplacian(orbital_field, padded, planes):
    total = 3.0 * center_weight * orbital_field
    for offset in range(1, 5):
        weight = side_weights[offset - 1]
        total = total + weight * (
            padded[HALO + offset : HALO + offset + planes]
            + padded[HALO - offset : HALO - offset + planes]
        )
        total = total + weight * (
            jnp.roll(orbital_field, offset, 1) + jnp.roll(orbital_field, -offset, 1)
        )
        total = total + weight * (
            jnp.roll(orbital_field, offset, 2) + jnp.roll(orbital_field, -offset, 2)
        )
    return total


def apply_hamiltonian(orbital_field, potential, layout_pieces):
    planes, side_y, side_z, local_orbs = orbital_field.shape
    beta_full, live_mask, sym_coupling = layout_pieces
    padded = with_halo(orbital_field, (("dom", 0),), HALO)
    extended = padded[HALO : HALO + planes + SPAN - 1].reshape(
        planes + SPAN - 1, side_y * side_z, local_orbs
    )
    correlations = (
        jnp.einsum(
            "ajpc,pco->ajo", beta_full, extended, precision=HIGH, preferred_element_type=jnp.float32
        )
        * live_mask[:, :, None]
    )
    weighted = (
        jnp.einsum(
            "aij,ajo->aio",
            sym_coupling,
            correlations,
            precision=HIGH,
            preferred_element_type=jnp.float32,
        )
        * live_mask[:, :, None]
    )
    contrib = jnp.einsum(
        "ajpc,ajo->pco", beta_full, weighted, precision=HIGH, preferred_element_type=jnp.float32
    )
    contrib = contrib.reshape(planes + SPAN - 1, side_y, side_z, local_orbs)
    arrived = passed_along(contrib[planes:], "dom", 1)
    own_planes = contrib[:planes]
    own_planes = jnp.concatenate([own_planes[: SPAN - 1] + arrived, own_planes[SPAN - 1 :]], axis=0)
    kinetic = -0.5 * laplacian(orbital_field, padded, planes)
    return kinetic + potential[:, :, :, None] * orbital_field + own_planes


def shards(orbitals, potential, projectors, coupling, atom_plane, projector_count):
    planes, side_y, side_z, local_orbs = orbitals.shape
    atom_total = projectors.shape[0]
    first_plane = atom_plane - lax.axis_index("dom") * planes
    plane_ids = jnp.arange(planes + SPAN - 1, dtype=jnp.int32)
    span_ids = jnp.arange(SPAN, dtype=jnp.int32)
    onehot = (
        plane_ids[None, None, :] == first_plane[:, None, None] + span_ids[None, :, None]
    ).astype(jnp.float32)
    beta_split = projectors.reshape(atom_total, MAXPROJ, SPAN, side_y * side_z)
    beta_full = jnp.einsum(
        "akp,ajkc->ajpc", onehot, beta_split, precision=HIGH, preferred_element_type=jnp.float32
    )
    slots = jnp.arange(MAXPROJ, dtype=jnp.int32)
    live_mask = (slots[None, :] < projector_count[:, None]).astype(jnp.float32)
    sym_coupling = 0.5 * (coupling + jnp.transpose(coupling, (0, 2, 1)))
    layout_pieces = (beta_full, live_mask, sym_coupling)
    first = (apply_hamiltonian(orbitals, potential, layout_pieces) - 7.0 * orbitals) / 6.0
    second = (
        2.0 * (apply_hamiltonian(first, potential, layout_pieces) - 7.0 * first) / 6.0 - orbitals
    )
    cells = planes * side_y * side_z
    total_cells = cells * lax.axis_size("dom")
    flat = second.reshape(cells, local_orbs)
    panels = lax.all_gather(flat, "band", axis=1, tiled=True)
    quarter = cells // lax.axis_size("band")
    slab = lax.dynamic_slice_in_dim(panels, lax.axis_index("band") * quarter, quarter, 0)
    partial_gram = jnp.dot(slab.T, slab, precision=HIGH, preferred_element_type=jnp.float32)
    gram = sum_gram(partial_gram, 1.0 / total_cells)
    inverse = inverse_factor(gram)
    own_rows = lax.dynamic_slice_in_dim(inverse, lax.axis_index("band") * local_orbs, local_orbs, 0)
    result = jnp.dot(panels, own_rows.T, precision=HIGH, preferred_element_type=jnp.float32)
    return (result.reshape(planes, side_y, side_z, local_orbs), gram)


def solution(mesh):
    placed = (
        P("dom", None, None, "band"),
        P("dom", None, None),
        P("dom", None, None),
        P("dom", None, None),
        P("dom"),
        P("dom"),
    )
    return jax.shard_map(
        shards,
        mesh=mesh,
        in_specs=placed,
        out_specs=(P("dom", None, None, "band"), P()),
        check_vma=False,
    )
```

```python
import functools

import jax
import jax.numpy as jnp
from jax import lax
from jax.experimental import pallas as pl
from jax.experimental.pallas import tpu as pltpu
from jax.sharding import PartitionSpec as P

NORB = 512
HALO = 4
SPAN = 3
MAXPROJ = 4
B = 128

center_weight = -205.0 / 72.0
side_weights = (8.0 / 5.0, -1.0 / 5.0, 8.0 / 315.0, -1.0 / 560.0)
HIGH = lax.Precision.HIGHEST


HIGHEST = lax.Precision.HIGHEST


def dot_f32(a, b, dims):
    return lax.dot_general(a, b, (dims, ((), ())), precision=HIGHEST, preferred_element_type=jnp.float32)


def block_inverse(tiles):
    count = len(tiles)
    tiles = list(tiles)
    shape = tiles[0].shape
    lane = lax.broadcasted_iota(jnp.int32, shape, 1)
    sub = lax.broadcasted_iota(jnp.int32, shape, 0)
    done = []
    for j in range(count):
        base = 8 * j
        cols = [
            [jnp.broadcast_to(tiles[t][:, base + k : base + k + 1], shape) for k in range(8)]
            for t in range(j, count)
        ]
        inside = (lane >= base) & (lane < base + 8)
        unit = jnp.where(lane == sub + base, 1.0, 0.0)
        own = jnp.where(inside, unit, tiles[j])
        rows = [jnp.broadcast_to(own[k : k + 1, :], shape) for k in range(8)]
        splat = [
            [jnp.broadcast_to(cols[0][k][i : i + 1, :], shape) if i >= k else None for k in range(8)]
            for i in range(8)
        ]
        rest = [jnp.where(inside, 0.0, tiles[t]) for t in range(j + 1, count)]
        result = jnp.zeros(shape, jnp.float32)
        for k in range(8):
            scale = lax.rsqrt(splat[k][k])
            rows[k] = rows[k] * scale
            for i in range(k + 1, 8):
                splat[i][k] = splat[i][k] * scale
            for i in range(k + 1, 8):
                for m in range(k + 1, i + 1):
                    splat[i][m] = splat[i][m] - splat[i][k] * splat[m][k]
                rows[i] = rows[i] - splat[i][k] * rows[k]
            for t in range(len(rest)):
                below = cols[t + 1]
                below[k] = below[k] * scale
                for m in range(k + 1, 8):
                    below[m] = below[m] - below[k] * splat[m][k]
                rest[t] = rest[t] - below[k] * rows[k]
            result = jnp.where(sub == k, rows[k], result)
        done.append(jnp.where(lane <= sub + base, result, 0.0))
        tiles[j + 1 :] = rest
    return done


def factor_kernel(gram_ref, inverse_ref, work):
    size = work.shape[0]
    work[...] = gram_ref[...]

    def step(k, carry):
        at = pl.ds(pl.multiple_of(k * B, B), B)
        tiles = [work[pl.ds(pl.multiple_of(k * B + 8 * t, 8), 8), at] for t in range(B // 8)]
        corner = jnp.concatenate(block_inverse(tiles), axis=0)
        row_id = lax.broadcasted_iota(jnp.int32, (size, B), 0)
        column = jnp.where(row_id >= (k + 1) * B, work[:, at], 0.0)
        unit = lax.broadcasted_iota(jnp.int32, (B, B), 0) == lax.broadcasted_iota(jnp.int32, (B, B), 1)
        work[at, at] = jnp.where(unit, 1.0, 0.0)
        below = dot_f32(column, corner, ((1,), (1,)))
        scaled = dot_f32(corner, work[at, :], ((1,), (0,)))
        block = work[:, at]
        work[:, at] = jnp.where(row_id >= (k + 1) * B, 0.0, block)
        work[...] = work[...] - dot_f32(below, scaled, ((1,), (0,)))
        work[at, :] = scaled
        return carry

    lax.fori_loop(0, size // B, step, 0)
    row_id = lax.broadcasted_iota(jnp.int32, (size, size), 0)
    col_id = lax.broadcasted_iota(jnp.int32, (size, size), 1)
    inverse_ref[...] = jnp.where(col_id <= row_id, work[...], 0.0)


def inverse_factor(gram):
    size = gram.shape[0]
    return pl.pallas_call(
        factor_kernel,
        out_shape=jax.ShapeDtypeStruct((size, size), jnp.float32),
        in_specs=[pl.BlockSpec(memory_space=pltpu.VMEM)],
        out_specs=pl.BlockSpec(memory_space=pltpu.VMEM),
        scratch_shapes=[pltpu.VMEM((size, size), jnp.float32)],
        compiler_params=pltpu.CompilerParams(vmem_limit_bytes=32 * 2**20),
    )(gram)


MESH = pl.DeviceIdType.MESH
NEAR = 8
FAR = 16
SUMMERS = 10


def tri_blocks(size):
    return [(i, j) for i in range(size // B) for j in range(i + 1)]


def sum_kernel(factor, part_ref, gram_ref, pack, near, mine, far, total, near_s, near_r, far_s, far_r, out_s, out_r, end_s, end_r):
    band, dom = lax.axis_index("band"), lax.axis_index("dom")
    pair, half = dom // 2, dom % 2
    rank = half * 4 + band
    blocks = tri_blocks(part_ref.shape[0])
    share = len(blocks) * B // NEAR
    piece = share // SUMMERS

    def near_peer(step):
        other = (rank + step) % NEAR
        return other, (other % 4, pair * 2 + other // 4)

    def far_peer(step):
        other = (pair + step) % FAR
        return other, (band, other * 2 + half)

    barrier = pltpu.get_barrier_semaphore()
    for step in range(1, NEAR):
        pl.semaphore_signal(barrier, inc=1, device_id=near_peer(step)[1], device_id_type=MESH)
    for step in range(1, FAR):
        pl.semaphore_signal(barrier, inc=1, device_id=far_peer(step)[1], device_id_type=MESH)
    for n, (i, j) in enumerate(blocks):
        pack[n * B : (n + 1) * B, :] = part_ref[i * B : (i + 1) * B, j * B : (j + 1) * B]
    pl.semaphore_wait(barrier, NEAR + FAR - 2)

    def rows(index, count):
        return pl.ds(pl.multiple_of(index * count, 8), count)

    def near_copy(step):
        other, device = near_peer(step)
        return pltpu.make_async_remote_copy(
            src_ref=pack.at[rows(other, share)], dst_ref=near.at[rank],
            send_sem=near_s.at[step], recv_sem=near_r.at[rank], device_id=device, device_id_type=MESH)

    def near_arrival(step):
        other, device = near_peer(step)
        return pltpu.make_async_remote_copy(
            src_ref=pack.at[rows(other, share)], dst_ref=near.at[other],
            send_sem=near_s.at[step], recv_sem=near_r.at[other], device_id=device, device_id_type=MESH)

    for step in range(1, NEAR):
        near_copy(step).start()
    near[rank] = pack[rows(rank, share), :]
    for step in range(1, NEAR):
        near_arrival(step).wait_recv()
    acc = near[0]
    for n in range(1, NEAR):
        acc = acc + near[n]
    mine[...] = acc

    def far_copy(step, slot):
        other, device = far_peer(step)
        return other, pltpu.make_async_remote_copy(
            src_ref=mine.at[rows(other % SUMMERS, piece)], dst_ref=far.at[pair if slot is None else other],
            send_sem=far_s.at[step], recv_sem=far_r.at[pair if slot is None else other],
            device_id=device, device_id_type=MESH)

    for step in range(1, FAR):
        other, copy = far_copy(step, None)
        pl.when(other < SUMMERS)(copy.start)

    place = rank * share

    def out_rows(index):
        return pl.ds(pl.multiple_of(place + (index % SUMMERS) * piece, 8), piece)

    def out_copy(step):
        other, device = far_peer(step)
        return pltpu.make_async_remote_copy(
            src_ref=total.at[out_rows(pair)], dst_ref=total.at[out_rows(pair)],
            send_sem=out_s.at[step], recv_sem=out_r.at[pair], device_id=device, device_id_type=MESH)

    def out_arrival(step):
        other, device = far_peer(step)
        return other, pltpu.make_async_remote_copy(
            src_ref=total.at[out_rows(other)], dst_ref=total.at[out_rows(other)],
            send_sem=out_s.at[step], recv_sem=out_r.at[other], device_id=device, device_id_type=MESH)

    @pl.when(pair < SUMMERS)
    def _():
        far[pair] = mine[rows(pair % SUMMERS, piece), :]
        for step in range(1, FAR):
            far_copy(step, 1)[1].wait_recv()
        acc = far[0]
        for n in range(1, FAR):
            acc = acc + far[n]
        total[out_rows(pair), :] = acc * factor
        for step in range(1, FAR):
            out_copy(step).start()

    for step in range(1, FAR):
        other, copy = out_arrival(step)
        pl.when(other < SUMMERS)(copy.wait_recv)

    def end_copy(step, slot):
        other, device = near_peer(step)
        at = rows(rank if slot is None else other, share)
        return pltpu.make_async_remote_copy(
            src_ref=total.at[at], dst_ref=total.at[at],
            send_sem=end_s.at[step], recv_sem=end_r.at[rank if slot is None else other],
            device_id=device, device_id_type=MESH)

    for step in range(1, NEAR):
        end_copy(step, None).start()
    for step in range(1, NEAR):
        end_copy(step, 1).wait_recv()
    for n, (i, j) in enumerate(blocks):
        block = total[n * B : (n + 1) * B, :]
        gram_ref[i * B : (i + 1) * B, j * B : (j + 1) * B] = block
        if i != j:
            gram_ref[j * B : (j + 1) * B, i * B : (i + 1) * B] = block.T

    for step in range(1, NEAR):
        near_copy(step).wait_send()
        end_copy(step, None).wait_send()
    for step in range(1, FAR):
        other, copy = far_copy(step, None)
        pl.when(other < SUMMERS)(copy.wait_send)

    @pl.when(pair < SUMMERS)
    def _():
        for step in range(1, FAR):
            out_copy(step).wait_send()


def sum_gram(part, factor):
    size = part.shape[0]
    packed = len(tri_blocks(size)) * B
    share = packed // NEAR
    dma = pltpu.SemaphoreType.DMA
    return pl.pallas_call(
        functools.partial(sum_kernel, factor),
        out_shape=jax.ShapeDtypeStruct((size, size), jnp.float32),
        in_specs=[pl.BlockSpec(memory_space=pltpu.VMEM)],
        out_specs=pl.BlockSpec(memory_space=pltpu.VMEM),
        scratch_shapes=[
            pltpu.VMEM((packed, B), jnp.float32),
            pltpu.VMEM((NEAR, share, B), jnp.float32),
            pltpu.VMEM((share, B), jnp.float32),
            pltpu.VMEM((FAR, share // SUMMERS, B), jnp.float32),
            pltpu.VMEM((packed, B), jnp.float32),
            dma((NEAR,)), dma((NEAR,)), dma((FAR,)), dma((FAR,)),
            dma((FAR,)), dma((FAR,)), dma((NEAR,)), dma((NEAR,)),
        ],
        compiler_params=pltpu.CompilerParams(collective_id=1, has_side_effects=True, vmem_limit_bytes=32 * 2**20),
    )(part)


PLANES = 8
ROWS = 16
DEPTH = 48
CELLS = ROWS * DEPTH
PROJ = 32
REACH = 6
FLAGS = PROJ


def shift_terms(field, p, r):
    centre = field[p + HALO, r + HALO]
    terms = []
    for k in range(1, 5):
        pair_x = field[p + HALO + k, r + HALO] + field[p + HALO - k, r + HALO]
        pair_y = field[p + HALO, r + HALO + k] + field[p + HALO, r + HALO - k]
        pair_z = pltpu.roll(centre, k, 0) + pltpu.roll(centre, DEPTH - k, 0)
        terms.append((pair_x + pair_y) + pair_z)
    return centre, terms


def split(value):
    high = value.astype(jnp.bfloat16)
    return high, (value - high.astype(jnp.float32)).astype(jnp.bfloat16)


def plane_order(i):
    return lax.rem(i, 2) * 4 + i // 2


def field_kernel(
    orb, pot, proj, info, slab,
    e1, e2, second, shift_pot, nonlocal_plane, left, right, raw, notes, pot_all, corr, corr_in, weights,
    local_s, x_s, x_r, own_s, fwd_s, halo_r, edge_s, edge_r, small_s, small_r, next_s, next_r,
    corr_s, corr_r, y2_s, y2_r, edge2_s, edge2_r, out_s, out_r,
):
    band, dom = lax.axis_index("band"), lax.axis_index("dom")
    pair, half = dom // 2, dom % 2
    other = 1 - half
    pairs = lax.axis_size("dom") // 2
    partner = (band, pair * 2 + other)

    def at_pair(step):
        return (band, lax.rem(pair + step + pairs, pairs) * 2 + half)

    def send(src, dst, ssem, rsem, device):
        return pltpu.make_async_remote_copy(
            src_ref=src, dst_ref=dst, send_sem=ssem, recv_sem=rsem, device_id=device, device_id_type=MESH)

    barrier = pltpu.get_barrier_semaphore()
    for peer in [at_pair(1), at_pair(-1)] + [(b, pair * 2 + other) for b in range(4)]:
        pl.semaphore_signal(barrier, inc=1, device_id=peer, device_id_type=MESH)

    def rows_of(which):
        return pl.ds(pl.multiple_of(which * ROWS, 8), ROWS)

    own_planes = pl.ds(HALO + 4 * half, 4)
    main = pl.ds(HALO, ROWS)

    def edge_rows(which, side):
        return pl.ds(pl.multiple_of(lax.rem(which * ROWS + (28 if side == 0 else 16), 32), 4), 4)

    low, high = pl.ds(0, 4), pl.ds(HALO + ROWS, 4)
    locals_ = [
        pltpu.make_async_copy(orb.at[:, rows_of(half)], e1.at[own_planes, main], local_s.at[0]),
        pltpu.make_async_copy(orb.at[:, edge_rows(half, 0)], e1.at[own_planes, low], local_s.at[1]),
        pltpu.make_async_copy(orb.at[:, edge_rows(half, 1)], e1.at[own_planes, high], local_s.at[2]),
    ]
    for copy in locals_:
        copy.start()

    small = [
        send(pot.at[:, rows_of(other)], pot_all.at[pl.ds(4 * half, 4)], small_s.at[0], small_r.at[0], partner),
        send(info, notes.at[1 + half], small_s.at[1], small_r.at[1], partner),
        send(proj.at[other], raw.at[1 + half], small_s.at[2], small_r.at[2], partner),
    ]
    small_in = [
        send(pot.at[:, rows_of(other)], pot_all.at[pl.ds(4 * other, 4)], small_s.at[0], small_r.at[0], partner),
        send(info, notes.at[1 + other], small_s.at[1], small_r.at[1], partner),
        send(proj.at[other], raw.at[1 + other], small_s.at[2], small_r.at[2], partner),
    ]
    cross = [
        send(orb.at[p, rows_of(other)], e1.at[HALO + 4 * half + p, main], x_s.at[p], x_r.at[p], partner)
        for p in range(4)
    ]
    cross_in = [
        send(orb.at[p, rows_of(other)], e1.at[HALO + 4 * other + p, main], x_s.at[p], x_r.at[p], partner)
        for p in range(4)
    ]
    own = [
        send(orb.at[p, rows_of(half)], e1.at[12 * other + p, main], own_s.at[p], halo_r.at[other, p],
             at_pair(2 * half - 1))
        for p in range(4)
    ]
    forward = [
        send(e1.at[HALO + 4 * other + p, main], e1.at[12 * half + p, main], fwd_s.at[p], halo_r.at[half, p],
             at_pair(1 - 2 * half))
        for p in range(4)
    ]
    halo_in = [
        send(orb.at[p, rows_of(half)], e1.at[12 * side + p, main], own_s.at[p], halo_r.at[side, p], at_pair(1))
        for side in range(2) for p in range(4)
    ]
    edges = [
        send(orb.at[:, edge_rows(other, side)], e1.at[own_planes, (low, high)[side]],
             edge_s.at[side], edge_r.at[side], partner)
        for side in range(2)
    ]
    edges_in = [
        send(orb.at[:, edge_rows(other, side)], e1.at[pl.ds(HALO + 4 * other, 4), (low, high)[side]],
             edge_s.at[side], edge_r.at[side], partner)
        for side in range(2)
    ]
    onward = [
        send(notes.at[2], notes.at[0], next_s.at[0], next_r.at[0], at_pair(1)),
        send(raw.at[2], raw.at[0], next_s.at[1], next_r.at[1], at_pair(1)),
    ]

    notes[1 + half] = info[...]
    raw[1 + half] = proj[half]
    pot_all[pl.ds(4 * half, 4)] = pot[:, rows_of(half)]
    pl.semaphore_wait(barrier, 6)
    for copy in small + cross + own:
        copy.start()
    for copy in small_in:
        copy.wait_recv()
    for copy in onward:
        copy.start()

    diagonal = lax.broadcasted_iota(jnp.int32, (DEPTH, DEPTH), 0) == lax.broadcasted_iota(
        jnp.int32, (DEPTH, DEPTH), 1)
    constant = -1.5 * center_weight - 7.0

    def spread(n, carry):
        p, r = n // ROWS, lax.rem(n, ROWS)
        line = jnp.broadcast_to(pot_all[p, pl.ds(r, 1), :], (DEPTH, DEPTH))
        column = jnp.sum(jnp.where(diagonal, line, 0.0), axis=1, keepdims=True)
        shift_pot[p, r] = jnp.broadcast_to(column, (DEPTH, NORB // 4)) + constant
        return carry

    lax.fori_loop(0, PLANES * ROWS, spread, 0)

    def placed(group, reach):
        total = jnp.zeros((PROJ, CELLS), jnp.float32)
        for k in range(SPAN):
            flag = notes[group, :, FLAGS + reach * SPAN + k : FLAGS + reach * SPAN + k + 1]
            total = total + flag * raw[group, :, k * CELLS : (k + 1) * CELLS]
        return total

    def store_group(group, start, slot, factor_slot):
        for reach in range(REACH):
            beta = placed(group, reach)
            high_part, low_part = split(beta)
            where = start + reach
            left[where + 4, 2 * slot * PROJ : (2 * slot + 1) * PROJ, :] = high_part
            left[where + 4, (2 * slot + 1) * PROJ : (2 * slot + 2) * PROJ, :] = low_part
            if 0 <= where < PLANES:
                wide = jnp.concatenate(
                    [high_part.astype(jnp.float32), low_part.astype(jnp.float32), high_part.astype(jnp.float32),
                     jnp.zeros((PROJ, CELLS), jnp.float32)], axis=0)
                right[where, :, factor_slot * 128 : (factor_slot + 1) * 128] = wide.T.astype(jnp.bfloat16)

    empty = jnp.zeros((2 * PROJ, CELLS), jnp.bfloat16)
    for e in range(14):
        if not 4 <= e < 10:
            left[e, 0 : 2 * PROJ, :] = empty
        if 6 <= e < 8:
            left[e, 2 * PROJ :, :] = empty
    for p in (2, 3, 6, 7):
        right[p, :, (128 if p < 4 else 0) : (256 if p < 4 else 128)] = jnp.zeros((CELLS, 128), jnp.bfloat16)
    store_group(1, 0, 0, 0)
    store_group(2, 4, 1, 1)
    for p in range(4):
        cross_in[p].wait_recv()
        forward[p].start()
        if p == 2:
            for copy in edges:
                copy.start()
    for copy in onward:
        copy.wait_recv()
    store_group(0, -4, 1, 1)
    for copy in locals_:
        copy.wait()
    for copy in halo_in:
        copy.wait_recv()

    def correlate(field, phase):
        def piece(e, total):
            high_part, low_part = split(field[e, main].reshape(CELLS, NORB // 4))
            both = jnp.concatenate([high_part, low_part], axis=1)
            return total + lax.dot_general(
                left[e], both, (((1,), (0,)), ((), ())), preferred_element_type=jnp.float32)

        start = jnp.zeros((4 * PROJ, 2 * (NORB // 4)), jnp.float32)
        first_part = lax.fori_loop(0, 8, piece, start)
        last_part = lax.fori_loop(8, 14, piece, start)

        def join(part, slot):
            at = 2 * slot * PROJ
            wide = part[at : at + PROJ] + part[at + PROJ : at + 2 * PROJ]
            return wide[:, : NORB // 4] + wide[:, NORB // 4 :]

        corr[phase, 0] = join(first_part, 1)
        corr[phase, 1] = join(first_part, 0) + join(last_part, 0)
        corr[phase, 2] = join(last_part, 1)
        copy = send(corr.at[phase], corr_in.at[phase], corr_s.at[phase], corr_r.at[phase], partner)
        copy.start()
        return copy

    def weigh(phase):
        parts = []
        for group in range(3):
            value = corr[phase, group] + corr_in[phase, group]
            value = dot_f32(notes[group, :, :PROJ], value, ((1,), (0,)))
            high_part, low_part = split(value)
            parts.append(jnp.concatenate(
                [high_part, high_part, low_part, jnp.zeros((PROJ, NORB // 4), jnp.bfloat16)], axis=0))
        weights[0] = jnp.concatenate([parts[1], parts[0]], axis=0)
        weights[1] = jnp.concatenate([parts[1], parts[2]], axis=0)

    def apply(field, p, scale, write):
        product = lax.dot_general(
            right[p], weights[p // 4], (((1,), (0,)), ((), ())), preferred_element_type=jnp.float32)
        nonlocal_plane[...] = product.reshape(ROWS, DEPTH, NORB // 4)

        def row(r, carry):
            centre, terms = shift_terms(field, p, r)
            total = centre * shift_pot[p, r] + nonlocal_plane[r]
            for weight, term in zip(side_weights, terms):
                total = total + (-0.5 * weight) * term
            write(p, r, total * scale)
            return carry

        lax.fori_loop(0, ROWS, row, 0)

    copy1 = correlate(e1, 0)
    for copy in edges_in:
        copy.wait_recv()
    copy1.wait_recv()
    weigh(0)

    def write_first(p, r, value):
        e2[p + HALO, r + HALO] = value

    def halo2(p):
        step = 2 * (p // 4) - 1
        return send(e2.at[p + HALO, main], e2.at[lax.rem(p + 12, 16), main], y2_s.at[p], y2_r.at[p], at_pair(step))

    def edge2(p, side):
        source = pl.ds(ROWS, 4) if side == 0 else pl.ds(HALO, 4)
        return send(e2.at[p + HALO, source], e2.at[p + HALO, (low, high)[side]],
                    edge2_s.at[side, p], edge2_r.at[side, p], partner)

    def first_plane(i, carry):
        p = plane_order(i)
        apply(e1, p, 1.0 / 6.0, write_first)
        halo2(p).start()
        edge2(p, 0).start()
        edge2(p, 1).start()
        return carry

    lax.fori_loop(0, PLANES, first_plane, 0)

    def arrive2(p, carry):
        halo2(p).wait_recv()
        return carry

    lax.fori_loop(0, PLANES, arrive2, 0)
    copy2 = correlate(e2, 1)

    def arrive_edges(p, carry):
        edge2(p, 0).wait_recv()
        edge2(p, 1).wait_recv()
        return carry

    lax.fori_loop(0, PLANES, arrive_edges, 0)
    copy2.wait_recv()
    weigh(1)

    def write_second(p, r, value):
        second[p, r] = value - e1[p + HALO, r + HALO]

    def give(p):
        return send(second.at[p], slab.at[band, lax.rem(p, 2)], out_s.at[p], out_r.at[band, lax.rem(p, 2)],
                    (p // 2, pair * 2 + other))

    def second_plane(i, carry):
        p = plane_order(i)
        apply(e2, p, 1.0 / 3.0, write_second)
        give(p).start()
        return carry

    lax.fori_loop(0, PLANES, second_plane, 0)

    for b in range(4):
        for n in range(2):
            send(second.at[0], slab.at[b, n], out_s.at[0], out_r.at[b, n], partner).wait_recv()
    for copy in small + cross + own + forward + edges + onward + [copy1, copy2]:
        copy.wait_send()

    def drain(p, carry):
        halo2(p).wait_send()
        edge2(p, 0).wait_send()
        edge2(p, 1).wait_send()
        give(p).wait_send()
        return carry

    lax.fori_loop(0, PLANES, drain, 0)


def filtered_slab(orbitals, potential, projectors, info):
    dma = pltpu.SemaphoreType.DMA
    width = orbitals.shape[3]
    f32, bf16 = jnp.float32, jnp.bfloat16
    vmem = pl.BlockSpec(memory_space=pltpu.VMEM)
    return pl.pallas_call(
        field_kernel,
        out_shape=jax.ShapeDtypeStruct((4, 2, ROWS, DEPTH, width), f32),
        in_specs=[pl.BlockSpec(memory_space=pl.ANY), vmem, vmem, vmem],
        out_specs=vmem,
        scratch_shapes=[
            pltpu.VMEM((PLANES + 2 * HALO, ROWS + 2 * HALO, DEPTH, width), f32),
            pltpu.VMEM((PLANES + 2 * HALO, ROWS + 2 * HALO, DEPTH, width), f32),
            pltpu.VMEM((PLANES, ROWS, DEPTH, width), f32),
            pltpu.VMEM((PLANES, ROWS, DEPTH, width), f32),
            pltpu.VMEM((ROWS, DEPTH, width), f32),
            pltpu.VMEM((14, 4 * PROJ, CELLS), bf16),
            pltpu.VMEM((PLANES, CELLS, 256), bf16),
            pltpu.VMEM((3, PROJ, SPAN * CELLS), f32),
            pltpu.VMEM((3, PROJ, 128), f32),
            pltpu.VMEM((PLANES, ROWS, DEPTH), f32),
            pltpu.VMEM((2, 3, PROJ, width), f32),
            pltpu.VMEM((2, 3, PROJ, width), f32),
            pltpu.VMEM((2, 256, width), bf16),
            dma((3,)), dma((4,)), dma((4,)), dma((4,)), dma((4,)), dma((2, 4)), dma((2,)), dma((2,)),
            dma((3,)), dma((3,)), dma((2,)), dma((2,)),
            dma((2,)), dma((2,)), dma((8,)), dma((8,)), dma((2, 8)), dma((2, 8)), dma((8,)), dma((4, 2)),
        ],
        compiler_params=pltpu.CompilerParams(collective_id=2, has_side_effects=True, vmem_limit_bytes=58 * 2**20),
    )(orbitals, potential, projectors, info)


def home_kernel(result, out, local_s, send_s, recv_s):
    band, dom = lax.axis_index("band"), lax.axis_index("dom")
    pair, half = dom // 2, dom % 2
    barrier = pltpu.get_barrier_semaphore()
    for step in range(1, 8):
        rank = lax.rem(half * 4 + band + step, 8)
        pl.semaphore_signal(
            barrier, inc=1, device_id=(lax.rem(rank, 4), pair * 2 + rank // 4), device_id_type=MESH)
    pl.semaphore_wait(barrier, 7)
    home = pair * 2 + band // 2
    place = lax.rem(band, 2)
    rows = 1 - half

    def target(index, row_half):
        return out.at[pl.ds(index * 2, 2), pl.ds(pl.multiple_of(row_half * ROWS, 8), ROWS)]

    def move(b):
        return pltpu.make_async_remote_copy(
            src_ref=result.at[b], dst_ref=target(place, rows), send_sem=send_s.at[b],
            recv_sem=recv_s.at[place, rows], device_id=(b, home), device_id_type=MESH)

    local = pltpu.make_async_copy(result.at[band], target(place, rows), local_s)
    for b in range(4):
        mine = (b == band) & (home == dom)
        pl.when(jnp.logical_not(mine))(lambda b=b: move(b).start())
        pl.when(mine)(local.start)
    for index in range(2):
        for row_half in range(2):
            mine = (half * 2 + index == band) & (1 - row_half == half)
            arrival = pltpu.make_async_remote_copy(
                src_ref=result.at[0], dst_ref=target(index, row_half), send_sem=send_s.at[0],
                recv_sem=recv_s.at[index, row_half], device_id=(lax.rem(band + 1, 4), dom), device_id_type=MESH)
            pl.when(jnp.logical_not(mine))(arrival.wait_recv)
            pl.when(mine)(local.wait)
    for b in range(4):
        mine = (b == band) & (home == dom)
        pl.when(jnp.logical_not(mine))(lambda b=b: move(b).wait_send())


def send_home(result):
    dma = pltpu.SemaphoreType.DMA
    hbm = pl.BlockSpec(memory_space=pl.ANY)
    return pl.pallas_call(
        home_kernel,
        out_shape=jax.ShapeDtypeStruct((4, 2 * ROWS, DEPTH, result.shape[-1]), jnp.float32),
        in_specs=[hbm],
        out_specs=hbm,
        scratch_shapes=[dma(()), dma((4,)), dma((2, 2))],
        compiler_params=pltpu.CompilerParams(collective_id=3, has_side_effects=True, vmem_limit_bytes=16 * 2**20),
    )(result)


def shards(orbitals, potential, projectors, coupling, atom_plane, projector_count):
    planes, side_y, side_z, local_orbs = orbitals.shape
    atoms = projectors.shape[0]
    first_plane = atom_plane - lax.axis_index("dom") * planes
    reach_ids = jnp.arange(REACH, dtype=jnp.int32)
    span_ids = jnp.arange(SPAN, dtype=jnp.int32)
    flags = (
        reach_ids[None, :, None] == first_plane[:, None, None] + span_ids[None, None, :]
    ).astype(jnp.float32).reshape(atoms, 1, REACH * SPAN)
    flags = jnp.broadcast_to(flags, (atoms, MAXPROJ, REACH * SPAN)).reshape(PROJ, REACH * SPAN)
    slots = jnp.arange(MAXPROJ, dtype=jnp.int32)
    live_mask = (slots[None, :] < projector_count[:, None]).astype(jnp.float32)
    sym_coupling = 0.5 * (coupling + jnp.transpose(coupling, (0, 2, 1)))
    sym_coupling = sym_coupling * live_mask[:, :, None] * live_mask[:, None, :]
    same_atom = jnp.eye(atoms, dtype=jnp.float32)
    blocks = (sym_coupling[:, :, None, :] * same_atom[:, None, :, None]).reshape(PROJ, PROJ)
    info = jnp.concatenate(
        [blocks, flags, jnp.zeros((PROJ, 128 - PROJ - REACH * SPAN), jnp.float32)], axis=1)
    halves = projectors.reshape(PROJ, SPAN, 2, CELLS).transpose(2, 0, 1, 3).reshape(2, PROJ, SPAN * CELLS)
    slab = filtered_slab(orbitals, potential, halves, info)
    total_cells = planes * side_y * side_z * lax.axis_size("dom")
    flat = slab.reshape(4, 2 * CELLS, local_orbs).transpose(1, 0, 2).reshape(2 * CELLS, NORB)
    partial_gram = jnp.dot(flat.T, flat, precision=HIGH, preferred_element_type=jnp.float32)
    gram = sum_gram(partial_gram, 1.0 / total_cells)
    inverse = inverse_factor(gram)
    result = jnp.einsum(
        "co,bpo->bcp", flat, inverse.reshape(4, local_orbs, NORB),
        precision=HIGH, preferred_element_type=jnp.float32,
    )
    filtered = send_home(result.reshape(4, 2, ROWS, DEPTH, local_orbs))
    return (filtered, gram)


def solution(mesh):
    placed = (
        P("dom", None, None, "band"),
        P("dom", None, None),
        P("dom", None, None),
        P("dom", None, None),
        P("dom"),
        P("dom"),
    )
    return jax.shard_map(
        shards,
        mesh=mesh,
        in_specs=placed,
        out_specs=(P("dom", None, None, "band"), P()),
        check_vma=False,
    )
```

```python
import functools

import jax
import jax.numpy as jnp
from jax import lax
from jax.experimental import pallas as pl
from jax.experimental.pallas import tpu as pltpu
from jax.sharding import PartitionSpec as P

NORB = 512
HALO = 4
SPAN = 3
MAXPROJ = 4
B = 128

center_weight = -205.0 / 72.0
side_weights = (8.0 / 5.0, -1.0 / 5.0, 8.0 / 315.0, -1.0 / 560.0)
HIGH = lax.Precision.HIGHEST


HIGHEST = lax.Precision.HIGHEST


def dot_f32(a, b, dims):
    return lax.dot_general(a, b, (dims, ((), ())), precision=HIGHEST, preferred_element_type=jnp.float32)


def block_inverse(tiles):
    count = len(tiles)
    tiles = list(tiles)
    shape = tiles[0].shape
    lane = lax.broadcasted_iota(jnp.int32, shape, 1)
    sub = lax.broadcasted_iota(jnp.int32, shape, 0)
    done = []
    for j in range(count):
        base = 8 * j
        cols = [
            [jnp.broadcast_to(tiles[t][:, base + k : base + k + 1], shape) for k in range(8)]
            for t in range(j, count)
        ]
        inside = (lane >= base) & (lane < base + 8)
        unit = jnp.where(lane == sub + base, 1.0, 0.0)
        own = jnp.where(inside, unit, tiles[j])
        rows = [jnp.broadcast_to(own[k : k + 1, :], shape) for k in range(8)]
        splat = [
            [jnp.broadcast_to(cols[0][k][i : i + 1, :], shape) if i >= k else None for k in range(8)]
            for i in range(8)
        ]
        rest = [jnp.where(inside, 0.0, tiles[t]) for t in range(j + 1, count)]
        result = jnp.zeros(shape, jnp.float32)
        for k in range(8):
            scale = lax.rsqrt(splat[k][k])
            rows[k] = rows[k] * scale
            for i in range(k + 1, 8):
                splat[i][k] = splat[i][k] * scale
            for i in range(k + 1, 8):
                for m in range(k + 1, i + 1):
                    splat[i][m] = splat[i][m] - splat[i][k] * splat[m][k]
                rows[i] = rows[i] - splat[i][k] * rows[k]
            for t in range(len(rest)):
                below = cols[t + 1]
                below[k] = below[k] * scale
                for m in range(k + 1, 8):
                    below[m] = below[m] - below[k] * splat[m][k]
                rest[t] = rest[t] - below[k] * rows[k]
            result = jnp.where(sub == k, rows[k], result)
        done.append(jnp.where(lane <= sub + base, result, 0.0))
        tiles[j + 1 :] = rest
    return done


def factor_kernel(gram_ref, inverse_ref, work):
    size = work.shape[0]
    work[...] = gram_ref[...]

    def step(k, carry):
        at = pl.ds(pl.multiple_of(k * B, B), B)
        tiles = [work[pl.ds(pl.multiple_of(k * B + 8 * t, 8), 8), at] for t in range(B // 8)]
        corner = jnp.concatenate(block_inverse(tiles), axis=0)
        row_id = lax.broadcasted_iota(jnp.int32, (size, B), 0)
        column = jnp.where(row_id >= (k + 1) * B, work[:, at], 0.0)
        unit = lax.broadcasted_iota(jnp.int32, (B, B), 0) == lax.broadcasted_iota(jnp.int32, (B, B), 1)
        work[at, at] = jnp.where(unit, 1.0, 0.0)
        below = dot_f32(column, corner, ((1,), (1,)))
        scaled = dot_f32(corner, work[at, :], ((1,), (0,)))
        block = work[:, at]
        work[:, at] = jnp.where(row_id >= (k + 1) * B, 0.0, block)
        work[...] = work[...] - dot_f32(below, scaled, ((1,), (0,)))
        work[at, :] = scaled
        return carry

    lax.fori_loop(0, size // B, step, 0)
    row_id = lax.broadcasted_iota(jnp.int32, (size, size), 0)
    col_id = lax.broadcasted_iota(jnp.int32, (size, size), 1)
    inverse_ref[...] = jnp.where(col_id <= row_id, work[...], 0.0)


def inverse_factor(gram):
    size = gram.shape[0]
    return pl.pallas_call(
        factor_kernel,
        out_shape=jax.ShapeDtypeStruct((size, size), jnp.float32),
        in_specs=[pl.BlockSpec(memory_space=pltpu.VMEM)],
        out_specs=pl.BlockSpec(memory_space=pltpu.VMEM),
        scratch_shapes=[pltpu.VMEM((size, size), jnp.float32)],
        compiler_params=pltpu.CompilerParams(vmem_limit_bytes=32 * 2**20),
    )(gram)


MESH = pl.DeviceIdType.MESH
NEAR = 8
FAR = 16
SUMMERS = 10


def tri_blocks(size):
    return [(i, j) for i in range(size // B) for j in range(i + 1)]


def sum_kernel(factor, part_ref, gram_ref, high, low, pack, near, mine, far, total, near_s, near_r, far_s, far_r, out_s, out_r, end_s, end_r):
    band, dom = lax.axis_index("band"), lax.axis_index("dom")
    pair, half = dom // 2, dom % 2
    rank = half * 4 + band
    size = part_ref.shape[1]
    blocks = tri_blocks(size)
    share = len(blocks) * B // NEAR
    piece = share // SUMMERS

    def near_peer(step):
        other = (rank + step) % NEAR
        return other, (other % 4, pair * 2 + other // 4)

    def far_peer(step):
        other = (pair + step) % FAR
        return other, (band, other * 2 + half)

    barrier = pltpu.get_barrier_semaphore()
    for step in range(1, NEAR):
        pl.semaphore_signal(barrier, inc=1, device_id=near_peer(step)[1], device_id_type=MESH)
    for step in range(1, FAR):
        pl.semaphore_signal(barrier, inc=1, device_id=far_peer(step)[1], device_id_type=MESH)
    contract = (((0,), (0,)), ((), ()))

    def split_rows(n, carry):
        at = pl.ds(pl.multiple_of(n * 128, 128), 128)
        high[at, :], low[at, :] = split(part_ref[at, :])
        return carry

    lax.fori_loop(0, part_ref.shape[0] // 128, split_rows, 0)
    for i in range(size // B):
        own, wide = slice(i * B, (i + 1) * B), slice(0, (i + 1) * B)
        block_row = lax.dot_general(high[:, own], high[:, wide], contract, preferred_element_type=jnp.float32)
        block_row += lax.dot_general(high[:, own], low[:, wide], contract, preferred_element_type=jnp.float32)
        block_row += lax.dot_general(low[:, own], high[:, wide], contract, preferred_element_type=jnp.float32)
        for j in range(i + 1):
            n = blocks.index((i, j))
            pack[n * B : (n + 1) * B, :] = block_row[:, j * B : (j + 1) * B]
    pl.semaphore_wait(barrier, NEAR + FAR - 2)

    def rows(index, count):
        return pl.ds(pl.multiple_of(index * count, 8), count)

    def near_copy(step):
        other, device = near_peer(step)
        return pltpu.make_async_remote_copy(
            src_ref=pack.at[rows(other, share)], dst_ref=near.at[rank],
            send_sem=near_s.at[step], recv_sem=near_r.at[rank], device_id=device, device_id_type=MESH)

    def near_arrival(step):
        other, device = near_peer(step)
        return pltpu.make_async_remote_copy(
            src_ref=pack.at[rows(other, share)], dst_ref=near.at[other],
            send_sem=near_s.at[step], recv_sem=near_r.at[other], device_id=device, device_id_type=MESH)

    for step in range(1, NEAR):
        near_copy(step).start()
    near[rank] = pack[rows(rank, share), :]
    for step in range(1, NEAR):
        near_arrival(step).wait_recv()
    acc = near[0]
    for n in range(1, NEAR):
        acc = acc + near[n]
    mine[...] = acc

    def far_copy(step, slot):
        other, device = far_peer(step)
        return other, pltpu.make_async_remote_copy(
            src_ref=mine.at[rows(other % SUMMERS, piece)], dst_ref=far.at[pair if slot is None else other],
            send_sem=far_s.at[step], recv_sem=far_r.at[pair if slot is None else other],
            device_id=device, device_id_type=MESH)

    for step in range(1, FAR):
        other, copy = far_copy(step, None)
        pl.when(other < SUMMERS)(copy.start)

    place = rank * share

    def out_rows(index):
        return pl.ds(pl.multiple_of(place + (index % SUMMERS) * piece, 8), piece)

    def out_copy(step):
        other, device = far_peer(step)
        return pltpu.make_async_remote_copy(
            src_ref=total.at[out_rows(pair)], dst_ref=total.at[out_rows(pair)],
            send_sem=out_s.at[step], recv_sem=out_r.at[pair], device_id=device, device_id_type=MESH)

    def out_arrival(step):
        other, device = far_peer(step)
        return other, pltpu.make_async_remote_copy(
            src_ref=total.at[out_rows(other)], dst_ref=total.at[out_rows(other)],
            send_sem=out_s.at[step], recv_sem=out_r.at[other], device_id=device, device_id_type=MESH)

    @pl.when(pair < SUMMERS)
    def _():
        far[pair] = mine[rows(pair % SUMMERS, piece), :]
        for step in range(1, FAR):
            far_copy(step, 1)[1].wait_recv()
        acc = far[0]
        for n in range(1, FAR):
            acc = acc + far[n]
        total[out_rows(pair), :] = acc * factor
        for step in range(1, FAR):
            out_copy(step).start()

    for step in range(1, FAR):
        other, copy = out_arrival(step)
        pl.when(other < SUMMERS)(copy.wait_recv)

    def end_copy(step, slot):
        other, device = near_peer(step)
        at = rows(rank if slot is None else other, share)
        return pltpu.make_async_remote_copy(
            src_ref=total.at[at], dst_ref=total.at[at],
            send_sem=end_s.at[step], recv_sem=end_r.at[rank if slot is None else other],
            device_id=device, device_id_type=MESH)

    for step in range(1, NEAR):
        end_copy(step, None).start()
    for step in range(1, NEAR):
        end_copy(step, 1).wait_recv()
    for n, (i, j) in enumerate(blocks):
        block = total[n * B : (n + 1) * B, :]
        gram_ref[i * B : (i + 1) * B, j * B : (j + 1) * B] = block
        if i != j:
            gram_ref[j * B : (j + 1) * B, i * B : (i + 1) * B] = block.T

    for step in range(1, NEAR):
        near_copy(step).wait_send()
        end_copy(step, None).wait_send()
    for step in range(1, FAR):
        other, copy = far_copy(step, None)
        pl.when(other < SUMMERS)(copy.wait_send)

    @pl.when(pair < SUMMERS)
    def _():
        for step in range(1, FAR):
            out_copy(step).wait_send()


def sum_gram(part, factor):
    cells, size = part.shape
    packed = len(tri_blocks(size)) * B
    share = packed // NEAR
    dma = pltpu.SemaphoreType.DMA
    return pl.pallas_call(
        functools.partial(sum_kernel, factor),
        out_shape=jax.ShapeDtypeStruct((size, size), jnp.float32),
        in_specs=[pl.BlockSpec(memory_space=pltpu.VMEM)],
        out_specs=pl.BlockSpec(memory_space=pltpu.VMEM),
        scratch_shapes=[
            pltpu.VMEM((cells, size), jnp.bfloat16),
            pltpu.VMEM((cells, size), jnp.bfloat16),
            pltpu.VMEM((packed, B), jnp.float32),
            pltpu.VMEM((NEAR, share, B), jnp.float32),
            pltpu.VMEM((share, B), jnp.float32),
            pltpu.VMEM((FAR, share // SUMMERS, B), jnp.float32),
            pltpu.VMEM((packed, B), jnp.float32),
            dma((NEAR,)), dma((NEAR,)), dma((FAR,)), dma((FAR,)),
            dma((FAR,)), dma((FAR,)), dma((NEAR,)), dma((NEAR,)),
        ],
        compiler_params=pltpu.CompilerParams(collective_id=1, has_side_effects=True, vmem_limit_bytes=32 * 2**20),
    )(part)


ROWS = 32
DEPTH = 48
WIDE = 128
CELLS = ROWS * DEPTH
PROJ = 32
REACH = 6
FLAGS = PROJ
GROUP = 8
STRIP = 8
STRIPS = ROWS // STRIP
PIECE = 4
PIECES = ROWS // PIECE
AREA = STRIP * DEPTH


def split(value):
    high = value.astype(jnp.bfloat16)
    return high, (value - high.astype(jnp.float32)).astype(jnp.bfloat16)


def swap(value):
    return pltpu.roll(value, WIDE // 2, value.ndim - 1)


def field_kernel(
    orb, pot, proj, info, out,
    e1, e2, second, shift_pot, nonlocal_plane, left, right, raw, notes, pot_all, corr, corr_in, weights,
    give_cross, give_keep, got_cross, got1, got2, slab,
    local_s, x_s, x_r, own_s, fwd_s, halo_r, small_s, small_r, core_s, core_r, next_s, next_r, last_s, last_r,
    corr_s, corr_r, y2_s, y2_r, out_s, out_r, self_s,
):
    band, dom = lax.axis_index("band"), lax.axis_index("dom")
    pair, half = dom // 2, dom % 2
    other = 1 - half
    core = lax.rem(band, 2)
    rank = half * 4 + band
    pairs = lax.axis_size("dom") // 2
    partner = (band, pair * 2 + other)
    sibling = (band + 1 - 2 * core, dom)

    def at_pair(step):
        return (band, lax.rem(pair + step + pairs, pairs) * 2 + half)

    def send(src, dst, ssem, rsem, device):
        return pltpu.make_async_remote_copy(
            src_ref=src, dst_ref=dst, send_sem=ssem, recv_sem=rsem, device_id=device, device_id_type=MESH)

    def member(index):
        return (lax.rem(index, 4), pair * 2 + index // 4)

    barrier = pltpu.get_barrier_semaphore()
    for peer in [at_pair(1), at_pair(-1)] + [member(lax.rem(rank + n, GROUP)) for n in range(1, GROUP)]:
        pl.semaphore_signal(barrier, inc=1, device_id=peer, device_id_type=MESH)

    loads = [pltpu.make_async_copy(orb.at[p], second.at[p], local_s.at[p]) for p in range(4)]
    for copy in loads:
        copy.start()
    lane = lax.broadcasted_iota(jnp.int32, (DEPTH, WIDE), 1)
    lower = lane < WIDE // 2
    kept = (lane // (WIDE // 2)) == half

    share = pl.ds(pl.multiple_of(core * (PROJ // 2), 16), PROJ // 2)
    twin = pl.ds(pl.multiple_of((1 - core) * (PROJ // 2), 16), PROJ // 2)
    small = [
        send(pot, pot_all.at[pl.ds(4 * half, 4)], small_s.at[0], small_r.at[0], partner),
        send(info, notes.at[1 + half], small_s.at[1], small_r.at[1], partner),
        send(proj.at[share], raw.at[1 + half, share], small_s.at[2], small_r.at[2], partner),
    ]
    small_in = [
        send(pot, pot_all.at[pl.ds(4 * other, 4)], small_s.at[0], small_r.at[0], partner),
        send(info, notes.at[1 + other], small_s.at[1], small_r.at[1], partner),
        send(proj.at[share], raw.at[1 + other, share], small_s.at[2], small_r.at[2], partner),
    ]
    across = send(raw.at[1 + other, share], raw.at[1 + other, share], core_s, core_r, sibling)
    across_in = send(raw.at[1 + other, twin], raw.at[1 + other, twin], core_s, core_r, sibling)
    onward = [
        send(notes.at[2], notes.at[0], next_s.at[0], next_r.at[0], at_pair(1)),
        send(raw.at[2, share], raw.at[0, share], next_s.at[1], next_r.at[1], at_pair(1)),
    ]
    last = send(raw.at[0, share], raw.at[0, share], last_s, last_r, sibling)
    last_in = send(raw.at[0, twin], raw.at[0, twin], last_s, last_r, sibling)

    def piece_rows(c):
        return pl.ds(c * PIECE, PIECE)

    def cross(c):
        at = (slice(None), piece_rows(c))
        return send(give_cross.at[at], got_cross.at[at], x_s.at[c], x_r.at[c], partner)

    def keep(c):
        at = piece_rows(c)
        return send(give_keep.at[:, at], got1.at[other, :, at], own_s.at[c], halo_r.at[other, c],
                    at_pair(2 * half - 1))

    def forward(c):
        at = piece_rows(c)
        return send(got_cross.at[:, at], got1.at[half, :, at], fwd_s.at[c], halo_r.at[half, c],
                    at_pair(1 - 2 * half))

    def halo_in(side, c):
        at = piece_rows(c)
        return send(give_keep.at[:, at], got1.at[side, :, at], own_s.at[c], halo_r.at[side, c], at_pair(1))

    notes[1 + half] = info[...]
    raw[1 + half] = proj[...]
    pot_all[pl.ds(4 * half, 4)] = pot[...]
    for copy in loads:
        copy.wait()
    pl.semaphore_wait(barrier, GROUP + 1)
    for copy in small:
        copy.start()

    def pack_piece(c, carry):
        for n in range(PIECE):
            r = c * PIECE + n
            for j in range(2):
                near, far = second[j, r], second[j + 2, r]
                give_cross[j, r] = jnp.where(kept, swap(near), far)
                give_keep[j, r] = jnp.where(kept, near, swap(far))
        cross(c).start()
        keep(c).start()
        return carry

    lax.fori_loop(0, PIECES, pack_piece, 0)

    for copy in small_in:
        copy.wait_recv()
    across.start()
    for copy in onward[:1]:
        copy.start()

    def placed(group, reach):
        total = jnp.zeros((PROJ, CELLS), jnp.float32)
        for k in range(SPAN):
            flag = notes[group, :, FLAGS + reach * SPAN + k : FLAGS + reach * SPAN + k + 1]
            total = total + flag * raw[group, :, k * CELLS : (k + 1) * CELLS]
        return total

    def store_pair(p, groups, reach, slot):
        beta = jnp.concatenate([placed(group, reach) for group in groups], axis=0)
        high_part, low_part = split(beta)
        both = jnp.concatenate([high_part, low_part], axis=0)
        for n in range(STRIPS):
            left[p, n, slot * 128 : (slot + 1) * 128, :] = both[:, n * AREA : (n + 1) * AREA]
        high32 = high_part.astype(jnp.float32)
        wide = jnp.concatenate([high32, low_part.astype(jnp.float32)], axis=0)
        turned = wide.T.astype(jnp.bfloat16)
        right[p, :, slot * 256 : slot * 256 + 128] = turned
        right[p, :, slot * 256 + 128 : slot * 256 + 192] = turned[:, :64]
        right[p, :, slot * 256 + 192 : slot * 256 + 256] = jnp.zeros((CELLS, 64), jnp.bfloat16)

    diagonal = lax.broadcasted_iota(jnp.int32, (DEPTH, DEPTH), 0) == lax.broadcasted_iota(
        jnp.int32, (DEPTH, DEPTH), 1)
    constant = -1.5 * center_weight - 7.0

    def spread(n, carry):
        p, r = n // ROWS, lax.rem(n, ROWS)
        columns = []
        for extra in (0, 4):
            line = jnp.broadcast_to(pot_all[p + extra, pl.ds(r, 1), :], (DEPTH, DEPTH))
            columns.append(jnp.sum(jnp.where(diagonal, line, 0.0), axis=1, keepdims=True))
        shift_pot[p, r] = jnp.where(lower, columns[0], columns[1]) + constant
        return carry

    def receive_piece(c):
        cross(c).wait_recv()
        forward(c).start()

        def one(n, carry):
            r = c * PIECE + n
            for j in range(2):
                arrived = got_cross[j, r]
                e1[4 + j, r] = jnp.where(kept, second[j, r], arrived)
                e1[6 + j, r] = jnp.where(kept, second[j + 2, r], swap(arrived))
            return carry

        lax.fori_loop(0, PIECE, one, 0)

    for p in (2, 3):
        left[p, :, 128:256, :] = jnp.zeros((STRIPS, 128, AREA), jnp.bfloat16)
        right[p, :, 256:512] = jnp.zeros((CELLS, 256), jnp.bfloat16)
    lax.fori_loop(0, 64, spread, 0)
    across_in.wait_recv()
    onward[1].start()
    receive_piece(0)
    store_pair(0, (1, 2), 0, 0)
    store_pair(1, (1, 2), 1, 0)
    receive_piece(1)
    store_pair(2, (1, 2), 2, 0)
    store_pair(3, (1, 2), 3, 0)
    receive_piece(2)
    for copy in onward:
        copy.wait_recv()
    last.start()
    lax.fori_loop(64, 4 * ROWS, spread, 0)
    receive_piece(3)
    last_in.wait_recv()
    store_pair(0, (0, 1), 4, 1)
    store_pair(1, (0, 1), 5, 1)
    for c in range(4, PIECES):
        receive_piece(c)

    def correlate(field, phase):
        def part(n, total):
            p, strip = n // STRIPS, lax.rem(n, STRIPS)
            cells = field[4 + p, pl.ds(strip * STRIP, STRIP)].reshape(AREA, WIDE)
            both = jnp.concatenate(split(cells), axis=1)
            return total + lax.dot_general(
                left[p, strip], both, (((1,), (0,)), ((), ())), preferred_element_type=jnp.float32)

        total = lax.fori_loop(0, 4 * STRIPS, part, jnp.zeros((256, 2 * WIDE), jnp.float32))
        total = total[:, :WIDE] + total[:, WIDE:]
        near, tail = total[0:64] + total[64:128], total[128:192] + total[192:256]
        corr[phase, 0] = tail[:PROJ]
        corr[phase, 1] = near[PROJ:]
        corr[phase, 2] = near[:PROJ] + swap(tail[PROJ:])
        down = send(corr.at[phase, 0], corr_in.at[phase, 1], corr_s.at[phase, 0], corr_r.at[phase, 1], at_pair(-1))
        up = send(corr.at[phase, 1], corr_in.at[phase, 0], corr_s.at[phase, 1], corr_r.at[phase, 0], at_pair(1))
        down.start()
        up.start()
        return [down, up]

    def weigh(phase, copies):
        for copy in copies:
            copy.wait_recv()
        before = corr[phase, 0] + swap(corr_in[phase, 0])
        after = corr[phase, 1] + swap(corr_in[phase, 1])
        before, own, after = (
            dot_f32(notes[group, :, :PROJ], value, ((1,), (0,)))
            for group, value in ((0, before), (1, corr[phase, 2]), (2, after))
        )
        in_low = lax.broadcasted_iota(jnp.int32, (PROJ, WIDE), 1) < WIDE // 2
        zero = jnp.zeros((64, WIDE), jnp.bfloat16)
        parts = []
        for low_value, high_value in ((own, after), (before, swap(own))):
            value = jnp.concatenate(
                [jnp.where(in_low, low_value, 0.0), jnp.where(in_low, 0.0, high_value)], axis=0)
            high_part, low_part = split(value)
            parts += [high_part, high_part, low_part, zero]
        weights[...] = jnp.concatenate(parts, axis=0)

    def open_strip(field, got, strip):
        def one(n, carry):
            r = strip * STRIP + n
            for j in range(2):
                near, far = field[4 + j, r], field[6 + j, r]
                up, down = got[0, j, r], got[1, j, r]
                field[j, r] = swap(jnp.where(lower, near, up))
                field[2 + j, r] = jnp.where(lower, up, swap(far))
                field[8 + j, r] = swap(jnp.where(lower, down, near))
                field[10 + j, r] = jnp.where(lower, swap(far), down)
            return carry

        lax.fori_loop(0, STRIP, one, 0)

    def apply(field, strip, scale, write):
        def plane(p, carry):
            product = lax.dot_general(
                right[p, pl.ds(pl.multiple_of(strip * AREA, AREA), AREA), :], weights[...],
                (((1,), (0,)), ((), ())), preferred_element_type=jnp.float32)
            nonlocal_plane[...] = product.reshape(STRIP, DEPTH, WIDE)

            def row(n, inner):
                r = strip * STRIP + n
                centre = field[p + 4, r]
                total = centre * shift_pot[p, r] + nonlocal_plane[n]
                for k in range(1, 5):
                    pair_x = field[p + 4 + k, r] + field[p + 4 - k, r]
                    pair_y = field[p + 4, lax.rem(r + k, ROWS)] + field[p + 4, lax.rem(r + ROWS - k, ROWS)]
                    pair_z = pltpu.roll(centre, k, 0) + pltpu.roll(centre, DEPTH - k, 0)
                    total = total + (-0.5 * side_weights[k - 1]) * ((pair_x + pair_y) + pair_z)
                write(p, r, total * scale)
                return inner

            lax.fori_loop(0, STRIP, row, 0)
            return carry

        lax.fori_loop(0, 4, plane, 0)

    copies1 = correlate(e1, 0)

    def halo_strip(strip, carry):
        for side in range(2):
            for n in range(STRIP // PIECE):
                halo_in(side, strip * (STRIP // PIECE) + n).wait_recv()
        open_strip(e1, got1, strip)
        return carry

    lax.fori_loop(0, STRIPS, halo_strip, 0)

    def sent_piece(c, carry):
        cross(c).wait_send()
        keep(c).wait_send()
        forward(c).wait_send()
        return carry

    lax.fori_loop(0, PIECES, sent_piece, 0)
    weigh(0, copies1)

    def write_first(p, r, value):
        e2[p + 4, r] = value

    def strip_rows(strip):
        return pl.ds(strip * STRIP, STRIP)

    def up2(strip):
        at = strip_rows(strip)
        return send(give_cross.at[:, at], got2.at[0, :, at], y2_s.at[0, strip], y2_r.at[0, strip], at_pair(1))

    def down2(strip):
        at = strip_rows(strip)
        return send(give_keep.at[:, at], got2.at[1, :, at], y2_s.at[1, strip], y2_r.at[1, strip], at_pair(-1))

    def first_strip(strip, carry):
        apply(e1, strip, 1.0 / 6.0, write_first)

        def pack(n, inner):
            r = strip * STRIP + n
            for j in range(2):
                near, turned = e2[4 + j, r], swap(e2[6 + j, r])
                give_cross[j, r] = jnp.where(lower, turned, near)
                give_keep[j, r] = jnp.where(lower, near, turned)
            return inner

        lax.fori_loop(0, STRIP, pack, 0)
        up2(strip).start()
        down2(strip).start()
        return carry

    lax.fori_loop(0, STRIPS, first_strip, 0)
    copies2 = correlate(e2, 1)
    weigh(1, copies2)

    def write_second(p, r, value):
        second[p, r] = value - e1[p + 4, r]

    def give(index, part):
        src = second.at[index // 2, pl.ds(lax.rem(index, 2) * 16 + part * STRIP, STRIP)]
        return send(src, slab.at[rank, pl.ds(part * STRIP, STRIP)], out_s.at[index, part], out_r.at[rank, part],
                    member(index))

    def own_part(part):
        src = second.at[rank // 2, pl.ds(lax.rem(rank, 2) * 16 + part * STRIP, STRIP)]
        return pltpu.make_async_copy(src, slab.at[rank, pl.ds(part * STRIP, STRIP)], self_s.at[part])

    def second_strip(strip, carry):
        up2(strip).wait_recv()
        down2(strip).wait_recv()
        open_strip(e2, got2, strip)
        apply(e2, strip, 1.0 / 3.0, write_second)
        part = lax.rem(strip, 2)
        for n in range(4):
            index = 2 * lax.rem(n + rank // 2 + 2, 4) + strip // 2
            pl.when(index != rank)(lambda index=index: give(index, part).start())
        pl.when(lax.rem(rank, 2) == strip // 2)(own_part(part).start)
        return carry

    lax.fori_loop(0, STRIPS, second_strip, 0)

    for n in range(1, GROUP):
        index = lax.rem(rank + n, GROUP)
        for part in range(2):
            send(second.at[0, pl.ds(0, STRIP)], slab.at[index, pl.ds(part * STRIP, STRIP)], out_s.at[index, part],
                 out_r.at[index, part], member(index)).wait_recv()
    own_part(0).wait()
    own_part(1).wait()

    def repack(n, carry):
        cells = pl.ds(pl.multiple_of(n * DEPTH, 8), DEPTH)
        more = pl.ds(pl.multiple_of(CELLS // 2 + n * DEPTH, 8), DEPTH)
        for b in range(4):
            at = slice(b * WIDE, (b + 1) * WIDE)
            here, there = slab[b, n], slab[4 + b, n]
            out[cells, at] = jnp.where(lower, here, swap(there))
            out[more, at] = jnp.where(lower, swap(here), there)
        return carry

    lax.fori_loop(0, ROWS // 2, repack, 0)

    for copy in small + [across, last] + onward + copies1 + copies2:
        copy.wait_send()
    for strip in range(STRIPS):
        up2(strip).wait_send()
        down2(strip).wait_send()
    for n in range(1, GROUP):
        for part in range(2):
            give(lax.rem(rank + n, GROUP), part).wait_send()


def filtered_slab(orbitals, potential, projectors, info):
    dma = pltpu.SemaphoreType.DMA
    f32, bf16 = jnp.float32, jnp.bfloat16
    vmem = pl.BlockSpec(memory_space=pltpu.VMEM)
    block = (ROWS, DEPTH, WIDE)
    return pl.pallas_call(
        field_kernel,
        out_shape=jax.ShapeDtypeStruct((CELLS, NORB), f32),
        in_specs=[pl.BlockSpec(memory_space=pl.ANY), vmem, vmem, vmem],
        out_specs=vmem,
        scratch_shapes=[
            pltpu.VMEM((12,) + block, f32),
            pltpu.VMEM((12,) + block, f32),
            pltpu.VMEM((4,) + block, f32),
            pltpu.VMEM((4,) + block, f32),
            pltpu.VMEM((STRIP, DEPTH, WIDE), f32),
            pltpu.VMEM((4, STRIPS, 256, AREA), bf16),
            pltpu.VMEM((4, CELLS, 512), bf16),
            pltpu.VMEM((3, PROJ, SPAN * CELLS), f32),
            pltpu.VMEM((3, PROJ, 128), f32),
            pltpu.VMEM((8, ROWS, DEPTH), f32),
            pltpu.VMEM((2, 3, PROJ, WIDE), f32),
            pltpu.VMEM((2, 2, PROJ, WIDE), f32),
            pltpu.VMEM((512, WIDE), bf16),
            pltpu.VMEM((2,) + block, f32),
            pltpu.VMEM((2,) + block, f32),
            pltpu.VMEM((2,) + block, f32),
            pltpu.VMEM((2, 2) + block, f32),
            pltpu.VMEM((2, 2) + block, f32),
            pltpu.VMEM((GROUP, ROWS // 2, DEPTH, WIDE), f32),
            dma((4,)), dma((PIECES,)), dma((PIECES,)), dma((PIECES,)), dma((PIECES,)), dma((2, PIECES)),
            dma((3,)), dma((3,)), dma(()), dma(()), dma((2,)), dma((2,)), dma(()), dma(()),
            dma((2, 2)), dma((2, 2)), dma((2, STRIPS)), dma((2, STRIPS)),
            dma((GROUP, 2)), dma((GROUP, 2)), dma((2,)),
        ],
        compiler_params=pltpu.CompilerParams(collective_id=2, has_side_effects=True, vmem_limit_bytes=62 * 2**20),
    )(orbitals, potential, projectors, info)


def home_kernel(flat, inverse, out, parts, turned, local_s, send_s, recv_s):
    band, dom = lax.axis_index("band"), lax.axis_index("dom")
    pair, half = dom // 2, dom % 2
    rank = half * 4 + band
    place, core = (band // 2) * 2 + half, lax.rem(band, 2)
    barrier = pltpu.get_barrier_semaphore()
    for step in range(1, GROUP):
        index = lax.rem(rank + step, GROUP)
        pl.semaphore_signal(
            barrier, inc=1, device_id=(lax.rem(index, 4), pair * 2 + index // 4), device_id_type=MESH)
    high_part, low_part = split(inverse[...])
    turned[0], turned[1] = high_part, low_part

    def target(index):
        return out.at[index // 2, pl.ds(pl.multiple_of(lax.rem(index, 2) * 16, 8), ROWS // 2)]

    def choice(n):
        chip = lax.rem(place + (2, 1, 3, 0)[n // 2], 4)
        return lax.rem(chip, 2), (chip // 2) * 2 + lax.rem(core + 1 + n, 2)

    def move(n):
        to_half, to_band = choice(n)
        return pltpu.make_async_remote_copy(
            src_ref=parts.at[n], dst_ref=target(rank), send_sem=send_s.at[n], recv_sem=recv_s.at[rank],
            device_id=(to_band, pair * 2 + to_half), device_id_type=MESH)

    local = pltpu.make_async_copy(parts.at[GROUP - 1], target(rank), local_s)
    contract = (((1,), (1,)), ((), ()))
    for n in range(GROUP):
        to_half, to_band = choice(n)
        rows = pl.ds(pl.multiple_of(to_band * B, B), B)

        def tile(m, carry, n=n, to_half=to_half, rows=rows):
            size = CELLS // 8
            cells = flat[pl.ds(pl.multiple_of(to_half * (CELLS // 2) + m * size, 8), size), :]
            high_cells, low_cells = split(cells)
            high_rot, low_rot = turned[0, rows, :], turned[1, rows, :]
            both = jnp.concatenate([high_rot, low_rot], axis=0)
            wide = lax.dot_general(high_cells, both, contract, preferred_element_type=jnp.float32)
            more = lax.dot_general(low_cells, high_rot, contract, preferred_element_type=jnp.float32)
            value = wide[:, :B] + (wide[:, B:] + more)
            parts[n, pl.ds(m * (size // DEPTH), size // DEPTH)] = value.reshape(size // DEPTH, DEPTH, WIDE)
            return carry

        lax.fori_loop(0, 4, tile, 0)
        if n == 0:
            pl.semaphore_wait(barrier, GROUP - 1)
        if n < GROUP - 1:
            move(n).start()
        else:
            local.start()
    for step in range(1, GROUP):
        index = lax.rem(rank + step, GROUP)
        pltpu.make_async_remote_copy(
            src_ref=parts.at[0], dst_ref=target(index), send_sem=send_s.at[0], recv_sem=recv_s.at[index],
            device_id=(lax.rem(index, 4), pair * 2 + index // 4), device_id_type=MESH).wait_recv()
    local.wait()
    for n in range(GROUP - 1):
        move(n).wait_send()


def rotate_home(flat, inverse):
    dma = pltpu.SemaphoreType.DMA
    vmem = pl.BlockSpec(memory_space=pltpu.VMEM)
    return pl.pallas_call(
        home_kernel,
        out_shape=jax.ShapeDtypeStruct((4, ROWS, DEPTH, WIDE), jnp.float32),
        in_specs=[vmem, vmem],
        out_specs=pl.BlockSpec(memory_space=pl.ANY),
        scratch_shapes=[
            pltpu.VMEM((GROUP, ROWS // 2, DEPTH, WIDE), jnp.float32),
            pltpu.VMEM((2, NORB, NORB), jnp.bfloat16),
            dma(()), dma((GROUP,)), dma((GROUP,)),
        ],
        compiler_params=pltpu.CompilerParams(collective_id=3, has_side_effects=True, vmem_limit_bytes=40 * 2**20),
    )(flat, inverse)


def shards(orbitals, potential, projectors, coupling, atom_plane, projector_count):
    planes, side_y, side_z, local_orbs = orbitals.shape
    atoms = projectors.shape[0]
    first_plane = atom_plane - lax.axis_index("dom") * planes
    reach_ids = jnp.arange(REACH, dtype=jnp.int32)
    span_ids = jnp.arange(SPAN, dtype=jnp.int32)
    flags = (
        reach_ids[None, :, None] == first_plane[:, None, None] + span_ids[None, None, :]
    ).astype(jnp.float32).reshape(atoms, 1, REACH * SPAN)
    flags = jnp.broadcast_to(flags, (atoms, MAXPROJ, REACH * SPAN)).reshape(PROJ, REACH * SPAN)
    slots = jnp.arange(MAXPROJ, dtype=jnp.int32)
    live_mask = (slots[None, :] < projector_count[:, None]).astype(jnp.float32)
    sym_coupling = 0.5 * (coupling + jnp.transpose(coupling, (0, 2, 1)))
    sym_coupling = sym_coupling * live_mask[:, :, None] * live_mask[:, None, :]
    same_atom = jnp.eye(atoms, dtype=jnp.float32)
    blocks = (sym_coupling[:, :, None, :] * same_atom[:, None, :, None]).reshape(PROJ, PROJ)
    info = jnp.concatenate(
        [blocks, flags, jnp.zeros((PROJ, 128 - PROJ - REACH * SPAN), jnp.float32)], axis=1)
    flat = filtered_slab(orbitals, potential, projectors.reshape(PROJ, SPAN * CELLS), info)
    total_cells = planes * side_y * side_z * lax.axis_size("dom")
    gram = sum_gram(flat, 1.0 / total_cells)
    filtered = rotate_home(flat, inverse_factor(gram))
    return (filtered, gram)


def solution(mesh):
    placed = (
        P("dom", None, None, "band"),
        P("dom", None, None),
        P("dom", None, None),
        P("dom", None, None),
        P("dom"),
        P("dom"),
    )
    return jax.shard_map(
        shards,
        mesh=mesh,
        in_specs=placed,
        out_specs=(P("dom", None, None, "band"), P()),
        check_vma=False,
    )
```

```python
import functools

import jax
import jax.numpy as jnp
from jax import lax
from jax.experimental import pallas as pl
from jax.experimental.pallas import tpu as pltpu
from jax.sharding import PartitionSpec as P

NORB = 512
HALO = 4
SPAN = 3
MAXPROJ = 4
B = 128

center_weight = -205.0 / 72.0
side_weights = (8.0 / 5.0, -1.0 / 5.0, 8.0 / 315.0, -1.0 / 560.0)
HIGH = lax.Precision.HIGHEST


HIGHEST = lax.Precision.HIGHEST


def dot_f32(a, b, dims):
    return lax.dot_general(a, b, (dims, ((), ())), precision=HIGHEST, preferred_element_type=jnp.float32)


def block_inverse(tiles):
    count = len(tiles)
    tiles = list(tiles)
    shape = tiles[0].shape
    lane = lax.broadcasted_iota(jnp.int32, shape, 1)
    sub = lax.broadcasted_iota(jnp.int32, shape, 0)
    done = []
    for j in range(count):
        base = 8 * j
        cols = [
            [jnp.broadcast_to(tiles[t][:, base + k : base + k + 1], shape) for k in range(8)]
            for t in range(j, count)
        ]
        inside = (lane >= base) & (lane < base + 8)
        unit = jnp.where(lane == sub + base, 1.0, 0.0)
        own = jnp.where(inside, unit, tiles[j])
        rows = [jnp.broadcast_to(own[k : k + 1, :], shape) for k in range(8)]
        splat = [
            [jnp.broadcast_to(cols[0][k][i : i + 1, :], shape) if i >= k else None for k in range(8)]
            for i in range(8)
        ]
        rest = [jnp.where(inside, 0.0, tiles[t]) for t in range(j + 1, count)]
        result = jnp.zeros(shape, jnp.float32)
        for k in range(8):
            scale = lax.rsqrt(splat[k][k])
            rows[k] = rows[k] * scale
            for i in range(k + 1, 8):
                splat[i][k] = splat[i][k] * scale
            for i in range(k + 1, 8):
                for m in range(k + 1, i + 1):
                    splat[i][m] = splat[i][m] - splat[i][k] * splat[m][k]
                rows[i] = rows[i] - splat[i][k] * rows[k]
            for t in range(len(rest)):
                below = cols[t + 1]
                below[k] = below[k] * scale
                for m in range(k + 1, 8):
                    below[m] = below[m] - below[k] * splat[m][k]
                rest[t] = rest[t] - below[k] * rows[k]
            result = jnp.where(sub == k, rows[k], result)
        done.append(jnp.where(lane <= sub + base, result, 0.0))
        tiles[j + 1 :] = rest
    return done


def factor_kernel(gram_ref, inverse_ref, work):
    size = work.shape[0]
    work[...] = gram_ref[...]

    def step(k, carry):
        at = pl.ds(pl.multiple_of(k * B, B), B)
        tiles = [work[pl.ds(pl.multiple_of(k * B + 8 * t, 8), 8), at] for t in range(B // 8)]
        corner = jnp.concatenate(block_inverse(tiles), axis=0)
        row_id = lax.broadcasted_iota(jnp.int32, (size, B), 0)
        column = jnp.where(row_id >= (k + 1) * B, work[:, at], 0.0)
        unit = lax.broadcasted_iota(jnp.int32, (B, B), 0) == lax.broadcasted_iota(jnp.int32, (B, B), 1)
        work[at, at] = jnp.where(unit, 1.0, 0.0)
        below = dot_f32(column, corner, ((1,), (1,)))
        scaled = dot_f32(corner, work[at, :], ((1,), (0,)))
        block = work[:, at]
        work[:, at] = jnp.where(row_id >= (k + 1) * B, 0.0, block)
        work[...] = work[...] - dot_f32(below, scaled, ((1,), (0,)))
        work[at, :] = scaled
        return carry

    lax.fori_loop(0, size // B, step, 0)
    row_id = lax.broadcasted_iota(jnp.int32, (size, size), 0)
    col_id = lax.broadcasted_iota(jnp.int32, (size, size), 1)
    inverse_ref[...] = jnp.where(col_id <= row_id, work[...], 0.0)


def inverse_factor(gram):
    size = gram.shape[0]
    return pl.pallas_call(
        factor_kernel,
        out_shape=jax.ShapeDtypeStruct((size, size), jnp.float32),
        in_specs=[pl.BlockSpec(memory_space=pltpu.VMEM)],
        out_specs=pl.BlockSpec(memory_space=pltpu.VMEM),
        scratch_shapes=[pltpu.VMEM((size, size), jnp.float32)],
        compiler_params=pltpu.CompilerParams(vmem_limit_bytes=32 * 2**20),
    )(gram)


MESH = pl.DeviceIdType.MESH
NEAR = 8
FAR = 16
SUMMERS = 10


def tri_blocks(size):
    return [(i, j) for i in range(size // B) for j in range(i + 1)]


def sum_kernel(factor, part_ref, gram_ref, high, low, pack, near, mine, far, total, near_s, near_r, far_s, far_r, out_s, out_r, end_s, end_r):
    band, dom = lax.axis_index("band"), lax.axis_index("dom")
    pair, half = dom // 2, dom % 2
    rank = half * 4 + band
    size = part_ref.shape[1]
    blocks = tri_blocks(size)
    share = len(blocks) * B // NEAR
    piece = share // SUMMERS

    def near_peer(step):
        other = (rank + step) % NEAR
        return other, (other % 4, pair * 2 + other // 4)

    def far_peer(step):
        other = (pair + step) % FAR
        return other, (band, other * 2 + half)

    barrier = pltpu.get_barrier_semaphore()
    for step in range(1, NEAR):
        pl.semaphore_signal(barrier, inc=1, device_id=near_peer(step)[1], device_id_type=MESH)
    for step in range(1, FAR):
        pl.semaphore_signal(barrier, inc=1, device_id=far_peer(step)[1], device_id_type=MESH)
    contract = (((0,), (0,)), ((), ()))

    def split_rows(n, carry):
        at = pl.ds(pl.multiple_of(n * 128, 128), 128)
        high[at, :], low[at, :] = split(part_ref[at, :])
        return carry

    lax.fori_loop(0, part_ref.shape[0] // 128, split_rows, 0)
    for i in range(size // B):
        own, wide = slice(i * B, (i + 1) * B), slice(0, (i + 1) * B)
        block_row = lax.dot_general(high[:, own], high[:, wide], contract, preferred_element_type=jnp.float32)
        block_row += lax.dot_general(high[:, own], low[:, wide], contract, preferred_element_type=jnp.float32)
        block_row += lax.dot_general(low[:, own], high[:, wide], contract, preferred_element_type=jnp.float32)
        for j in range(i + 1):
            n = blocks.index((i, j))
            pack[n * B : (n + 1) * B, :] = block_row[:, j * B : (j + 1) * B]
    pl.semaphore_wait(barrier, NEAR + FAR - 2)

    def rows(index, count):
        return pl.ds(pl.multiple_of(index * count, 8), count)

    def near_copy(step):
        other, device = near_peer(step)
        return pltpu.make_async_remote_copy(
            src_ref=pack.at[rows(other, share)], dst_ref=near.at[rank],
            send_sem=near_s.at[step], recv_sem=near_r.at[rank], device_id=device, device_id_type=MESH)

    def near_arrival(step):
        other, device = near_peer(step)
        return pltpu.make_async_remote_copy(
            src_ref=pack.at[rows(other, share)], dst_ref=near.at[other],
            send_sem=near_s.at[step], recv_sem=near_r.at[other], device_id=device, device_id_type=MESH)

    for step in range(1, NEAR):
        near_copy(step).start()
    near[rank] = pack[rows(rank, share), :]
    for step in range(1, NEAR):
        near_arrival(step).wait_recv()
    acc = near[0]
    for n in range(1, NEAR):
        acc = acc + near[n]
    mine[...] = acc

    def far_copy(step, slot):
        other, device = far_peer(step)
        return other, pltpu.make_async_remote_copy(
            src_ref=mine.at[rows(other % SUMMERS, piece)], dst_ref=far.at[pair if slot is None else other],
            send_sem=far_s.at[step], recv_sem=far_r.at[pair if slot is None else other],
            device_id=device, device_id_type=MESH)

    for step in range(1, FAR):
        other, copy = far_copy(step, None)
        pl.when(other < SUMMERS)(copy.start)

    place = rank * share

    def out_rows(index):
        return pl.ds(pl.multiple_of(place + (index % SUMMERS) * piece, 8), piece)

    def out_copy(step):
        other, device = far_peer(step)
        return pltpu.make_async_remote_copy(
            src_ref=total.at[out_rows(pair)], dst_ref=total.at[out_rows(pair)],
            send_sem=out_s.at[step], recv_sem=out_r.at[pair], device_id=device, device_id_type=MESH)

    def out_arrival(step):
        other, device = far_peer(step)
        return other, pltpu.make_async_remote_copy(
            src_ref=total.at[out_rows(other)], dst_ref=total.at[out_rows(other)],
            send_sem=out_s.at[step], recv_sem=out_r.at[other], device_id=device, device_id_type=MESH)

    @pl.when(pair < SUMMERS)
    def _():
        far[pair] = mine[rows(pair % SUMMERS, piece), :]
        for step in range(1, FAR):
            far_copy(step, 1)[1].wait_recv()
        acc = far[0]
        for n in range(1, FAR):
            acc = acc + far[n]
        total[out_rows(pair), :] = acc * factor
        for step in range(1, FAR):
            out_copy(step).start()

    for step in range(1, FAR):
        other, copy = out_arrival(step)
        pl.when(other < SUMMERS)(copy.wait_recv)

    def end_copy(step, slot):
        other, device = near_peer(step)
        at = rows(rank if slot is None else other, share)
        return pltpu.make_async_remote_copy(
            src_ref=total.at[at], dst_ref=total.at[at],
            send_sem=end_s.at[step], recv_sem=end_r.at[rank if slot is None else other],
            device_id=device, device_id_type=MESH)

    for step in range(1, NEAR):
        end_copy(step, None).start()
    for step in range(1, NEAR):
        end_copy(step, 1).wait_recv()
    for n, (i, j) in enumerate(blocks):
        block = total[n * B : (n + 1) * B, :]
        gram_ref[i * B : (i + 1) * B, j * B : (j + 1) * B] = block
        if i != j:
            gram_ref[j * B : (j + 1) * B, i * B : (i + 1) * B] = block.T

    for step in range(1, NEAR):
        near_copy(step).wait_send()
        end_copy(step, None).wait_send()
    for step in range(1, FAR):
        other, copy = far_copy(step, None)
        pl.when(other < SUMMERS)(copy.wait_send)

    @pl.when(pair < SUMMERS)
    def _():
        for step in range(1, FAR):
            out_copy(step).wait_send()


def sum_gram(part, factor):
    cells, size = part.shape
    packed = len(tri_blocks(size)) * B
    share = packed // NEAR
    dma = pltpu.SemaphoreType.DMA
    return pl.pallas_call(
        functools.partial(sum_kernel, factor),
        out_shape=jax.ShapeDtypeStruct((size, size), jnp.float32),
        in_specs=[pl.BlockSpec(memory_space=pltpu.VMEM)],
        out_specs=pl.BlockSpec(memory_space=pltpu.VMEM),
        scratch_shapes=[
            pltpu.VMEM((cells, size), jnp.bfloat16),
            pltpu.VMEM((cells, size), jnp.bfloat16),
            pltpu.VMEM((packed, B), jnp.float32),
            pltpu.VMEM((NEAR, share, B), jnp.float32),
            pltpu.VMEM((share, B), jnp.float32),
            pltpu.VMEM((FAR, share // SUMMERS, B), jnp.float32),
            pltpu.VMEM((packed, B), jnp.float32),
            dma((NEAR,)), dma((NEAR,)), dma((FAR,)), dma((FAR,)),
            dma((FAR,)), dma((FAR,)), dma((NEAR,)), dma((NEAR,)),
        ],
        compiler_params=pltpu.CompilerParams(collective_id=1, has_side_effects=True, vmem_limit_bytes=32 * 2**20),
    )(part)


ROWS = 32
DEPTH = 48
WIDE = 128
CELLS = ROWS * DEPTH
PROJ = 32
REACH = 6
FLAGS = PROJ
GROUP = 8
STRIP = 8
STRIPS = ROWS // STRIP
PIECE = 4
PIECES = ROWS // PIECE
WINDOW = 3
AREA = STRIP * DEPTH


def split(value):
    high = value.astype(jnp.bfloat16)
    return high, (value - high.astype(jnp.float32)).astype(jnp.bfloat16)


def swap(value):
    return pltpu.roll(value, WIDE // 2, value.ndim - 1)


def field_kernel(
    orb, pot, proj, info, out,
    e1, e2, second, shift_pot, nonlocal_plane, left, right, raw, notes, pot_all, corr_sum, corr, corr_in, weights,
    give_cross, give_keep, got_cross, got1, got2, slab,
    local_s, x_s, x_r, own_s, fwd_s, halo_r, small_s, small_r, core_s, core_r, next_s, next_r, last_s, last_r,
    corr_s, corr_r, y2_s, y2_r, out_s, out_r, self_s,
):
    band, dom = lax.axis_index("band"), lax.axis_index("dom")
    pair, half = dom // 2, dom % 2
    other = 1 - half
    core = lax.rem(band, 2)
    rank = half * 4 + band
    pairs = lax.axis_size("dom") // 2
    partner = (band, pair * 2 + other)
    sibling = (band + 1 - 2 * core, dom)

    def at_pair(step):
        return (band, lax.rem(pair + step + pairs, pairs) * 2 + half)

    def send(src, dst, ssem, rsem, device):
        return pltpu.make_async_remote_copy(
            src_ref=src, dst_ref=dst, send_sem=ssem, recv_sem=rsem, device_id=device, device_id_type=MESH)

    def member(index):
        return (lax.rem(index, 4), pair * 2 + index // 4)

    barrier = pltpu.get_barrier_semaphore()
    for peer in [at_pair(1), at_pair(-1)] + [member(lax.rem(rank + n, GROUP)) for n in range(1, GROUP)]:
        pl.semaphore_signal(barrier, inc=1, device_id=peer, device_id_type=MESH)

    loads = [pltpu.make_async_copy(orb.at[p], second.at[p], local_s.at[p]) for p in range(4)]
    for copy in loads:
        copy.start()
    lane = lax.broadcasted_iota(jnp.int32, (DEPTH, WIDE), 1)
    lower = lane < WIDE // 2
    kept = (lane // (WIDE // 2)) == half

    share = pl.ds(pl.multiple_of(core * (PROJ // 2), 16), PROJ // 2)
    twin = pl.ds(pl.multiple_of((1 - core) * (PROJ // 2), 16), PROJ // 2)
    small = [
        send(pot, pot_all.at[pl.ds(4 * half, 4)], small_s.at[0], small_r.at[0], partner),
        send(info, notes.at[1 + half], small_s.at[1], small_r.at[1], partner),
        send(proj.at[share], raw.at[1 + half, share], small_s.at[2], small_r.at[2], partner),
    ]
    small_in = [
        send(pot, pot_all.at[pl.ds(4 * other, 4)], small_s.at[0], small_r.at[0], partner),
        send(info, notes.at[1 + other], small_s.at[1], small_r.at[1], partner),
        send(proj.at[share], raw.at[1 + other, share], small_s.at[2], small_r.at[2], partner),
    ]
    across = send(raw.at[1 + other, share], raw.at[1 + other, share], core_s, core_r, sibling)
    across_in = send(raw.at[1 + other, twin], raw.at[1 + other, twin], core_s, core_r, sibling)
    onward = [
        send(notes.at[2], notes.at[0], next_s.at[0], next_r.at[0], at_pair(1)),
        send(raw.at[2, share], raw.at[0, share], next_s.at[1], next_r.at[1], at_pair(1)),
    ]
    last = send(raw.at[0, share], raw.at[0, share], last_s, last_r, sibling)
    last_in = send(raw.at[0, twin], raw.at[0, twin], last_s, last_r, sibling)

    def piece_rows(c):
        return pl.ds(c * PIECE, PIECE)

    def cross(c):
        at = (slice(None), piece_rows(c))
        return send(give_cross.at[at], got_cross.at[at], x_s.at[c], x_r.at[c], partner)

    def keep(c):
        at = piece_rows(c)
        return send(give_keep.at[:, at], got1.at[other, :, at], own_s.at[c], halo_r.at[other, c],
                    at_pair(2 * half - 1))

    def forward(c):
        at = piece_rows(c)
        return send(got_cross.at[:, at], got1.at[half, :, at], fwd_s.at[c], halo_r.at[half, c],
                    at_pair(1 - 2 * half))

    def halo_in(side, c):
        at = piece_rows(c)
        return send(give_keep.at[:, at], got1.at[side, :, at], own_s.at[c], halo_r.at[side, c], at_pair(1))

    notes[1 + half] = info[...]
    raw[1 + half] = proj[...]
    pot_all[pl.ds(4 * half, 4)] = pot[...]
    for copy in loads:
        copy.wait()

    def pack_piece(c, carry):
        for n in range(PIECE):
            r = c * PIECE + n
            for j in range(2):
                near, far = second[j, r], second[j + 2, r]
                give_cross[j, r] = jnp.where(kept, swap(near), far)
                give_keep[j, r] = jnp.where(kept, near, swap(far))
        return carry

    def start_piece(c):
        cross(c).start()
        keep(c).start()

    lax.fori_loop(0, WINDOW, pack_piece, 0)
    pl.semaphore_wait(barrier, GROUP + 1)
    for copy in small:
        copy.start()
    for c in range(WINDOW):
        start_piece(c)
    lax.fori_loop(WINDOW, PIECES, pack_piece, 0)

    for copy in small_in:
        copy.wait_recv()
    across.start()
    for copy in onward[:1]:
        copy.start()

    def placed(group, reach):
        total = jnp.zeros((PROJ, CELLS), jnp.float32)
        for k in range(SPAN):
            flag = notes[group, :, FLAGS + reach * SPAN + k : FLAGS + reach * SPAN + k + 1]
            total = total + flag * raw[group, :, k * CELLS : (k + 1) * CELLS]
        return total

    def store_pair(p, groups, reach, slot):
        beta = jnp.concatenate([placed(group, reach) for group in groups], axis=0)
        high_part, low_part = split(beta)
        both = jnp.concatenate([high_part, low_part], axis=0)
        for n in range(STRIPS):
            left[p, n, slot * 128 : (slot + 1) * 128, :] = both[:, n * AREA : (n + 1) * AREA]
        high32 = high_part.astype(jnp.float32)
        wide = jnp.concatenate([high32, low_part.astype(jnp.float32)], axis=0)
        turned = wide.T.astype(jnp.bfloat16)
        right[p, :, slot * 256 : slot * 256 + 128] = turned
        right[p, :, slot * 256 + 128 : slot * 256 + 192] = turned[:, :64]
        right[p, :, slot * 256 + 192 : slot * 256 + 256] = jnp.zeros((CELLS, 64), jnp.bfloat16)

    diagonal = lax.broadcasted_iota(jnp.int32, (DEPTH, DEPTH), 0) == lax.broadcasted_iota(
        jnp.int32, (DEPTH, DEPTH), 1)
    constant = -1.5 * center_weight - 7.0

    def spread(n, carry):
        p, r = n // ROWS, lax.rem(n, ROWS)
        columns = []
        for extra in (0, 4):
            line = jnp.broadcast_to(pot_all[p + extra, pl.ds(r, 1), :], (DEPTH, DEPTH))
            columns.append(jnp.sum(jnp.where(diagonal, line, 0.0), axis=1, keepdims=True))
        shift_pot[p, r] = jnp.where(lower, columns[0], columns[1]) + constant
        return carry

    def receive_piece(c):
        cross(c).wait_recv()
        forward(c).start()
        cross(c).wait_send()
        keep(c).wait_send()
        if c + WINDOW < PIECES:
            start_piece(c + WINDOW)

        def one(n, carry):
            r = c * PIECE + n
            for j in range(2):
                arrived = got_cross[j, r]
                e1[4 + j, r] = jnp.where(kept, second[j, r], arrived)
                e1[6 + j, r] = jnp.where(kept, second[j + 2, r], swap(arrived))
            return carry

        lax.fori_loop(0, PIECE, one, 0)

    for p in (2, 3):
        left[p, :, 128:256, :] = jnp.zeros((STRIPS, 128, AREA), jnp.bfloat16)
        right[p, :, 256:512] = jnp.zeros((CELLS, 256), jnp.bfloat16)
    def spread_rows(n):
        lax.fori_loop(n * 4 * ROWS // PIECES, (n + 1) * 4 * ROWS // PIECES, spread, 0)

    def add_strip(field, strip):
        def part(p, total):
            cells = field[4 + p, pl.ds(strip * STRIP, STRIP)].reshape(AREA, WIDE)
            both = jnp.concatenate(split(cells), axis=1)
            return total + lax.dot_general(
                left[p, strip], both, (((1,), (0,)), ((), ())), preferred_element_type=jnp.float32)

        corr_sum[...] = lax.fori_loop(0, 4, part, corr_sum[...])

    def share_sums(phase):
        total = corr_sum[:, :WIDE] + corr_sum[:, WIDE:]
        corr_sum[...] = jnp.zeros_like(corr_sum)
        near, tail = total[0:64] + total[64:128], total[128:192] + total[192:256]
        corr[phase, 0] = tail[:PROJ]
        corr[phase, 1] = near[PROJ:]
        corr[phase, 2] = near[:PROJ] + swap(tail[PROJ:])
        down = send(corr.at[phase, 0], corr_in.at[phase, 1], corr_s.at[phase, 0], corr_r.at[phase, 1], at_pair(-1))
        up = send(corr.at[phase, 1], corr_in.at[phase, 0], corr_s.at[phase, 1], corr_r.at[phase, 0], at_pair(1))
        down.start()
        up.start()
        return [down, up]

    def weigh(phase, copies):
        for copy in copies:
            copy.wait_recv()
        before = corr[phase, 0] + swap(corr_in[phase, 0])
        after = corr[phase, 1] + swap(corr_in[phase, 1])
        before, own, after = (
            dot_f32(notes[group, :, :PROJ], value, ((1,), (0,)))
            for group, value in ((0, before), (1, corr[phase, 2]), (2, after))
        )
        in_low = lax.broadcasted_iota(jnp.int32, (PROJ, WIDE), 1) < WIDE // 2
        zero = jnp.zeros((64, WIDE), jnp.bfloat16)
        parts = []
        for low_value, high_value in ((own, after), (before, swap(own))):
            value = jnp.concatenate(
                [jnp.where(in_low, low_value, 0.0), jnp.where(in_low, 0.0, high_value)], axis=0)
            high_part, low_part = split(value)
            parts += [high_part, high_part, low_part, zero]
        weights[...] = jnp.concatenate(parts, axis=0)

    def open_strip(field, got, strip):
        def one(n, carry):
            r = strip * STRIP + n
            for j in range(2):
                near, far = field[4 + j, r], field[6 + j, r]
                up, down = got[0, j, r], got[1, j, r]
                field[j, r] = swap(jnp.where(lower, near, up))
                field[2 + j, r] = jnp.where(lower, up, swap(far))
                field[8 + j, r] = swap(jnp.where(lower, down, near))
                field[10 + j, r] = jnp.where(lower, swap(far), down)
            return carry

        lax.fori_loop(0, STRIP, one, 0)

    def apply(field, strip, scale, write):
        def plane(p, carry):
            product = lax.dot_general(
                right[p, pl.ds(pl.multiple_of(strip * AREA, AREA), AREA), :], weights[...],
                (((1,), (0,)), ((), ())), preferred_element_type=jnp.float32)
            nonlocal_plane[...] = product.reshape(STRIP, DEPTH, WIDE)

            def row(n, inner):
                r = strip * STRIP + n
                centre = field[p + 4, r]
                total = centre * shift_pot[p, r] + nonlocal_plane[n]
                for k in range(1, 5):
                    pair_x = field[p + 4 + k, r] + field[p + 4 - k, r]
                    pair_y = field[p + 4, lax.rem(r + k, ROWS)] + field[p + 4, lax.rem(r + ROWS - k, ROWS)]
                    pair_z = pltpu.roll(centre, k, 0) + pltpu.roll(centre, DEPTH - k, 0)
                    total = total + (-0.5 * side_weights[k - 1]) * ((pair_x + pair_y) + pair_z)
                write(p, r, total * scale)
                return inner

            lax.fori_loop(0, STRIP, row, 0)
            return carry

        lax.fori_loop(0, 4, plane, 0)

    def open_first(strip):
        for side in range(2):
            for n in range(STRIP // PIECE):
                halo_in(side, strip * (STRIP // PIECE) + n).wait_recv()
        open_strip(e1, got1, strip)

    spread_rows(0)
    across_in.wait_recv()
    onward[1].start()
    receive_piece(0)
    store_pair(0, (1, 2), 0, 0)
    store_pair(1, (1, 2), 1, 0)
    spread_rows(1)
    receive_piece(1)
    store_pair(2, (1, 2), 2, 0)
    store_pair(3, (1, 2), 3, 0)
    spread_rows(2)
    receive_piece(2)
    for copy in onward:
        copy.wait_recv()
    last.start()
    spread_rows(3)
    spread_rows(4)
    receive_piece(3)
    last_in.wait_recv()
    store_pair(0, (0, 1), 4, 1)
    store_pair(1, (0, 1), 5, 1)
    corr_sum[...] = jnp.zeros_like(corr_sum)
    add_strip(e1, 0)
    receive_piece(4)
    spread_rows(5)
    add_strip(e1, 1)
    receive_piece(5)
    spread_rows(6)
    open_first(0)
    receive_piece(6)
    spread_rows(7)
    add_strip(e1, 2)
    receive_piece(7)
    add_strip(e1, 3)
    copies1 = share_sums(0)
    for strip in range(1, STRIPS):
        open_first(strip)
    for c in range(PIECES):
        forward(c).wait_send()
    weigh(0, copies1)

    def write_first(p, r, value):
        e2[p + 4, r] = value

    def up2(c):
        at = piece_rows(c)
        return send(give_cross.at[:, at], got2.at[0, :, at], y2_s.at[0, c], y2_r.at[0, c], at_pair(1))

    def down2(c):
        at = piece_rows(c)
        return send(give_keep.at[:, at], got2.at[1, :, at], y2_s.at[1, c], y2_r.at[1, c], at_pair(-1))

    def first_strip(strip):
        apply(e1, strip, 1.0 / 6.0, write_first)

        def pack(n, inner):
            r = strip * STRIP + n
            for j in range(2):
                near, turned = e2[4 + j, r], swap(e2[6 + j, r])
                give_cross[j, r] = jnp.where(lower, turned, near)
                give_keep[j, r] = jnp.where(lower, near, turned)
            return inner

        lax.fori_loop(0, STRIP, pack, 0)
        for c in range(2 * strip, 2 * strip + 2):
            if c < WINDOW:
                up2(c).start()
                down2(c).start()
        add_strip(e2, strip)

    for strip in range(STRIPS):
        first_strip(strip)
    copies2 = share_sums(1)
    weigh(1, copies2)

    def write_second(p, r, value):
        second[p, r] = value - e1[p + 4, r]

    def give(index, part):
        src = second.at[index // 2, pl.ds(lax.rem(index, 2) * 16 + part * STRIP, STRIP)]
        return send(src, slab.at[rank, pl.ds(part * STRIP, STRIP)], out_s.at[index, part], out_r.at[rank, part],
                    member(index))

    def own_part(part):
        src = second.at[rank // 2, pl.ds(lax.rem(rank, 2) * 16 + part * STRIP, STRIP)]
        return pltpu.make_async_copy(src, slab.at[rank, pl.ds(part * STRIP, STRIP)], self_s.at[part])

    def second_strip(strip):
        for c in range(2 * strip, 2 * strip + 2):
            for copy in (up2(c), down2(c)):
                copy.wait_recv()
                copy.wait_send()
            if c + WINDOW < PIECES:
                up2(c + WINDOW).start()
                down2(c + WINDOW).start()
        open_strip(e2, got2, strip)
        apply(e2, strip, 1.0 / 3.0, write_second)
        part = strip % 2
        for n in range(4):
            index = 2 * lax.rem(n + rank // 2 + 2, 4) + strip // 2
            pl.when(index != rank)(lambda index=index: give(index, part).start())
        pl.when(lax.rem(rank, 2) == strip // 2)(own_part(part).start)

    for strip in range(STRIPS):
        second_strip(strip)

    for n in range(1, GROUP):
        index = lax.rem(rank + n, GROUP)
        for part in range(2):
            send(second.at[0, pl.ds(0, STRIP)], slab.at[index, pl.ds(part * STRIP, STRIP)], out_s.at[index, part],
                 out_r.at[index, part], member(index)).wait_recv()
    own_part(0).wait()
    own_part(1).wait()

    def repack(n, carry):
        cells = pl.ds(pl.multiple_of(n * DEPTH, 8), DEPTH)
        more = pl.ds(pl.multiple_of(CELLS // 2 + n * DEPTH, 8), DEPTH)
        for b in range(4):
            at = slice(b * WIDE, (b + 1) * WIDE)
            here, there = slab[b, n], slab[4 + b, n]
            out[cells, at] = jnp.where(lower, here, swap(there))
            out[more, at] = jnp.where(lower, swap(here), there)
        return carry

    lax.fori_loop(0, ROWS // 2, repack, 0)

    for copy in small + [across, last] + onward + copies1 + copies2:
        copy.wait_send()
    for n in range(1, GROUP):
        for part in range(2):
            give(lax.rem(rank + n, GROUP), part).wait_send()


def filtered_slab(orbitals, potential, projectors, info):
    dma = pltpu.SemaphoreType.DMA
    f32, bf16 = jnp.float32, jnp.bfloat16
    vmem = pl.BlockSpec(memory_space=pltpu.VMEM)
    block = (ROWS, DEPTH, WIDE)
    return pl.pallas_call(
        field_kernel,
        out_shape=jax.ShapeDtypeStruct((CELLS, NORB), f32),
        in_specs=[pl.BlockSpec(memory_space=pl.ANY), vmem, vmem, vmem],
        out_specs=vmem,
        scratch_shapes=[
            pltpu.VMEM((12,) + block, f32),
            pltpu.VMEM((12,) + block, f32),
            pltpu.VMEM((4,) + block, f32),
            pltpu.VMEM((4,) + block, f32),
            pltpu.VMEM((STRIP, DEPTH, WIDE), f32),
            pltpu.VMEM((4, STRIPS, 256, AREA), bf16),
            pltpu.VMEM((4, CELLS, 512), bf16),
            pltpu.VMEM((3, PROJ, SPAN * CELLS), f32),
            pltpu.VMEM((3, PROJ, 128), f32),
            pltpu.VMEM((8, ROWS, DEPTH), f32),
            pltpu.VMEM((256, 2 * WIDE), f32),
            pltpu.VMEM((2, 3, PROJ, WIDE), f32),
            pltpu.VMEM((2, 2, PROJ, WIDE), f32),
            pltpu.VMEM((512, WIDE), bf16),
            pltpu.VMEM((2,) + block, f32),
            pltpu.VMEM((2,) + block, f32),
            pltpu.VMEM((2,) + block, f32),
            pltpu.VMEM((2, 2) + block, f32),
            pltpu.VMEM((2, 2) + block, f32),
            pltpu.VMEM((GROUP, ROWS // 2, DEPTH, WIDE), f32),
            dma((4,)), dma((PIECES,)), dma((PIECES,)), dma((PIECES,)), dma((PIECES,)), dma((2, PIECES)),
            dma((3,)), dma((3,)), dma(()), dma(()), dma((2,)), dma((2,)), dma(()), dma(()),
            dma((2, 2)), dma((2, 2)), dma((2, PIECES)), dma((2, PIECES)),
            dma((GROUP, 2)), dma((GROUP, 2)), dma((2,)),
        ],
        compiler_params=pltpu.CompilerParams(collective_id=2, has_side_effects=True, vmem_limit_bytes=62 * 2**20),
    )(orbitals, potential, projectors, info)


def home_kernel(flat, inverse, out, parts, turned, local_s, send_s, recv_s):
    band, dom = lax.axis_index("band"), lax.axis_index("dom")
    pair, half = dom // 2, dom % 2
    rank = half * 4 + band
    place, core = (band // 2) * 2 + half, lax.rem(band, 2)
    barrier = pltpu.get_barrier_semaphore()
    for step in range(1, GROUP):
        index = lax.rem(rank + step, GROUP)
        pl.semaphore_signal(
            barrier, inc=1, device_id=(lax.rem(index, 4), pair * 2 + index // 4), device_id_type=MESH)
    high_part, low_part = split(inverse[...])
    turned[0], turned[1] = high_part, low_part

    def target(index):
        return out.at[index // 2, pl.ds(pl.multiple_of(lax.rem(index, 2) * 16, 8), ROWS // 2)]

    def choice(n):
        chip = lax.rem(place + (2, 1, 3, 0)[n // 2], 4)
        return lax.rem(chip, 2), (chip // 2) * 2 + lax.rem(core + 1 + n, 2)

    def move(n):
        to_half, to_band = choice(n)
        return pltpu.make_async_remote_copy(
            src_ref=parts.at[n], dst_ref=target(rank), send_sem=send_s.at[n], recv_sem=recv_s.at[rank],
            device_id=(to_band, pair * 2 + to_half), device_id_type=MESH)

    local = pltpu.make_async_copy(parts.at[GROUP - 1], target(rank), local_s)
    contract = (((1,), (1,)), ((), ()))
    for n in range(GROUP):
        to_half, to_band = choice(n)
        rows = pl.ds(pl.multiple_of(to_band * B, B), B)

        def tile(m, carry, n=n, to_half=to_half, rows=rows):
            size = CELLS // 8
            cells = flat[pl.ds(pl.multiple_of(to_half * (CELLS // 2) + m * size, 8), size), :]
            high_cells, low_cells = split(cells)
            high_rot, low_rot = turned[0, rows, :], turned[1, rows, :]
            both = jnp.concatenate([high_rot, low_rot], axis=0)
            wide = lax.dot_general(high_cells, both, contract, preferred_element_type=jnp.float32)
            more = lax.dot_general(low_cells, high_rot, contract, preferred_element_type=jnp.float32)
            value = wide[:, :B] + (wide[:, B:] + more)
            parts[n, pl.ds(m * (size // DEPTH), size // DEPTH)] = value.reshape(size // DEPTH, DEPTH, WIDE)
            return carry

        lax.fori_loop(0, 4, tile, 0)
        if n == 0:
            pl.semaphore_wait(barrier, GROUP - 1)
        if n < GROUP - 1:
            move(n).start()
        else:
            local.start()
    for step in range(1, GROUP):
        index = lax.rem(rank + step, GROUP)
        pltpu.make_async_remote_copy(
            src_ref=parts.at[0], dst_ref=target(index), send_sem=send_s.at[0], recv_sem=recv_s.at[index],
            device_id=(lax.rem(index, 4), pair * 2 + index // 4), device_id_type=MESH).wait_recv()
    local.wait()
    for n in range(GROUP - 1):
        move(n).wait_send()


def rotate_home(flat, inverse):
    dma = pltpu.SemaphoreType.DMA
    vmem = pl.BlockSpec(memory_space=pltpu.VMEM)
    return pl.pallas_call(
        home_kernel,
        out_shape=jax.ShapeDtypeStruct((4, ROWS, DEPTH, WIDE), jnp.float32),
        in_specs=[vmem, vmem],
        out_specs=pl.BlockSpec(memory_space=pl.ANY),
        scratch_shapes=[
            pltpu.VMEM((GROUP, ROWS // 2, DEPTH, WIDE), jnp.float32),
            pltpu.VMEM((2, NORB, NORB), jnp.bfloat16),
            dma(()), dma((GROUP,)), dma((GROUP,)),
        ],
        compiler_params=pltpu.CompilerParams(collective_id=3, has_side_effects=True, vmem_limit_bytes=40 * 2**20),
    )(flat, inverse)


def shards(orbitals, potential, projectors, coupling, atom_plane, projector_count):
    planes, side_y, side_z, local_orbs = orbitals.shape
    atoms = projectors.shape[0]
    first_plane = atom_plane - lax.axis_index("dom") * planes
    reach_ids = jnp.arange(REACH, dtype=jnp.int32)
    span_ids = jnp.arange(SPAN, dtype=jnp.int32)
    flags = (
        reach_ids[None, :, None] == first_plane[:, None, None] + span_ids[None, None, :]
    ).astype(jnp.float32).reshape(atoms, 1, REACH * SPAN)
    flags = jnp.broadcast_to(flags, (atoms, MAXPROJ, REACH * SPAN)).reshape(PROJ, REACH * SPAN)
    slots = jnp.arange(MAXPROJ, dtype=jnp.int32)
    live_mask = (slots[None, :] < projector_count[:, None]).astype(jnp.float32)
    sym_coupling = 0.5 * (coupling + jnp.transpose(coupling, (0, 2, 1)))
    sym_coupling = sym_coupling * live_mask[:, :, None] * live_mask[:, None, :]
    same_atom = jnp.eye(atoms, dtype=jnp.float32)
    blocks = (sym_coupling[:, :, None, :] * same_atom[:, None, :, None]).reshape(PROJ, PROJ)
    info = jnp.concatenate(
        [blocks, flags, jnp.zeros((PROJ, 128 - PROJ - REACH * SPAN), jnp.float32)], axis=1)
    flat = filtered_slab(orbitals, potential, projectors.reshape(PROJ, SPAN * CELLS), info)
    total_cells = planes * side_y * side_z * lax.axis_size("dom")
    gram = sum_gram(flat, 1.0 / total_cells)
    filtered = rotate_home(flat, inverse_factor(gram))
    return (filtered, gram)


def solution(mesh):
    placed = (
        P("dom", None, None, "band"),
        P("dom", None, None),
        P("dom", None, None),
        P("dom", None, None),
        P("dom"),
        P("dom"),
    )
    return jax.shard_map(
        shards,
        mesh=mesh,
        in_specs=placed,
        out_specs=(P("dom", None, None, "band"), P()),
        check_vma=False,
    )
```

```python
import functools

import jax
import jax.numpy as jnp
from jax import lax
from jax.experimental import pallas as pl
from jax.experimental.pallas import tpu as pltpu
from jax.sharding import PartitionSpec as P

NORB = 512
HALO = 4
SPAN = 3
MAXPROJ = 4
B = 128

center_weight = -205.0 / 72.0
side_weights = (8.0 / 5.0, -1.0 / 5.0, 8.0 / 315.0, -1.0 / 560.0)
HIGH = lax.Precision.HIGHEST


HIGHEST = lax.Precision.HIGHEST


def dot_f32(a, b, dims):
    return lax.dot_general(a, b, (dims, ((), ())), precision=HIGHEST, preferred_element_type=jnp.float32)


def block_inverse(tiles):
    count = len(tiles)
    tiles = list(tiles)
    shape = tiles[0].shape
    lane = lax.broadcasted_iota(jnp.int32, shape, 1)
    sub = lax.broadcasted_iota(jnp.int32, shape, 0)
    done = []
    for j in range(count):
        base = 8 * j
        cols = [
            [jnp.broadcast_to(tiles[t][:, base + k : base + k + 1], shape) for k in range(8)]
            for t in range(j, count)
        ]
        inside = (lane >= base) & (lane < base + 8)
        unit = jnp.where(lane == sub + base, 1.0, 0.0)
        own = jnp.where(inside, unit, tiles[j])
        rows = [jnp.broadcast_to(own[k : k + 1, :], shape) for k in range(8)]
        splat = [
            [jnp.broadcast_to(cols[0][k][i : i + 1, :], shape) if i >= k else None for k in range(8)]
            for i in range(8)
        ]
        rest = [jnp.where(inside, 0.0, tiles[t]) for t in range(j + 1, count)]
        result = jnp.zeros(shape, jnp.float32)
        for k in range(8):
            scale = lax.rsqrt(splat[k][k])
            rows[k] = rows[k] * scale
            for i in range(k + 1, 8):
                splat[i][k] = splat[i][k] * scale
            for i in range(k + 1, 8):
                for m in range(k + 1, i + 1):
                    splat[i][m] = splat[i][m] - splat[i][k] * splat[m][k]
                rows[i] = rows[i] - splat[i][k] * rows[k]
            for t in range(len(rest)):
                below = cols[t + 1]
                below[k] = below[k] * scale
                for m in range(k + 1, 8):
                    below[m] = below[m] - below[k] * splat[m][k]
                rest[t] = rest[t] - below[k] * rows[k]
            result = jnp.where(sub == k, rows[k], result)
        done.append(jnp.where(lane <= sub + base, result, 0.0))
        tiles[j + 1 :] = rest
    return done


def factor_steps(work, done):
    size = work.shape[0]

    def step(k, carry):
        at = pl.ds(pl.multiple_of(k * B, B), B)
        tiles = [work[pl.ds(pl.multiple_of(k * B + 8 * t, 8), 8), at] for t in range(B // 8)]
        corner = jnp.concatenate(block_inverse(tiles), axis=0)
        row_id = lax.broadcasted_iota(jnp.int32, (size, B), 0)
        column = jnp.where(row_id >= (k + 1) * B, work[:, at], 0.0)
        unit = lax.broadcasted_iota(jnp.int32, (B, B), 0) == lax.broadcasted_iota(jnp.int32, (B, B), 1)
        work[at, at] = jnp.where(unit, 1.0, 0.0)
        scaled = dot_f32(corner, work[at, :], ((1,), (0,)))
        row_at = lax.broadcasted_iota(jnp.int32, (B, size), 0) + k * B
        done(k, jnp.where(lax.broadcasted_iota(jnp.int32, (B, size), 1) <= row_at, scaled, 0.0))
        below = dot_f32(column, corner, ((1,), (1,)))
        block = work[:, at]
        work[:, at] = jnp.where(row_id >= (k + 1) * B, 0.0, block)
        work[...] = work[...] - dot_f32(below, scaled, ((1,), (0,)))
        return carry

    lax.fori_loop(0, size // B, step, 0)


MESH = pl.DeviceIdType.MESH
NEAR = 8
FAR = 16
SUMMERS = 10


def tri_blocks(size):
    return [(i, j) for i in range(size // B) for j in range(i + 1)]


def finish_part(
    factor, gram_ref, filtered_ref,
    high, low, pack, near, mine, far, total, work, parts, near_s, near_r, far_s, far_r, out_s, out_r, end_s, end_r,
    local_s, home_s, home_r,
):
    band, dom = lax.axis_index("band"), lax.axis_index("dom")
    pair, half = dom // 2, dom % 2
    rank = half * 4 + band
    blocks = tri_blocks(work.shape[0])
    share = len(blocks) * B // NEAR
    piece = share // SUMMERS

    def near_peer(step):
        other = (rank + step) % NEAR
        return other, (other % 4, pair * 2 + other // 4)

    def far_peer(step):
        other = (pair + step) % FAR
        return other, (band, other * 2 + half)

    def rows(index, count):
        return pl.ds(pl.multiple_of(index * count, 8), count)

    def near_copy(step):
        other, device = near_peer(step)
        return pltpu.make_async_remote_copy(
            src_ref=pack.at[rows(other, share)], dst_ref=near.at[rank],
            send_sem=near_s.at[step], recv_sem=near_r.at[rank], device_id=device, device_id_type=MESH)

    def near_arrival(step):
        other, device = near_peer(step)
        return pltpu.make_async_remote_copy(
            src_ref=pack.at[rows(other, share)], dst_ref=near.at[other],
            send_sem=near_s.at[step], recv_sem=near_r.at[other], device_id=device, device_id_type=MESH)

    for step in range(1, NEAR):
        near_copy(step).start()
    near[rank] = pack[rows(rank, share), :]
    for step in range(1, NEAR):
        near_arrival(step).wait_recv()
    acc = near[0]
    for n in range(1, NEAR):
        acc = acc + near[n]
    mine[...] = acc

    def far_copy(step, slot):
        other, device = far_peer(step)
        return other, pltpu.make_async_remote_copy(
            src_ref=mine.at[rows(other % SUMMERS, piece)], dst_ref=far.at[pair if slot is None else other],
            send_sem=far_s.at[step], recv_sem=far_r.at[pair if slot is None else other],
            device_id=device, device_id_type=MESH)

    for step in range(1, FAR):
        other, copy = far_copy(step, None)
        pl.when(other < SUMMERS)(copy.start)

    place = rank * share

    def out_rows(index):
        return pl.ds(pl.multiple_of(place + (index % SUMMERS) * piece, 8), piece)

    def out_copy(step):
        other, device = far_peer(step)
        return pltpu.make_async_remote_copy(
            src_ref=total.at[out_rows(pair)], dst_ref=total.at[out_rows(pair)],
            send_sem=out_s.at[step], recv_sem=out_r.at[pair], device_id=device, device_id_type=MESH)

    def out_arrival(step):
        other, device = far_peer(step)
        return other, pltpu.make_async_remote_copy(
            src_ref=total.at[out_rows(other)], dst_ref=total.at[out_rows(other)],
            send_sem=out_s.at[step], recv_sem=out_r.at[other], device_id=device, device_id_type=MESH)

    @pl.when(pair < SUMMERS)
    def _():
        far[pair] = mine[rows(pair % SUMMERS, piece), :]
        for step in range(1, FAR):
            far_copy(step, 1)[1].wait_recv()
        acc = far[0]
        for n in range(1, FAR):
            acc = acc + far[n]
        total[out_rows(pair), :] = acc * factor
        for step in range(1, FAR):
            out_copy(step).start()

    for step in range(1, FAR):
        other, copy = out_arrival(step)
        pl.when(other < SUMMERS)(copy.wait_recv)

    def end_copy(step, slot):
        other, device = near_peer(step)
        at = rows(rank if slot is None else other, share)
        return pltpu.make_async_remote_copy(
            src_ref=total.at[at], dst_ref=total.at[at],
            send_sem=end_s.at[step], recv_sem=end_r.at[rank if slot is None else other],
            device_id=device, device_id_type=MESH)

    for step in range(1, NEAR):
        end_copy(step, None).start()
    for step in range(1, NEAR):
        end_copy(step, 1).wait_recv()
    for n, (i, j) in enumerate(blocks):
        block = total[n * B : (n + 1) * B, :]
        gram_ref[i * B : (i + 1) * B, j * B : (j + 1) * B] = block
        if i != j:
            gram_ref[j * B : (j + 1) * B, i * B : (i + 1) * B] = block.T
    work[...] = gram_ref[...]

    def target(index):
        return filtered_ref.at[index // 2, pl.ds(pl.multiple_of(lax.rem(index, 2) * 16, 8), ROWS // 2)]

    def move(k, to_half):
        return pltpu.make_async_remote_copy(
            src_ref=parts.at[k, rows(to_half, ROWS // 2)], dst_ref=target(rank), send_sem=home_s.at[k, to_half],
            recv_sem=home_r.at[rank], device_id=(k, pair * 2 + to_half), device_id_type=MESH)

    local = pltpu.make_async_copy(parts.at[band, rows(half, ROWS // 2)], target(rank), local_s)
    across = (((1,), (1,)), ((), ()))
    cells = high.shape[0] // 2

    def rotate(k, inverse_rows):
        high_rot, low_rot = split(inverse_rows)
        both = jnp.concatenate([high_rot, low_rot], axis=0)
        for to_half in range(2):
            at = slice(to_half * cells, (to_half + 1) * cells)
            wide = lax.dot_general(high[at, :], both, across, preferred_element_type=jnp.float32)
            more = lax.dot_general(low[at, :], high_rot, across, preferred_element_type=jnp.float32)
            value = wide[:, :B] + (wide[:, B:] + more)
            parts[k, rows(to_half, ROWS // 2)] = value.reshape(ROWS // 2, DEPTH, B)
            here = (k == band) & (to_half == half)
            pl.when(jnp.logical_not(here))(lambda to_half=to_half: move(k, to_half).start())
            pl.when(here)(local.start)

    factor_steps(work, rotate)
    for step in range(1, NEAR):
        other, device = near_peer(step)
        pltpu.make_async_remote_copy(
            src_ref=parts.at[0, rows(0, ROWS // 2)], dst_ref=target(other), send_sem=home_s.at[0, 0], recv_sem=home_r.at[other],
            device_id=device, device_id_type=MESH).wait_recv()
    local.wait()
    for k in range(4):
        for to_half in range(2):
            here = (k == band) & (to_half == half)
            pl.when(jnp.logical_not(here))(lambda k=k, to_half=to_half: move(k, to_half).wait_send())

    for step in range(1, NEAR):
        near_copy(step).wait_send()
        end_copy(step, None).wait_send()
    for step in range(1, FAR):
        other, copy = far_copy(step, None)
        pl.when(other < SUMMERS)(copy.wait_send)

    @pl.when(pair < SUMMERS)
    def _():
        for step in range(1, FAR):
            out_copy(step).wait_send()


ROWS = 32
DEPTH = 48
WIDE = 128
CELLS = ROWS * DEPTH
PROJ = 32
REACH = 6
FLAGS = PROJ
GROUP = 8
STRIP = 8
STRIPS = ROWS // STRIP
PIECE = 4
PIECES = ROWS // PIECE
WINDOW = 3
AREA = STRIP * DEPTH


def split(value):
    high = value.astype(jnp.bfloat16)
    return high, (value - high.astype(jnp.float32)).astype(jnp.bfloat16)


def swap(value):
    return pltpu.roll(value, WIDE // 2, value.ndim - 1)


def whole_kernel(
    factor, orb, pot, proj, info, gram_ref, filtered_ref,
    e1, e2, second, shift_pot, nonlocal_plane, left, right, raw, notes, pot_all, corr_sum, corr, corr_in, weights,
    give_cross, give_keep, got_cross, got1, got2, slab,
    local_s, x_s, x_r, own_s, fwd_s, halo_r, small_s, small_r, core_s, core_r, next_s, next_r, last_s, last_r,
    corr_s, corr_r, y2_s, y2_r, out_s, out_r, self_s,
    high_cells, low_cells, pack, *rest,
):
    band, dom = lax.axis_index("band"), lax.axis_index("dom")
    pair, half = dom // 2, dom % 2
    other = 1 - half
    core = lax.rem(band, 2)
    rank = half * 4 + band
    pairs = lax.axis_size("dom") // 2
    partner = (band, pair * 2 + other)
    sibling = (band + 1 - 2 * core, dom)

    def at_pair(step):
        return (band, lax.rem(pair + step + pairs, pairs) * 2 + half)

    def send(src, dst, ssem, rsem, device):
        return pltpu.make_async_remote_copy(
            src_ref=src, dst_ref=dst, send_sem=ssem, recv_sem=rsem, device_id=device, device_id_type=MESH)

    def member(index):
        return (lax.rem(index, 4), pair * 2 + index // 4)

    barrier = pltpu.get_barrier_semaphore()
    for n in range(1, GROUP):
        pl.semaphore_signal(barrier, inc=1, device_id=member(lax.rem(rank + n, GROUP)), device_id_type=MESH)
    for n in range(1, FAR):
        pl.semaphore_signal(barrier, inc=1, device_id=at_pair(n), device_id_type=MESH)

    loads = [pltpu.make_async_copy(orb.at[p], second.at[p], local_s.at[p]) for p in range(4)]
    for copy in loads:
        copy.start()
    lane = lax.broadcasted_iota(jnp.int32, (DEPTH, WIDE), 1)
    lower = lane < WIDE // 2
    kept = (lane // (WIDE // 2)) == half

    share = pl.ds(pl.multiple_of(core * (PROJ // 2), 16), PROJ // 2)
    twin = pl.ds(pl.multiple_of((1 - core) * (PROJ // 2), 16), PROJ // 2)
    small = [
        send(pot, pot_all.at[pl.ds(4 * half, 4)], small_s.at[0], small_r.at[0], partner),
        send(info, notes.at[1 + half], small_s.at[1], small_r.at[1], partner),
        send(raw.at[1 + half, share], raw.at[1 + half, share], small_s.at[2], small_r.at[2], partner),
    ]
    small_in = [
        send(pot, pot_all.at[pl.ds(4 * other, 4)], small_s.at[0], small_r.at[0], partner),
        send(info, notes.at[1 + other], small_s.at[1], small_r.at[1], partner),
        send(raw.at[1 + other, share], raw.at[1 + other, share], small_s.at[2], small_r.at[2], partner),
    ]
    across = send(raw.at[1 + other, share], raw.at[1 + other, share], core_s, core_r, sibling)
    across_in = send(raw.at[1 + other, twin], raw.at[1 + other, twin], core_s, core_r, sibling)
    onward = [
        send(notes.at[2], notes.at[0], next_s.at[0], next_r.at[0], at_pair(1)),
        send(raw.at[2, share], raw.at[0, share], next_s.at[1], next_r.at[1], at_pair(1)),
    ]
    last = send(raw.at[0, share], raw.at[0, share], last_s, last_r, sibling)
    last_in = send(raw.at[0, twin], raw.at[0, twin], last_s, last_r, sibling)

    def piece_rows(c):
        return pl.ds(c * PIECE, PIECE)

    def cross(c):
        at = (slice(None), piece_rows(c))
        return send(give_cross.at[at], got_cross.at[at], x_s.at[c], x_r.at[c], partner)

    def keep(c):
        at = piece_rows(c)
        return send(give_keep.at[:, at], got1.at[other, :, at], own_s.at[c], halo_r.at[other, c],
                    at_pair(2 * half - 1))

    def forward(c):
        at = piece_rows(c)
        return send(got_cross.at[:, at], got1.at[half, :, at], fwd_s.at[c], halo_r.at[half, c],
                    at_pair(1 - 2 * half))

    def halo_in(side, c):
        at = piece_rows(c)
        return send(give_keep.at[:, at], got1.at[side, :, at], own_s.at[c], halo_r.at[side, c], at_pair(1))

    notes[1 + half] = info[...]
    for a in range(PROJ // MAXPROJ):
        raw[1 + half, a * MAXPROJ : (a + 1) * MAXPROJ, :] = proj[a]
    pot_all[pl.ds(4 * half, 4)] = pot[...]
    for copy in loads:
        copy.wait()

    def pack_piece(c, carry):
        for n in range(PIECE):
            r = c * PIECE + n
            for j in range(2):
                near, far = second[j, r], second[j + 2, r]
                give_cross[j, r] = jnp.where(kept, swap(near), far)
                give_keep[j, r] = jnp.where(kept, near, swap(far))
        return carry

    def start_piece(c):
        cross(c).start()
        keep(c).start()

    lax.fori_loop(0, WINDOW, pack_piece, 0)
    pl.semaphore_wait(barrier, GROUP + FAR - 2)
    for copy in small:
        copy.start()
    for c in range(WINDOW):
        start_piece(c)
    lax.fori_loop(WINDOW, PIECES, pack_piece, 0)

    for copy in small_in:
        copy.wait_recv()
    across.start()
    for copy in onward[:1]:
        copy.start()

    def placed(group, reach):
        total = jnp.zeros((PROJ, CELLS), jnp.float32)
        for k in range(SPAN):
            flag = notes[group, :, FLAGS + reach * SPAN + k : FLAGS + reach * SPAN + k + 1]
            total = total + flag * raw[group, :, k * CELLS : (k + 1) * CELLS]
        return total

    def store_pair(p, groups, reach, slot):
        beta = jnp.concatenate([placed(group, reach) for group in groups], axis=0)
        high_part, low_part = split(beta)
        both = jnp.concatenate([high_part, low_part], axis=0)
        for n in range(STRIPS):
            left[p, n, slot * 128 : (slot + 1) * 128, :] = both[:, n * AREA : (n + 1) * AREA]
        high32 = high_part.astype(jnp.float32)
        wide = jnp.concatenate([high32, low_part.astype(jnp.float32)], axis=0)
        turned = wide.T.astype(jnp.bfloat16)
        right[p, :, slot * 256 : slot * 256 + 128] = turned
        right[p, :, slot * 256 + 128 : slot * 256 + 192] = turned[:, :64]
        right[p, :, slot * 256 + 192 : slot * 256 + 256] = jnp.zeros((CELLS, 64), jnp.bfloat16)

    diagonal = lax.broadcasted_iota(jnp.int32, (DEPTH, DEPTH), 0) == lax.broadcasted_iota(
        jnp.int32, (DEPTH, DEPTH), 1)
    constant = -1.5 * center_weight - 7.0

    def spread(n, carry):
        p, r = n // ROWS, lax.rem(n, ROWS)
        columns = []
        for extra in (0, 4):
            line = jnp.broadcast_to(pot_all[p + extra, pl.ds(r, 1), :], (DEPTH, DEPTH))
            columns.append(jnp.sum(jnp.where(diagonal, line, 0.0), axis=1, keepdims=True))
        shift_pot[p, r] = jnp.where(lower, columns[0], columns[1]) + constant
        return carry

    def receive_piece(c):
        cross(c).wait_recv()
        forward(c).start()
        cross(c).wait_send()
        keep(c).wait_send()
        if c + WINDOW < PIECES:
            start_piece(c + WINDOW)

        def one(n, carry):
            r = c * PIECE + n
            for j in range(2):
                arrived = got_cross[j, r]
                e1[4 + j, r] = jnp.where(kept, second[j, r], arrived)
                e1[6 + j, r] = jnp.where(kept, second[j + 2, r], swap(arrived))
            return carry

        lax.fori_loop(0, PIECE, one, 0)

    for p in (2, 3):
        left[p, :, 128:256, :] = jnp.zeros((STRIPS, 128, AREA), jnp.bfloat16)
        right[p, :, 256:512] = jnp.zeros((CELLS, 256), jnp.bfloat16)
    def spread_rows(n):
        lax.fori_loop(n * 4 * ROWS // PIECES, (n + 1) * 4 * ROWS // PIECES, spread, 0)

    def add_strip(field, strip):
        def part(p, total):
            cells = field[4 + p, pl.ds(strip * STRIP, STRIP)].reshape(AREA, WIDE)
            both = jnp.concatenate(split(cells), axis=1)
            return total + lax.dot_general(
                left[p, strip], both, (((1,), (0,)), ((), ())), preferred_element_type=jnp.float32)

        corr_sum[...] = lax.fori_loop(0, 4, part, corr_sum[...])

    def share_sums(phase):
        total = corr_sum[:, :WIDE] + corr_sum[:, WIDE:]
        corr_sum[...] = jnp.zeros_like(corr_sum)
        near, tail = total[0:64] + total[64:128], total[128:192] + total[192:256]
        corr[phase, 0] = tail[:PROJ]
        corr[phase, 1] = near[PROJ:]
        corr[phase, 2] = near[:PROJ] + swap(tail[PROJ:])
        down = send(corr.at[phase, 0], corr_in.at[phase, 1], corr_s.at[phase, 0], corr_r.at[phase, 1], at_pair(-1))
        up = send(corr.at[phase, 1], corr_in.at[phase, 0], corr_s.at[phase, 1], corr_r.at[phase, 0], at_pair(1))
        down.start()
        up.start()
        return [down, up]

    def weigh(phase, copies):
        for copy in copies:
            copy.wait_recv()
        before = corr[phase, 0] + swap(corr_in[phase, 0])
        after = corr[phase, 1] + swap(corr_in[phase, 1])
        before, own, after = (
            dot_f32(notes[group, :, :PROJ], value, ((1,), (0,)))
            for group, value in ((0, before), (1, corr[phase, 2]), (2, after))
        )
        in_low = lax.broadcasted_iota(jnp.int32, (PROJ, WIDE), 1) < WIDE // 2
        zero = jnp.zeros((64, WIDE), jnp.bfloat16)
        parts = []
        for low_value, high_value in ((own, after), (before, swap(own))):
            value = jnp.concatenate(
                [jnp.where(in_low, low_value, 0.0), jnp.where(in_low, 0.0, high_value)], axis=0)
            high_part, low_part = split(value)
            parts += [high_part, high_part, low_part, zero]
        weights[...] = jnp.concatenate(parts, axis=0)

    def open_strip(field, got, strip):
        def one(n, carry):
            r = strip * STRIP + n
            for j in range(2):
                near, far = field[4 + j, r], field[6 + j, r]
                up, down = got[0, j, r], got[1, j, r]
                field[j, r] = swap(jnp.where(lower, near, up))
                field[2 + j, r] = jnp.where(lower, up, swap(far))
                field[8 + j, r] = swap(jnp.where(lower, down, near))
                field[10 + j, r] = jnp.where(lower, swap(far), down)
            return carry

        lax.fori_loop(0, STRIP, one, 0)

    def apply(field, strip, scale, write):
        def plane(p, carry):
            product = lax.dot_general(
                right[p, pl.ds(pl.multiple_of(strip * AREA, AREA), AREA), :], weights[...],
                (((1,), (0,)), ((), ())), preferred_element_type=jnp.float32)
            nonlocal_plane[...] = product.reshape(STRIP, DEPTH, WIDE)

            def row(n, inner):
                r = strip * STRIP + n
                centre = field[p + 4, r]
                total = centre * shift_pot[p, r] + nonlocal_plane[n]
                for k in range(1, 5):
                    pair_x = field[p + 4 + k, r] + field[p + 4 - k, r]
                    pair_y = field[p + 4, lax.rem(r + k, ROWS)] + field[p + 4, lax.rem(r + ROWS - k, ROWS)]
                    pair_z = pltpu.roll(centre, k, 0) + pltpu.roll(centre, DEPTH - k, 0)
                    total = total + (-0.5 * side_weights[k - 1]) * ((pair_x + pair_y) + pair_z)
                write(p, r, total * scale)
                return inner

            lax.fori_loop(0, STRIP, row, 0)
            return carry

        lax.fori_loop(0, 4, plane, 0)

    def open_first(strip):
        for side in range(2):
            for n in range(STRIP // PIECE):
                halo_in(side, strip * (STRIP // PIECE) + n).wait_recv()
        open_strip(e1, got1, strip)

    spread_rows(0)
    across_in.wait_recv()
    onward[1].start()
    receive_piece(0)
    store_pair(0, (1, 2), 0, 0)
    store_pair(1, (1, 2), 1, 0)
    spread_rows(1)
    receive_piece(1)
    store_pair(2, (1, 2), 2, 0)
    store_pair(3, (1, 2), 3, 0)
    spread_rows(2)
    receive_piece(2)
    for copy in onward:
        copy.wait_recv()
    last.start()
    spread_rows(3)
    spread_rows(4)
    receive_piece(3)
    last_in.wait_recv()
    store_pair(0, (0, 1), 4, 1)
    store_pair(1, (0, 1), 5, 1)
    corr_sum[...] = jnp.zeros_like(corr_sum)
    add_strip(e1, 0)
    receive_piece(4)
    spread_rows(5)
    add_strip(e1, 1)
    receive_piece(5)
    spread_rows(6)
    open_first(0)
    receive_piece(6)
    spread_rows(7)
    add_strip(e1, 2)
    receive_piece(7)
    add_strip(e1, 3)
    copies1 = share_sums(0)
    for strip in range(1, STRIPS):
        open_first(strip)
    for c in range(PIECES):
        forward(c).wait_send()
    weigh(0, copies1)

    def write_first(p, r, value):
        e2[p + 4, r] = value

    def up2(c):
        at = piece_rows(c)
        return send(give_cross.at[:, at], got2.at[0, :, at], y2_s.at[0, c], y2_r.at[0, c], at_pair(1))

    def down2(c):
        at = piece_rows(c)
        return send(give_keep.at[:, at], got2.at[1, :, at], y2_s.at[1, c], y2_r.at[1, c], at_pair(-1))

    def first_strip(strip):
        apply(e1, strip, 1.0 / 6.0, write_first)

        def pack(n, inner):
            r = strip * STRIP + n
            for j in range(2):
                near, turned = e2[4 + j, r], swap(e2[6 + j, r])
                give_cross[j, r] = jnp.where(lower, turned, near)
                give_keep[j, r] = jnp.where(lower, near, turned)
            return inner

        lax.fori_loop(0, STRIP, pack, 0)
        for c in range(2 * strip, 2 * strip + 2):
            if c < WINDOW:
                up2(c).start()
                down2(c).start()
        add_strip(e2, strip)

    for strip in range(STRIPS):
        first_strip(strip)
    copies2 = share_sums(1)
    weigh(1, copies2)

    def write_second(p, r, value):
        second[p, r] = value - e1[p + 4, r]

    def give(index, part):
        src = second.at[index // 2, pl.ds(lax.rem(index, 2) * 16 + part * STRIP, STRIP)]
        return send(src, slab.at[rank, pl.ds(part * STRIP, STRIP)], out_s.at[index, part], out_r.at[rank, part],
                    member(index))

    def own_part(part):
        src = second.at[rank // 2, pl.ds(lax.rem(rank, 2) * 16 + part * STRIP, STRIP)]
        return pltpu.make_async_copy(src, slab.at[rank, pl.ds(part * STRIP, STRIP)], self_s.at[part])

    def second_strip(strip):
        for c in range(2 * strip, 2 * strip + 2):
            for copy in (up2(c), down2(c)):
                copy.wait_recv()
                copy.wait_send()
            if c + WINDOW < PIECES:
                up2(c + WINDOW).start()
                down2(c + WINDOW).start()
        open_strip(e2, got2, strip)
        apply(e2, strip, 1.0 / 3.0, write_second)
        part = strip % 2
        for n in range(4):
            index = 2 * lax.rem(n + rank // 2 + 2, 4) + strip // 2
            pl.when(index != rank)(lambda index=index: give(index, part).start())
        pl.when(lax.rem(rank, 2) == strip // 2)(own_part(part).start)

    for strip in range(STRIPS):
        second_strip(strip)

    blocks = tri_blocks(NORB)
    pack[...] = jnp.zeros_like(pack)

    def repack(n, carry):
        cells = pl.ds(pl.multiple_of(n * DEPTH, 16), DEPTH)
        more = pl.ds(pl.multiple_of(CELLS // 2 + n * DEPTH, 16), DEPTH)
        for b in range(4):
            at = slice(b * WIDE, (b + 1) * WIDE)
            here, there = slab[b, n], slab[4 + b, n]
            high_cells[cells, at], low_cells[cells, at] = split(jnp.where(lower, here, swap(there)))
            high_cells[more, at], low_cells[more, at] = split(jnp.where(lower, swap(here), there))
        return carry

    def add_gram(part):
        contract = (((0,), (0,)), ((), ()))

        def chunk(side, carry):
            cells = pl.ds(pl.multiple_of(side * (CELLS // 2) + part * AREA, 16), AREA)
            for i in range(NORB // B):
                own, wide = slice(i * B, (i + 1) * B), slice(0, (i + 1) * B)
                row = lax.dot_general(
                    high_cells[cells, own], high_cells[cells, wide], contract, preferred_element_type=jnp.float32)
                row += lax.dot_general(
                    high_cells[cells, own], low_cells[cells, wide], contract, preferred_element_type=jnp.float32)
                row += lax.dot_general(
                    low_cells[cells, own], high_cells[cells, wide], contract, preferred_element_type=jnp.float32)
                for j in range(i + 1):
                    n = blocks.index((i, j))
                    pack[n * B : (n + 1) * B, :] += row[:, j * B : (j + 1) * B]
            return carry

        lax.fori_loop(0, 2, chunk, 0)

    for part in range(2):
        for n in range(1, GROUP):
            index = lax.rem(rank + n, GROUP)
            send(second.at[0, pl.ds(0, STRIP)], slab.at[index, pl.ds(part * STRIP, STRIP)], out_s.at[index, part],
                 out_r.at[index, part], member(index)).wait_recv()
        own_part(part).wait()
        lax.fori_loop(part * STRIP, (part + 1) * STRIP, repack, 0)
        add_gram(part)

    for copy in small + [across, last] + onward + copies1 + copies2:
        copy.wait_send()
    for n in range(1, GROUP):
        for part in range(2):
            give(lax.rem(rank + n, GROUP), part).wait_send()
    finish_part(factor, gram_ref, filtered_ref, high_cells, low_cells, pack, *rest[:5], second, *rest[5:])


def run(orbitals, potential, projectors, info, factor):
    dma = pltpu.SemaphoreType.DMA
    f32, bf16 = jnp.float32, jnp.bfloat16
    vmem, hbm = pl.BlockSpec(memory_space=pltpu.VMEM), pl.BlockSpec(memory_space=pl.ANY)
    block = (ROWS, DEPTH, WIDE)
    packed = len(tri_blocks(NORB)) * B
    share = packed // NEAR
    return pl.pallas_call(
        functools.partial(whole_kernel, factor),
        out_shape=[jax.ShapeDtypeStruct((NORB, NORB), f32), jax.ShapeDtypeStruct((4,) + block, f32)],
        in_specs=[hbm, vmem, vmem, vmem],
        out_specs=[vmem, hbm],
        scratch_shapes=[
            pltpu.VMEM((12,) + block, f32),
            pltpu.VMEM((12,) + block, f32),
            pltpu.VMEM((4,) + block, f32),
            pltpu.VMEM((4,) + block, f32),
            pltpu.VMEM((STRIP, DEPTH, WIDE), f32),
            pltpu.VMEM((4, STRIPS, 256, AREA), bf16),
            pltpu.VMEM((4, CELLS, 512), bf16),
            pltpu.VMEM((3, PROJ, SPAN * CELLS), f32),
            pltpu.VMEM((3, PROJ, 128), f32),
            pltpu.VMEM((8, ROWS, DEPTH), f32),
            pltpu.VMEM((256, 2 * WIDE), f32),
            pltpu.VMEM((2, 3, PROJ, WIDE), f32),
            pltpu.VMEM((2, 2, PROJ, WIDE), f32),
            pltpu.VMEM((512, WIDE), bf16),
            pltpu.VMEM((2,) + block, f32),
            pltpu.VMEM((2,) + block, f32),
            pltpu.VMEM((2,) + block, f32),
            pltpu.VMEM((2, 2) + block, f32),
            pltpu.VMEM((2, 2) + block, f32),
            pltpu.VMEM((GROUP, ROWS // 2, DEPTH, WIDE), f32),
            dma((4,)), dma((PIECES,)), dma((PIECES,)), dma((PIECES,)), dma((PIECES,)), dma((2, PIECES)),
            dma((3,)), dma((3,)), dma(()), dma(()), dma((2,)), dma((2,)), dma(()), dma(()),
            dma((2, 2)), dma((2, 2)), dma((2, PIECES)), dma((2, PIECES)),
            dma((GROUP, 2)), dma((GROUP, 2)), dma((2,)),
            pltpu.VMEM((CELLS, NORB), bf16),
            pltpu.VMEM((CELLS, NORB), bf16),
            pltpu.VMEM((packed, B), f32),
            pltpu.VMEM((NEAR, share, B), f32),
            pltpu.VMEM((share, B), f32),
            pltpu.VMEM((FAR, share // SUMMERS, B), f32),
            pltpu.VMEM((packed, B), f32),
            pltpu.VMEM((NORB, NORB), f32),
            dma((NEAR,)), dma((NEAR,)), dma((FAR,)), dma((FAR,)),
            dma((FAR,)), dma((FAR,)), dma((NEAR,)), dma((NEAR,)),
            dma(()), dma((4, 2)), dma((NEAR,)),
        ],
        compiler_params=pltpu.CompilerParams(collective_id=2, has_side_effects=True, vmem_limit_bytes=62 * 2**20),
    )(orbitals, potential, projectors, info)


def shards(orbitals, potential, projectors, coupling, atom_plane, projector_count):
    planes, side_y, side_z, local_orbs = orbitals.shape
    atoms = projectors.shape[0]
    first_plane = atom_plane - lax.axis_index("dom") * planes
    reach_ids = jnp.arange(REACH, dtype=jnp.int32)
    span_ids = jnp.arange(SPAN, dtype=jnp.int32)
    flags = (
        reach_ids[None, :, None] == first_plane[:, None, None] + span_ids[None, None, :]
    ).astype(jnp.float32).reshape(atoms, 1, REACH * SPAN)
    flags = jnp.broadcast_to(flags, (atoms, MAXPROJ, REACH * SPAN)).reshape(PROJ, REACH * SPAN)
    slots = jnp.arange(MAXPROJ, dtype=jnp.int32)
    live_mask = (slots[None, :] < projector_count[:, None]).astype(jnp.float32)
    sym_coupling = 0.5 * (coupling + jnp.transpose(coupling, (0, 2, 1)))
    sym_coupling = sym_coupling * live_mask[:, :, None] * live_mask[:, None, :]
    same_atom = jnp.eye(atoms, dtype=jnp.float32)
    blocks = (sym_coupling[:, :, None, :] * same_atom[:, None, :, None]).reshape(PROJ, PROJ)
    info = jnp.concatenate(
        [blocks, flags, jnp.zeros((PROJ, 128 - PROJ - REACH * SPAN), jnp.float32)], axis=1)
    total_cells = planes * side_y * side_z * lax.axis_size("dom")
    gram, filtered = run(orbitals, potential, projectors, info, 1.0 / total_cells)
    return (filtered, gram)


def solution(mesh):
    placed = (
        P("dom", None, None, "band"),
        P("dom", None, None),
        P("dom", None, None),
        P("dom", None, None),
        P("dom"),
        P("dom"),
    )
    return jax.shard_map(
        shards,
        mesh=mesh,
        in_specs=placed,
        out_specs=(P("dom", None, None, "band"), P()),
        check_vma=False,
    )
```

```python
import functools

import jax
import jax.numpy as jnp
from jax import lax
from jax.experimental import pallas as pl
from jax.experimental.pallas import tpu as pltpu
from jax.sharding import PartitionSpec as P

NORB = 512
HALO = 4
SPAN = 3
MAXPROJ = 4
B = 128

center_weight = -205.0 / 72.0
side_weights = (8.0 / 5.0, -1.0 / 5.0, 8.0 / 315.0, -1.0 / 560.0)
HIGH = lax.Precision.HIGHEST


HIGHEST = lax.Precision.HIGHEST


def dot_f32(a, b, dims):
    return lax.dot_general(a, b, (dims, ((), ())), precision=HIGHEST, preferred_element_type=jnp.float32)


def block_inverse(tiles):
    count = len(tiles)
    tiles = list(tiles)
    shape = tiles[0].shape
    lane = lax.broadcasted_iota(jnp.int32, shape, 1)
    sub = lax.broadcasted_iota(jnp.int32, shape, 0)
    done = []
    for j in range(count):
        base = 8 * j
        cols = [
            [jnp.broadcast_to(tiles[t][:, base + k : base + k + 1], shape) for k in range(8)]
            for t in range(j, count)
        ]
        inside = (lane >= base) & (lane < base + 8)
        unit = jnp.where(lane == sub + base, 1.0, 0.0)
        own = jnp.where(inside, unit, tiles[j])
        rows = [jnp.broadcast_to(own[k : k + 1, :], shape) for k in range(8)]
        splat = [
            [jnp.broadcast_to(cols[0][k][i : i + 1, :], shape) if i >= k else None for k in range(8)]
            for i in range(8)
        ]
        rest = [jnp.where(inside, 0.0, tiles[t]) for t in range(j + 1, count)]
        result = jnp.zeros(shape, jnp.float32)
        for k in range(8):
            scale = lax.rsqrt(splat[k][k])
            rows[k] = rows[k] * scale
            for i in range(k + 1, 8):
                splat[i][k] = splat[i][k] * scale
            for i in range(k + 1, 8):
                for m in range(k + 1, i + 1):
                    splat[i][m] = splat[i][m] - splat[i][k] * splat[m][k]
                rows[i] = rows[i] - splat[i][k] * rows[k]
            for t in range(len(rest)):
                below = cols[t + 1]
                below[k] = below[k] * scale
                for m in range(k + 1, 8):
                    below[m] = below[m] - below[k] * splat[m][k]
                rest[t] = rest[t] - below[k] * rows[k]
            result = jnp.where(sub == k, rows[k], result)
        done.append(jnp.where(lane <= sub + base, result, 0.0))
        tiles[j + 1 :] = rest
    return done


def factor_steps(work, begin, complete, done):
    size = work.shape[0]

    def step(k, carry):
        at = pl.ds(pl.multiple_of(k * B, B), B)
        pl.when(k == 0)(begin)
        tiles = [work[pl.ds(pl.multiple_of(k * B + 8 * t, 8), 8), at] for t in range(B // 8)]
        corner = jnp.concatenate(block_inverse(tiles), axis=0)
        pl.when(k == 0)(complete)
        row_id = lax.broadcasted_iota(jnp.int32, (size, B), 0)
        column = jnp.where(row_id >= (k + 1) * B, work[:, at], 0.0)
        unit = lax.broadcasted_iota(jnp.int32, (B, B), 0) == lax.broadcasted_iota(jnp.int32, (B, B), 1)
        work[at, at] = jnp.where(unit, 1.0, 0.0)
        scaled = dot_f32(corner, work[at, :], ((1,), (0,)))
        row_at = lax.broadcasted_iota(jnp.int32, (B, size), 0) + k * B
        done(k, jnp.where(lax.broadcasted_iota(jnp.int32, (B, size), 1) <= row_at, scaled, 0.0))
        below = dot_f32(column, corner, ((1,), (1,)))
        block = work[:, at]
        work[:, at] = jnp.where(row_id >= (k + 1) * B, 0.0, block)
        work[...] = work[...] - dot_f32(below, scaled, ((1,), (0,)))
        return carry

    lax.fori_loop(0, size // B, step, 0)


MESH = pl.DeviceIdType.MESH
NEAR = 8
FAR = 16
SUMMERS = 10


def tri_blocks(size):
    return [(i, j) for i in range(size // B) for j in range(i + 1)]


def finish_part(
    factor, gram_ref, filtered_ref,
    high, low, pack, near, mine, far, total, work, parts, near_s, near_r, far_s, far_r, out_s, out_r, end_s, end_r,
    local_s, home_s, home_r,
):
    band, dom = lax.axis_index("band"), lax.axis_index("dom")
    pair, half = dom // 2, dom % 2
    rank = half * 4 + band
    blocks = tri_blocks(work.shape[0])
    share = len(blocks) * B // NEAR
    piece = share // SUMMERS

    def near_peer(step):
        other = (rank + step) % NEAR
        return other, (other % 4, pair * 2 + other // 4)

    def far_peer(step):
        other = (pair + step) % FAR
        return other, (band, other * 2 + half)

    def rows(index, count):
        return pl.ds(pl.multiple_of(index * count, 8), count)

    def near_copy(step):
        other, device = near_peer(step)
        return pltpu.make_async_remote_copy(
            src_ref=pack.at[rows(other, share)], dst_ref=near.at[rank],
            send_sem=near_s.at[step], recv_sem=near_r.at[rank], device_id=device, device_id_type=MESH)

    def near_arrival(step):
        other, device = near_peer(step)
        return pltpu.make_async_remote_copy(
            src_ref=pack.at[rows(other, share)], dst_ref=near.at[other],
            send_sem=near_s.at[step], recv_sem=near_r.at[other], device_id=device, device_id_type=MESH)

    for step in range(1, NEAR):
        near_copy(step).start()
    near[rank] = pack[rows(rank, share), :]
    for step in range(1, NEAR):
        near_arrival(step).wait_recv()
    acc = near[0]
    for n in range(1, NEAR):
        acc = acc + near[n]
    mine[...] = acc

    def far_copy(step, slot):
        other, device = far_peer(step)
        return other, pltpu.make_async_remote_copy(
            src_ref=mine.at[rows(other % SUMMERS, piece)], dst_ref=far.at[pair if slot is None else other],
            send_sem=far_s.at[step], recv_sem=far_r.at[pair if slot is None else other],
            device_id=device, device_id_type=MESH)

    for step in range(1, FAR):
        other, copy = far_copy(step, None)
        pl.when(other < SUMMERS)(copy.start)

    place = rank * share

    def out_rows(index):
        return pl.ds(pl.multiple_of(place + (index % SUMMERS) * piece, 8), piece)

    def out_copy(step):
        other, device = far_peer(step)
        return pltpu.make_async_remote_copy(
            src_ref=total.at[out_rows(pair)], dst_ref=total.at[out_rows(pair)],
            send_sem=out_s.at[step], recv_sem=out_r.at[pair], device_id=device, device_id_type=MESH)

    def out_arrival(step):
        other, device = far_peer(step)
        return other, pltpu.make_async_remote_copy(
            src_ref=total.at[out_rows(other)], dst_ref=total.at[out_rows(other)],
            send_sem=out_s.at[step], recv_sem=out_r.at[other], device_id=device, device_id_type=MESH)

    @pl.when(pair < SUMMERS)
    def _():
        far[pair] = mine[rows(pair % SUMMERS, piece), :]
        for step in range(1, FAR):
            far_copy(step, 1)[1].wait_recv()
        acc = far[0]
        for n in range(1, FAR):
            acc = acc + far[n]
        total[out_rows(pair), :] = acc * factor
        for step in range(1, FAR):
            out_copy(step).start()

    for step in range(1, FAR):
        other, copy = out_arrival(step)
        pl.when(other < SUMMERS)(copy.wait_recv)

    def end_copy(step, slot):
        other, device = near_peer(step)
        at = rows(rank if slot is None else other, share)
        return pltpu.make_async_remote_copy(
            src_ref=total.at[at], dst_ref=total.at[at],
            send_sem=end_s.at[step], recv_sem=end_r.at[rank if slot is None else other],
            device_id=device, device_id_type=MESH)

    for step in range(1, NEAR):
        end_copy(step, None).start()

    def share_in(index):
        at = rows(index, share)
        return pltpu.make_async_remote_copy(
            src_ref=total.at[at], dst_ref=total.at[at], send_sem=end_s.at[1], recv_sem=end_r.at[index],
            device_id=near_peer(1)[1], device_id_type=MESH)

    def begin():
        pl.when(rank != 0)(share_in(0).wait_recv)
        work[:B, :B] = total[:B, :]

    def complete():
        for index in range(1, NEAR):
            pl.when(rank != index)(share_in(index).wait_recv)
        for n, (i, j) in enumerate(blocks):
            block = total[n * B : (n + 1) * B, :]
            gram_ref[i * B : (i + 1) * B, j * B : (j + 1) * B] = block
            if i != j:
                gram_ref[j * B : (j + 1) * B, i * B : (i + 1) * B] = block.T
        work[...] = gram_ref[...]

    def target(index):
        return filtered_ref.at[index // 2, pl.ds(pl.multiple_of(lax.rem(index, 2) * 16, 8), ROWS // 2)]

    def move(k, to_half):
        return pltpu.make_async_remote_copy(
            src_ref=parts.at[k, rows(to_half, ROWS // 2)], dst_ref=target(rank), send_sem=home_s.at[k, to_half],
            recv_sem=home_r.at[rank], device_id=(k, pair * 2 + to_half), device_id_type=MESH)

    local = pltpu.make_async_copy(parts.at[band, rows(half, ROWS // 2)], target(rank), local_s)
    across = (((1,), (1,)), ((), ()))
    cells = high.shape[0] // 2

    def rotate(k, inverse_rows):
        high_rot, low_rot = split(inverse_rows)
        both = jnp.concatenate([high_rot, low_rot], axis=0)
        for to_half in range(2):
            at = slice(to_half * cells, (to_half + 1) * cells)
            wide = lax.dot_general(high[at, :], both, across, preferred_element_type=jnp.float32)
            more = lax.dot_general(low[at, :], high_rot, across, preferred_element_type=jnp.float32)
            value = wide[:, :B] + (wide[:, B:] + more)
            parts[k, rows(to_half, ROWS // 2)] = value.reshape(ROWS // 2, DEPTH, B)
            here = (k == band) & (to_half == half)
            pl.when(jnp.logical_not(here))(lambda to_half=to_half: move(k, to_half).start())
            pl.when(here)(local.start)

    factor_steps(work, begin, complete, rotate)
    for step in range(1, NEAR):
        other, device = near_peer(step)
        pltpu.make_async_remote_copy(
            src_ref=parts.at[0, rows(0, ROWS // 2)], dst_ref=target(other), send_sem=home_s.at[0, 0], recv_sem=home_r.at[other],
            device_id=device, device_id_type=MESH).wait_recv()
    local.wait()
    for k in range(4):
        for to_half in range(2):
            here = (k == band) & (to_half == half)
            pl.when(jnp.logical_not(here))(lambda k=k, to_half=to_half: move(k, to_half).wait_send())

    for step in range(1, NEAR):
        near_copy(step).wait_send()
        end_copy(step, None).wait_send()
    for step in range(1, FAR):
        other, copy = far_copy(step, None)
        pl.when(other < SUMMERS)(copy.wait_send)

    @pl.when(pair < SUMMERS)
    def _():
        for step in range(1, FAR):
            out_copy(step).wait_send()


ROWS = 32
DEPTH = 48
WIDE = 128
CELLS = ROWS * DEPTH
PROJ = 32
REACH = 6
FLAGS = PROJ
GROUP = 8
STRIP = 8
STRIPS = ROWS // STRIP
PIECE = 4
PIECES = ROWS // PIECE
WINDOW = 3
AREA = STRIP * DEPTH


def split(value):
    high = value.astype(jnp.bfloat16)
    return high, (value - high.astype(jnp.float32)).astype(jnp.bfloat16)


def swap(value):
    return pltpu.roll(value, WIDE // 2, value.ndim - 1)


def whole_kernel(
    factor, orb, pot, proj, coupling, planes, counts, gram_ref, filtered_ref,
    e1, e2, second, shift_pot, nonlocal_plane, left, right, raw, notes, scratch_notes, pot_all, corr_sum, corr, corr_in, weights,
    give_cross, give_keep, got_cross, got1, got2, slab,
    local_s, x_s, x_r, own_s, fwd_s, halo_r, small_s, small_r, core_s, core_r, next_s, next_r, last_s, last_r,
    corr_s, corr_r, y2_s, y2_r, out_s, out_r, self_s,
    high_cells, low_cells, pack, *rest,
):
    band, dom = lax.axis_index("band"), lax.axis_index("dom")
    pair, half = dom // 2, dom % 2
    other = 1 - half
    core = lax.rem(band, 2)
    rank = half * 4 + band
    pairs = lax.axis_size("dom") // 2
    partner = (band, pair * 2 + other)
    sibling = (band + 1 - 2 * core, dom)

    def at_pair(step):
        return (band, lax.rem(pair + step + pairs, pairs) * 2 + half)

    def send(src, dst, ssem, rsem, device):
        return pltpu.make_async_remote_copy(
            src_ref=src, dst_ref=dst, send_sem=ssem, recv_sem=rsem, device_id=device, device_id_type=MESH)

    def member(index):
        return (lax.rem(index, 4), pair * 2 + index // 4)

    barrier = pltpu.get_barrier_semaphore()
    for n in range(1, GROUP):
        pl.semaphore_signal(barrier, inc=1, device_id=member(lax.rem(rank + n, GROUP)), device_id_type=MESH)
    for n in range(1, FAR):
        pl.semaphore_signal(barrier, inc=1, device_id=at_pair(n), device_id_type=MESH)

    loads = [pltpu.make_async_copy(orb.at[p], second.at[p], local_s.at[p]) for p in range(4)]
    for copy in loads:
        copy.start()
    lane = lax.broadcasted_iota(jnp.int32, (DEPTH, WIDE), 1)
    lower = lane < WIDE // 2
    kept = (lane // (WIDE // 2)) == half

    share = pl.ds(pl.multiple_of(core * (PROJ // 2), 16), PROJ // 2)
    twin = pl.ds(pl.multiple_of((1 - core) * (PROJ // 2), 16), PROJ // 2)
    small = [
        send(pot, pot_all.at[pl.ds(4 * half, 4)], small_s.at[0], small_r.at[0], partner),
        send(notes.at[1 + half], notes.at[1 + half], small_s.at[1], small_r.at[1], partner),
        send(raw.at[1 + half, share], raw.at[1 + half, share], small_s.at[2], small_r.at[2], partner),
    ]
    small_in = [
        send(pot, pot_all.at[pl.ds(4 * other, 4)], small_s.at[0], small_r.at[0], partner),
        send(notes.at[1 + other], notes.at[1 + other], small_s.at[1], small_r.at[1], partner),
        send(raw.at[1 + other, share], raw.at[1 + other, share], small_s.at[2], small_r.at[2], partner),
    ]
    across = send(raw.at[1 + other, share], raw.at[1 + other, share], core_s, core_r, sibling)
    across_in = send(raw.at[1 + other, twin], raw.at[1 + other, twin], core_s, core_r, sibling)
    onward = [
        send(notes.at[2], notes.at[0], next_s.at[0], next_r.at[0], at_pair(1)),
        send(raw.at[2, share], raw.at[0, share], next_s.at[1], next_r.at[1], at_pair(1)),
    ]
    last = send(raw.at[0, share], raw.at[0, share], last_s, last_r, sibling)
    last_in = send(raw.at[0, twin], raw.at[0, twin], last_s, last_r, sibling)

    def piece_rows(c):
        return pl.ds(c * PIECE, PIECE)

    def cross(c):
        at = (slice(None), piece_rows(c))
        return send(give_cross.at[at], got_cross.at[at], x_s.at[c], x_r.at[c], partner)

    def keep(c):
        at = piece_rows(c)
        return send(give_keep.at[:, at], got1.at[other, :, at], own_s.at[c], halo_r.at[other, c],
                    at_pair(2 * half - 1))

    def forward(c):
        at = piece_rows(c)
        return send(got_cross.at[:, at], got1.at[half, :, at], fwd_s.at[c], halo_r.at[half, c],
                    at_pair(1 - 2 * half))

    def halo_in(side, c):
        at = piece_rows(c)
        return send(give_keep.at[:, at], got1.at[side, :, at], own_s.at[c], halo_r.at[side, c], at_pair(1))

    line = lax.broadcasted_iota(jnp.int32, (PROJ, WIDE), 0)
    column = lax.broadcasted_iota(jnp.int32, (PROJ, WIDE), 1)
    start, live = jnp.zeros_like(line), jnp.zeros_like(line)
    for a in range(PROJ // MAXPROJ):
        at_atom = (line >> 2) == a
        start = jnp.where(at_atom, planes[a] - dom * 4, start)
        live = jnp.where(at_atom, counts[a], live)
        scratch_notes[a * MAXPROJ : (a + 1) * MAXPROJ, 0:MAXPROJ] = coupling[a]
    same = (line >> 2) == (column >> 2)
    spread_out = jnp.zeros((PROJ, WIDE), jnp.float32)
    for j in range(MAXPROJ):
        value = jnp.broadcast_to(scratch_notes[:, j : j + 1], (PROJ, WIDE))
        spread_out = jnp.where(same & ((column & 3) == j), value, spread_out)
    square = jnp.concatenate([spread_out, jnp.zeros((WIDE - PROJ, WIDE), jnp.float32)], axis=0)
    symmetric = 0.5 * (spread_out + square.T[:PROJ])
    symmetric = jnp.where(((line & 3) < live) & ((column & 3) < live), symmetric, 0.0)
    wanted = jnp.full((PROJ, WIDE), -WIDE, jnp.int32)
    for reach in range(REACH):
        for k in range(SPAN):
            wanted = jnp.where(column == FLAGS + reach * SPAN + k, reach - k, wanted)
    flag_rows = jnp.where(wanted == start, 1.0, 0.0)
    notes[1 + half] = jnp.where(column < FLAGS, symmetric, flag_rows)
    for a in range(PROJ // MAXPROJ):
        raw[1 + half, a * MAXPROJ : (a + 1) * MAXPROJ, :] = proj[a]
    pot_all[pl.ds(4 * half, 4)] = pot[...]
    for copy in loads:
        copy.wait()

    def pack_piece(c, carry):
        for n in range(PIECE):
            r = c * PIECE + n
            for j in range(2):
                near, far = second[j, r], second[j + 2, r]
                give_cross[j, r] = jnp.where(kept, swap(near), far)
                give_keep[j, r] = jnp.where(kept, near, swap(far))
        return carry

    def start_piece(c):
        cross(c).start()
        keep(c).start()

    lax.fori_loop(0, WINDOW, pack_piece, 0)
    pl.semaphore_wait(barrier, GROUP + FAR - 2)
    for copy in small:
        copy.start()
    for c in range(WINDOW):
        start_piece(c)
    lax.fori_loop(WINDOW, PIECES, pack_piece, 0)

    for copy in small_in:
        copy.wait_recv()
    across.start()
    for copy in onward[:1]:
        copy.start()

    def placed(group, reach):
        total = jnp.zeros((PROJ, CELLS), jnp.float32)
        for k in range(SPAN):
            flag = notes[group, :, FLAGS + reach * SPAN + k : FLAGS + reach * SPAN + k + 1]
            total = total + flag * raw[group, :, k * CELLS : (k + 1) * CELLS]
        return total

    def store_pair(p, groups, reach, slot):
        beta = jnp.concatenate([placed(group, reach) for group in groups], axis=0)
        high_part, low_part = split(beta)
        both = jnp.concatenate([high_part, low_part], axis=0)
        for n in range(STRIPS):
            left[p, n, slot * 128 : (slot + 1) * 128, :] = both[:, n * AREA : (n + 1) * AREA]
        high32 = high_part.astype(jnp.float32)
        wide = jnp.concatenate([high32, low_part.astype(jnp.float32)], axis=0)
        turned = wide.T.astype(jnp.bfloat16)
        right[p, :, slot * 256 : slot * 256 + 128] = turned
        right[p, :, slot * 256 + 128 : slot * 256 + 192] = turned[:, :64]
        right[p, :, slot * 256 + 192 : slot * 256 + 256] = jnp.zeros((CELLS, 64), jnp.bfloat16)

    diagonal = lax.broadcasted_iota(jnp.int32, (DEPTH, DEPTH), 0) == lax.broadcasted_iota(
        jnp.int32, (DEPTH, DEPTH), 1)
    constant = -1.5 * center_weight - 7.0

    def spread(n, carry):
        p, r = n // ROWS, lax.rem(n, ROWS)
        columns = []
        for extra in (0, 4):
            line = jnp.broadcast_to(pot_all[p + extra, pl.ds(r, 1), :], (DEPTH, DEPTH))
            columns.append(jnp.sum(jnp.where(diagonal, line, 0.0), axis=1, keepdims=True))
        shift_pot[p, r] = jnp.where(lower, columns[0], columns[1]) + constant
        return carry

    def receive_piece(c):
        cross(c).wait_recv()
        forward(c).start()
        cross(c).wait_send()
        keep(c).wait_send()
        if c + WINDOW < PIECES:
            start_piece(c + WINDOW)

        def one(n, carry):
            r = c * PIECE + n
            for j in range(2):
                arrived = got_cross[j, r]
                e1[4 + j, r] = jnp.where(kept, second[j, r], arrived)
                e1[6 + j, r] = jnp.where(kept, second[j + 2, r], swap(arrived))
            return carry

        lax.fori_loop(0, PIECE, one, 0)

    for p in (2, 3):
        left[p, :, 128:256, :] = jnp.zeros((STRIPS, 128, AREA), jnp.bfloat16)
        right[p, :, 256:512] = jnp.zeros((CELLS, 256), jnp.bfloat16)
    def spread_rows(n):
        lax.fori_loop(n * 4 * ROWS // PIECES, (n + 1) * 4 * ROWS // PIECES, spread, 0)

    def add_strip(field, strip):
        def part(p, total):
            cells = field[4 + p, pl.ds(strip * STRIP, STRIP)].reshape(AREA, WIDE)
            both = jnp.concatenate(split(cells), axis=1)
            return total + lax.dot_general(
                left[p, strip], both, (((1,), (0,)), ((), ())), preferred_element_type=jnp.float32)

        corr_sum[...] = lax.fori_loop(0, 4, part, corr_sum[...])

    def share_sums(phase):
        total = corr_sum[:, :WIDE] + corr_sum[:, WIDE:]
        corr_sum[...] = jnp.zeros_like(corr_sum)
        near, tail = total[0:64] + total[64:128], total[128:192] + total[192:256]
        corr[phase, 0] = tail[:PROJ]
        corr[phase, 1] = near[PROJ:]
        corr[phase, 2] = near[:PROJ] + swap(tail[PROJ:])
        down = send(corr.at[phase, 0], corr_in.at[phase, 1], corr_s.at[phase, 0], corr_r.at[phase, 1], at_pair(-1))
        up = send(corr.at[phase, 1], corr_in.at[phase, 0], corr_s.at[phase, 1], corr_r.at[phase, 0], at_pair(1))
        down.start()
        up.start()
        return [down, up]

    def weigh(phase, copies):
        for copy in copies:
            copy.wait_recv()
        before = corr[phase, 0] + swap(corr_in[phase, 0])
        after = corr[phase, 1] + swap(corr_in[phase, 1])
        before, own, after = (
            dot_f32(notes[group, :, :PROJ], value, ((1,), (0,)))
            for group, value in ((0, before), (1, corr[phase, 2]), (2, after))
        )
        in_low = lax.broadcasted_iota(jnp.int32, (PROJ, WIDE), 1) < WIDE // 2
        zero = jnp.zeros((64, WIDE), jnp.bfloat16)
        parts = []
        for low_value, high_value in ((own, after), (before, swap(own))):
            value = jnp.concatenate(
                [jnp.where(in_low, low_value, 0.0), jnp.where(in_low, 0.0, high_value)], axis=0)
            high_part, low_part = split(value)
            parts += [high_part, high_part, low_part, zero]
        weights[...] = jnp.concatenate(parts, axis=0)

    def open_strip(field, got, strip):
        def one(n, carry):
            r = strip * STRIP + n
            for j in range(2):
                near, far = field[4 + j, r], field[6 + j, r]
                up, down = got[0, j, r], got[1, j, r]
                field[j, r] = swap(jnp.where(lower, near, up))
                field[2 + j, r] = jnp.where(lower, up, swap(far))
                field[8 + j, r] = swap(jnp.where(lower, down, near))
                field[10 + j, r] = jnp.where(lower, swap(far), down)
            return carry

        lax.fori_loop(0, STRIP, one, 0)

    def apply(field, strip, scale, write):
        def plane(p, carry):
            product = lax.dot_general(
                right[p, pl.ds(pl.multiple_of(strip * AREA, AREA), AREA), :], weights[...],
                (((1,), (0,)), ((), ())), preferred_element_type=jnp.float32)
            nonlocal_plane[...] = product.reshape(STRIP, DEPTH, WIDE)

            def row(n, inner):
                r = strip * STRIP + n
                centre = field[p + 4, r]
                total = centre * shift_pot[p, r] + nonlocal_plane[n]
                for k in range(1, 5):
                    pair_x = field[p + 4 + k, r] + field[p + 4 - k, r]
                    pair_y = field[p + 4, lax.rem(r + k, ROWS)] + field[p + 4, lax.rem(r + ROWS - k, ROWS)]
                    pair_z = pltpu.roll(centre, k, 0) + pltpu.roll(centre, DEPTH - k, 0)
                    total = total + (-0.5 * side_weights[k - 1]) * ((pair_x + pair_y) + pair_z)
                write(p, r, total * scale)
                return inner

            lax.fori_loop(0, STRIP, row, 0)
            return carry

        lax.fori_loop(0, 4, plane, 0)

    def open_first(strip):
        for side in range(2):
            for n in range(STRIP // PIECE):
                halo_in(side, strip * (STRIP // PIECE) + n).wait_recv()
        open_strip(e1, got1, strip)

    spread_rows(0)
    across_in.wait_recv()
    onward[1].start()
    receive_piece(0)
    store_pair(0, (1, 2), 0, 0)
    store_pair(1, (1, 2), 1, 0)
    spread_rows(1)
    receive_piece(1)
    store_pair(2, (1, 2), 2, 0)
    store_pair(3, (1, 2), 3, 0)
    spread_rows(2)
    receive_piece(2)
    for copy in onward:
        copy.wait_recv()
    last.start()
    spread_rows(3)
    spread_rows(4)
    receive_piece(3)
    last_in.wait_recv()
    store_pair(0, (0, 1), 4, 1)
    store_pair(1, (0, 1), 5, 1)
    corr_sum[...] = jnp.zeros_like(corr_sum)
    add_strip(e1, 0)
    receive_piece(4)
    spread_rows(5)
    add_strip(e1, 1)
    receive_piece(5)
    spread_rows(6)
    open_first(0)
    receive_piece(6)
    spread_rows(7)
    add_strip(e1, 2)
    receive_piece(7)
    add_strip(e1, 3)
    copies1 = share_sums(0)
    for strip in range(1, STRIPS):
        open_first(strip)
    for c in range(PIECES):
        forward(c).wait_send()
    weigh(0, copies1)

    def write_first(p, r, value):
        e2[p + 4, r] = value

    def up2(c):
        at = piece_rows(c)
        return send(give_cross.at[:, at], got2.at[0, :, at], y2_s.at[0, c], y2_r.at[0, c], at_pair(1))

    def down2(c):
        at = piece_rows(c)
        return send(give_keep.at[:, at], got2.at[1, :, at], y2_s.at[1, c], y2_r.at[1, c], at_pair(-1))

    def first_strip(strip):
        apply(e1, strip, 1.0 / 6.0, write_first)

        def pack(n, inner):
            r = strip * STRIP + n
            for j in range(2):
                near, turned = e2[4 + j, r], swap(e2[6 + j, r])
                give_cross[j, r] = jnp.where(lower, turned, near)
                give_keep[j, r] = jnp.where(lower, near, turned)
            return inner

        lax.fori_loop(0, STRIP, pack, 0)
        for c in range(2 * strip, 2 * strip + 2):
            if c < WINDOW:
                up2(c).start()
                down2(c).start()
        add_strip(e2, strip)

    for strip in range(STRIPS):
        first_strip(strip)
    copies2 = share_sums(1)
    weigh(1, copies2)

    def write_second(p, r, value):
        second[p, r] = value - e1[p + 4, r]

    def give(index, part):
        src = second.at[index // 2, pl.ds(lax.rem(index, 2) * 16 + part * STRIP, STRIP)]
        return send(src, slab.at[rank, pl.ds(part * STRIP, STRIP)], out_s.at[index, part], out_r.at[rank, part],
                    member(index))

    def own_part(part):
        src = second.at[rank // 2, pl.ds(lax.rem(rank, 2) * 16 + part * STRIP, STRIP)]
        return pltpu.make_async_copy(src, slab.at[rank, pl.ds(part * STRIP, STRIP)], self_s.at[part])

    def second_strip(strip):
        for c in range(2 * strip, 2 * strip + 2):
            for copy in (up2(c), down2(c)):
                copy.wait_recv()
                copy.wait_send()
            if c + WINDOW < PIECES:
                up2(c + WINDOW).start()
                down2(c + WINDOW).start()
        open_strip(e2, got2, strip)
        apply(e2, strip, 1.0 / 3.0, write_second)
        part = strip % 2
        for n in range(4):
            index = 2 * lax.rem(n + rank // 2 + 2, 4) + strip // 2
            pl.when(index != rank)(lambda index=index: give(index, part).start())
        pl.when(lax.rem(rank, 2) == strip // 2)(own_part(part).start)

    for strip in range(STRIPS):
        second_strip(strip)

    blocks = tri_blocks(NORB)
    pack[...] = jnp.zeros_like(pack)

    def repack(n, carry):
        cells = pl.ds(pl.multiple_of(n * DEPTH, 16), DEPTH)
        more = pl.ds(pl.multiple_of(CELLS // 2 + n * DEPTH, 16), DEPTH)
        for b in range(4):
            at = slice(b * WIDE, (b + 1) * WIDE)
            here, there = slab[b, n], slab[4 + b, n]
            high_cells[cells, at], low_cells[cells, at] = split(jnp.where(lower, here, swap(there)))
            high_cells[more, at], low_cells[more, at] = split(jnp.where(lower, swap(here), there))
        return carry

    def add_gram(part):
        contract = (((0,), (0,)), ((), ()))

        def chunk(side, carry):
            cells = pl.ds(pl.multiple_of(side * (CELLS // 2) + part * AREA, 16), AREA)
            for i in range(NORB // B):
                own, wide = slice(i * B, (i + 1) * B), slice(0, (i + 1) * B)
                row = lax.dot_general(
                    high_cells[cells, own], high_cells[cells, wide], contract, preferred_element_type=jnp.float32)
                row += lax.dot_general(
                    high_cells[cells, own], low_cells[cells, wide], contract, preferred_element_type=jnp.float32)
                row += lax.dot_general(
                    low_cells[cells, own], high_cells[cells, wide], contract, preferred_element_type=jnp.float32)
                for j in range(i + 1):
                    n = blocks.index((i, j))
                    pack[n * B : (n + 1) * B, :] += row[:, j * B : (j + 1) * B]
            return carry

        lax.fori_loop(0, 2, chunk, 0)

    for part in range(2):
        for n in range(1, GROUP):
            index = lax.rem(rank + n, GROUP)
            send(second.at[0, pl.ds(0, STRIP)], slab.at[index, pl.ds(part * STRIP, STRIP)], out_s.at[index, part],
                 out_r.at[index, part], member(index)).wait_recv()
        own_part(part).wait()
        lax.fori_loop(part * STRIP, (part + 1) * STRIP, repack, 0)
        add_gram(part)

    for copy in small + [across, last] + onward + copies1 + copies2:
        copy.wait_send()
    for n in range(1, GROUP):
        for part in range(2):
            give(lax.rem(rank + n, GROUP), part).wait_send()
    finish_part(factor, gram_ref, filtered_ref, high_cells, low_cells, pack, *rest[:5], second, *rest[5:])


def run(orbitals, potential, projectors, coupling, atom_plane, projector_count, factor):
    dma = pltpu.SemaphoreType.DMA
    f32, bf16 = jnp.float32, jnp.bfloat16
    smem = pl.BlockSpec(memory_space=pltpu.SMEM)
    vmem, hbm = pl.BlockSpec(memory_space=pltpu.VMEM), pl.BlockSpec(memory_space=pl.ANY)
    block = (ROWS, DEPTH, WIDE)
    packed = len(tri_blocks(NORB)) * B
    share = packed // NEAR
    return pl.pallas_call(
        functools.partial(whole_kernel, factor),
        out_shape=[jax.ShapeDtypeStruct((NORB, NORB), f32), jax.ShapeDtypeStruct((4,) + block, f32)],
        in_specs=[hbm, vmem, vmem, vmem, smem, smem],
        out_specs=[vmem, hbm],
        scratch_shapes=[
            pltpu.VMEM((12,) + block, f32),
            pltpu.VMEM((12,) + block, f32),
            pltpu.VMEM((4,) + block, f32),
            pltpu.VMEM((4,) + block, f32),
            pltpu.VMEM((STRIP, DEPTH, WIDE), f32),
            pltpu.VMEM((4, STRIPS, 256, AREA), bf16),
            pltpu.VMEM((4, CELLS, 512), bf16),
            pltpu.VMEM((3, PROJ, SPAN * CELLS), f32),
            pltpu.VMEM((3, PROJ, 128), f32),
            pltpu.VMEM((PROJ, MAXPROJ), f32),
            pltpu.VMEM((8, ROWS, DEPTH), f32),
            pltpu.VMEM((256, 2 * WIDE), f32),
            pltpu.VMEM((2, 3, PROJ, WIDE), f32),
            pltpu.VMEM((2, 2, PROJ, WIDE), f32),
            pltpu.VMEM((512, WIDE), bf16),
            pltpu.VMEM((2,) + block, f32),
            pltpu.VMEM((2,) + block, f32),
            pltpu.VMEM((2,) + block, f32),
            pltpu.VMEM((2, 2) + block, f32),
            pltpu.VMEM((2, 2) + block, f32),
            pltpu.VMEM((GROUP, ROWS // 2, DEPTH, WIDE), f32),
            dma((4,)), dma((PIECES,)), dma((PIECES,)), dma((PIECES,)), dma((PIECES,)), dma((2, PIECES)),
            dma((3,)), dma((3,)), dma(()), dma(()), dma((2,)), dma((2,)), dma(()), dma(()),
            dma((2, 2)), dma((2, 2)), dma((2, PIECES)), dma((2, PIECES)),
            dma((GROUP, 2)), dma((GROUP, 2)), dma((2,)),
            pltpu.VMEM((CELLS, NORB), bf16),
            pltpu.VMEM((CELLS, NORB), bf16),
            pltpu.VMEM((packed, B), f32),
            pltpu.VMEM((NEAR, share, B), f32),
            pltpu.VMEM((share, B), f32),
            pltpu.VMEM((FAR, share // SUMMERS, B), f32),
            pltpu.VMEM((packed, B), f32),
            pltpu.VMEM((NORB, NORB), f32),
            dma((NEAR,)), dma((NEAR,)), dma((FAR,)), dma((FAR,)),
            dma((FAR,)), dma((FAR,)), dma((NEAR,)), dma((NEAR,)),
            dma(()), dma((4, 2)), dma((NEAR,)),
        ],
        compiler_params=pltpu.CompilerParams(collective_id=2, has_side_effects=True, vmem_limit_bytes=62 * 2**20),
    )(orbitals, potential, projectors, coupling, atom_plane, projector_count)


def settle_kernel(gram, filtered, gram_out, filtered_out, sems):
    copies = [pltpu.make_async_copy(filtered.at[p], filtered_out.at[p], sems.at[p]) for p in range(4)]
    copies.append(pltpu.make_async_copy(gram, gram_out, sems.at[4]))
    for copy in copies:
        copy.start()
    for copy in copies:
        copy.wait()


def settle(gram, filtered):
    hbm = pl.BlockSpec(memory_space=pl.ANY)
    return pl.pallas_call(
        settle_kernel,
        out_shape=[jax.ShapeDtypeStruct(x.shape, x.dtype) for x in (gram, filtered)],
        in_specs=[hbm, hbm],
        out_specs=[hbm, hbm],
        scratch_shapes=[pltpu.SemaphoreType.DMA((5,))],
        compiler_params=pltpu.CompilerParams(vmem_limit_bytes=8 * 2**20),
    )(gram, filtered)


def shards(orbitals, potential, projectors, coupling, atom_plane, projector_count):
    planes, side_y, side_z, _ = orbitals.shape
    total_cells = planes * side_y * side_z * lax.axis_size("dom")
    gram, filtered = run(
        orbitals, potential, projectors, coupling, atom_plane, projector_count, 1.0 / total_cells)
    gram, filtered = settle(gram, filtered)
    return (filtered, gram)


def solution(mesh):
    placed = (
        P("dom", None, None, "band"),
        P("dom", None, None),
        P("dom", None, None),
        P("dom", None, None),
        P("dom"),
        P("dom"),
    )
    return jax.shard_map(
        shards,
        mesh=mesh,
        in_specs=placed,
        out_specs=(P("dom", None, None, "band"), P()),
        check_vma=False,
    )
```

```python
import functools

import jax
import jax.numpy as jnp
from jax import lax
from jax.experimental import pallas as pl
from jax.experimental.pallas import tpu as pltpu
from jax.sharding import PartitionSpec as P

NORB = 512
HALO = 4
SPAN = 3
MAXPROJ = 4
B = 128

center_weight = -205.0 / 72.0
side_weights = (8.0 / 5.0, -1.0 / 5.0, 8.0 / 315.0, -1.0 / 560.0)
HIGH = lax.Precision.HIGHEST


HIGHEST = lax.Precision.HIGHEST


def dot_f32(a, b, dims):
    return lax.dot_general(a, b, (dims, ((), ())), precision=HIGHEST, preferred_element_type=jnp.float32)


def block_inverse(tiles):
    count = len(tiles)
    tiles = list(tiles)
    shape = tiles[0].shape
    lane = lax.broadcasted_iota(jnp.int32, shape, 1)
    sub = lax.broadcasted_iota(jnp.int32, shape, 0)
    done = []
    for j in range(count):
        base = 8 * j
        cols = [
            [jnp.broadcast_to(tiles[t][:, base + k : base + k + 1], shape) for k in range(8)]
            for t in range(j, count)
        ]
        inside = (lane >= base) & (lane < base + 8)
        unit = jnp.where(lane == sub + base, 1.0, 0.0)
        own = jnp.where(inside, unit, tiles[j])
        rows = [jnp.broadcast_to(own[k : k + 1, :], shape) for k in range(8)]
        splat = [
            [jnp.broadcast_to(cols[0][k][i : i + 1, :], shape) if i >= k else None for k in range(8)]
            for i in range(8)
        ]
        rest = [jnp.where(inside, 0.0, tiles[t]) for t in range(j + 1, count)]
        result = jnp.zeros(shape, jnp.float32)
        for k in range(8):
            scale = lax.rsqrt(splat[k][k])
            rows[k] = rows[k] * scale
            for i in range(k + 1, 8):
                splat[i][k] = splat[i][k] * scale
            for i in range(k + 1, 8):
                for m in range(k + 1, i + 1):
                    splat[i][m] = splat[i][m] - splat[i][k] * splat[m][k]
                rows[i] = rows[i] - splat[i][k] * rows[k]
            for t in range(len(rest)):
                below = cols[t + 1]
                below[k] = below[k] * scale
                for m in range(k + 1, 8):
                    below[m] = below[m] - below[k] * splat[m][k]
                rest[t] = rest[t] - below[k] * rows[k]
            result = jnp.where(sub == k, rows[k], result)
        done.append(jnp.where(lane <= sub + base, result, 0.0))
        tiles[j + 1 :] = rest
    return done


def factor_steps(work, begin, complete, done):
    size = work.shape[0]

    def step(k, carry):
        at = pl.ds(pl.multiple_of(k * B, B), B)
        pl.when(k == 0)(begin)
        tiles = [work[pl.ds(pl.multiple_of(k * B + 8 * t, 8), 8), at] for t in range(B // 8)]
        corner = jnp.concatenate(block_inverse(tiles), axis=0)
        pl.when(k == 0)(complete)
        row_id = lax.broadcasted_iota(jnp.int32, (size, B), 0)
        column = jnp.where(row_id >= (k + 1) * B, work[:, at], 0.0)
        unit = lax.broadcasted_iota(jnp.int32, (B, B), 0) == lax.broadcasted_iota(jnp.int32, (B, B), 1)
        work[at, at] = jnp.where(unit, 1.0, 0.0)
        scaled = dot_f32(corner, work[at, :], ((1,), (0,)))
        row_at = lax.broadcasted_iota(jnp.int32, (B, size), 0) + k * B
        done(k, jnp.where(lax.broadcasted_iota(jnp.int32, (B, size), 1) <= row_at, scaled, 0.0))
        below = dot_f32(column, corner, ((1,), (1,)))
        block = work[:, at]
        work[:, at] = jnp.where(row_id >= (k + 1) * B, 0.0, block)
        work[...] = work[...] - dot_f32(below, scaled, ((1,), (0,)))
        return carry

    lax.fori_loop(0, size // B, step, 0)


MESH = pl.DeviceIdType.MESH
NEAR = 8
FAR = 16
SUMMERS = 10


def tri_blocks(size):
    return [(i, j) for i in range(size // B) for j in range(i + 1)]


def finish_part(
    factor, gram_ref, filtered_ref,
    high, low, pack, near, mine, far, total, work, parts, near_s, near_r, far_s, far_r, out_s, out_r, end_s, end_r,
    local_s, home_s, home_r,
):
    band, dom = lax.axis_index("band"), lax.axis_index("dom")
    pair, half = dom // 2, dom % 2
    rank = half * 4 + band
    blocks = tri_blocks(work.shape[0])
    share = len(blocks) * B // NEAR
    piece = share // SUMMERS

    def near_peer(step):
        other = (rank + step) % NEAR
        return other, (other % 4, pair * 2 + other // 4)

    def far_peer(step):
        other = (pair + step) % FAR
        return other, (band, other * 2 + half)

    def rows(index, count):
        return pl.ds(pl.multiple_of(index * count, 8), count)

    def near_copy(step):
        other, device = near_peer(step)
        return pltpu.make_async_remote_copy(
            src_ref=pack.at[rows(other, share)], dst_ref=near.at[rank],
            send_sem=near_s.at[step], recv_sem=near_r.at[rank], device_id=device, device_id_type=MESH)

    def near_arrival(step):
        other, device = near_peer(step)
        return pltpu.make_async_remote_copy(
            src_ref=pack.at[rows(other, share)], dst_ref=near.at[other],
            send_sem=near_s.at[step], recv_sem=near_r.at[other], device_id=device, device_id_type=MESH)

    for step in range(1, NEAR):
        near_copy(step).start()
    near[rank] = pack[rows(rank, share), :]
    for step in range(1, NEAR):
        near_arrival(step).wait_recv()
    acc = near[0]
    for n in range(1, NEAR):
        acc = acc + near[n]
    mine[...] = acc

    def far_copy(step, slot):
        other, device = far_peer(step)
        return other, pltpu.make_async_remote_copy(
            src_ref=mine.at[rows(other % SUMMERS, piece)], dst_ref=far.at[pair if slot is None else other],
            send_sem=far_s.at[step], recv_sem=far_r.at[pair if slot is None else other],
            device_id=device, device_id_type=MESH)

    for step in range(1, FAR):
        other, copy = far_copy(step, None)
        pl.when(other < SUMMERS)(copy.start)

    place = rank * share

    def out_rows(index):
        return pl.ds(pl.multiple_of(place + (index % SUMMERS) * piece, 8), piece)

    def out_copy(step):
        other, device = far_peer(step)
        return pltpu.make_async_remote_copy(
            src_ref=total.at[out_rows(pair)], dst_ref=total.at[out_rows(pair)],
            send_sem=out_s.at[step], recv_sem=out_r.at[pair], device_id=device, device_id_type=MESH)

    def out_arrival(step):
        other, device = far_peer(step)
        return other, pltpu.make_async_remote_copy(
            src_ref=total.at[out_rows(other)], dst_ref=total.at[out_rows(other)],
            send_sem=out_s.at[step], recv_sem=out_r.at[other], device_id=device, device_id_type=MESH)

    @pl.when(pair < SUMMERS)
    def _():
        far[pair] = mine[rows(pair % SUMMERS, piece), :]
        for step in range(1, FAR):
            far_copy(step, 1)[1].wait_recv()
        acc = far[0]
        for n in range(1, FAR):
            acc = acc + far[n]
        total[out_rows(pair), :] = acc * factor
        for step in range(1, FAR):
            out_copy(step).start()

    for step in range(1, FAR):
        other, copy = out_arrival(step)
        pl.when(other < SUMMERS)(copy.wait_recv)

    def end_copy(step, slot):
        other, device = near_peer(step)
        at = rows(rank if slot is None else other, share)
        return pltpu.make_async_remote_copy(
            src_ref=total.at[at], dst_ref=total.at[at],
            send_sem=end_s.at[step], recv_sem=end_r.at[rank if slot is None else other],
            device_id=device, device_id_type=MESH)

    for step in range(1, NEAR):
        end_copy(step, None).start()

    def share_in(index):
        at = rows(index, share)
        return pltpu.make_async_remote_copy(
            src_ref=total.at[at], dst_ref=total.at[at], send_sem=end_s.at[1], recv_sem=end_r.at[index],
            device_id=near_peer(1)[1], device_id_type=MESH)

    def begin():
        pl.when(rank != 0)(share_in(0).wait_recv)
        work[:B, :B] = total[:B, :]

    def complete():
        for index in range(1, NEAR):
            pl.when(rank != index)(share_in(index).wait_recv)
        for n, (i, j) in enumerate(blocks):
            block = total[n * B : (n + 1) * B, :]
            gram_ref[i * B : (i + 1) * B, j * B : (j + 1) * B] = block
            if i != j:
                gram_ref[j * B : (j + 1) * B, i * B : (i + 1) * B] = block.T
        work[...] = gram_ref[...]

    def target(index):
        return filtered_ref.at[index // 2, pl.ds(pl.multiple_of(lax.rem(index, 2) * 16, 8), ROWS // 2)]

    def move(k, to_half):
        return pltpu.make_async_remote_copy(
            src_ref=parts.at[k, rows(to_half, ROWS // 2)], dst_ref=target(rank), send_sem=home_s.at[k, to_half],
            recv_sem=home_r.at[rank], device_id=(k, pair * 2 + to_half), device_id_type=MESH)

    local = pltpu.make_async_copy(parts.at[band, rows(half, ROWS // 2)], target(rank), local_s)
    across = (((1,), (1,)), ((), ()))
    cells = high.shape[0] // 2

    def rotate(k, inverse_rows):
        high_rot, low_rot = split(inverse_rows)
        both = jnp.concatenate([high_rot, low_rot], axis=0)
        for to_half in range(2):
            at = slice(to_half * cells, (to_half + 1) * cells)
            wide = lax.dot_general(high[at, :], both, across, preferred_element_type=jnp.float32)
            more = lax.dot_general(low[at, :], high_rot, across, preferred_element_type=jnp.float32)
            value = wide[:, :B] + (wide[:, B:] + more)
            parts[k, rows(to_half, ROWS // 2)] = value.reshape(ROWS // 2, DEPTH, B)
            here = (k == band) & (to_half == half)
            pl.when(jnp.logical_not(here))(lambda to_half=to_half: move(k, to_half).start())
            pl.when(here)(local.start)

    factor_steps(work, begin, complete, rotate)
    for step in range(1, NEAR):
        other, device = near_peer(step)
        pltpu.make_async_remote_copy(
            src_ref=parts.at[0, rows(0, ROWS // 2)], dst_ref=target(other), send_sem=home_s.at[0, 0], recv_sem=home_r.at[other],
            device_id=device, device_id_type=MESH).wait_recv()
    local.wait()
    for k in range(4):
        for to_half in range(2):
            here = (k == band) & (to_half == half)
            pl.when(jnp.logical_not(here))(lambda k=k, to_half=to_half: move(k, to_half).wait_send())

    for step in range(1, NEAR):
        near_copy(step).wait_send()
        end_copy(step, None).wait_send()
    for step in range(1, FAR):
        other, copy = far_copy(step, None)
        pl.when(other < SUMMERS)(copy.wait_send)

    @pl.when(pair < SUMMERS)
    def _():
        for step in range(1, FAR):
            out_copy(step).wait_send()


ROWS = 32
DEPTH = 48
WIDE = 128
CELLS = ROWS * DEPTH
PROJ = 32
REACH = 6
FLAGS = PROJ
GROUP = 8
STRIP = 8
STRIPS = ROWS // STRIP
PIECE = 4
PIECES = ROWS // PIECE
WINDOW = 3
AREA = STRIP * DEPTH


def split(value):
    high = value.astype(jnp.bfloat16)
    return high, (value - high.astype(jnp.float32)).astype(jnp.bfloat16)


def swap(value):
    return pltpu.roll(value, WIDE // 2, value.ndim - 1)


def whole_kernel(
    factor, orb, pot, proj, coupling, planes, counts, gram_ref, filtered_ref,
    e1, e2, second, shift_pot, nonlocal_plane, left, right, raw, notes, scratch_notes, pot_all, corr_sum, corr, corr_in, weights,
    give_cross, give_keep, got_cross, got1, got2, slab,
    local_s, x_s, x_r, own_s, fwd_s, halo_r, small_s, small_r, core_s, core_r, next_s, next_r, last_s, last_r,
    corr_s, corr_r, y2_s, y2_r, out_s, out_r, self_s,
    high_cells, low_cells, pack, *rest,
):
    band, dom = lax.axis_index("band"), lax.axis_index("dom")
    pair, half = dom // 2, dom % 2
    other = 1 - half
    core = lax.rem(band, 2)
    rank = half * 4 + band
    pairs = lax.axis_size("dom") // 2
    partner = (band, pair * 2 + other)
    sibling = (band + 1 - 2 * core, dom)

    def at_pair(step):
        return (band, lax.rem(pair + step + pairs, pairs) * 2 + half)

    def send(src, dst, ssem, rsem, device):
        return pltpu.make_async_remote_copy(
            src_ref=src, dst_ref=dst, send_sem=ssem, recv_sem=rsem, device_id=device, device_id_type=MESH)

    def member(index):
        return (lax.rem(index, 4), pair * 2 + index // 4)

    barrier = pltpu.get_barrier_semaphore()
    for n in range(1, GROUP):
        pl.semaphore_signal(barrier, inc=1, device_id=member(lax.rem(rank + n, GROUP)), device_id_type=MESH)
    for n in range(1, FAR):
        pl.semaphore_signal(barrier, inc=1, device_id=at_pair(n), device_id_type=MESH)

    loads = [pltpu.make_async_copy(orb.at[p], second.at[p], local_s.at[p]) for p in range(4)]
    for copy in loads:
        copy.start()
    lane = lax.broadcasted_iota(jnp.int32, (DEPTH, WIDE), 1)
    lower = lane < WIDE // 2
    kept = (lane // (WIDE // 2)) == half

    share = pl.ds(pl.multiple_of(core * (PROJ // 2), 16), PROJ // 2)
    twin = pl.ds(pl.multiple_of((1 - core) * (PROJ // 2), 16), PROJ // 2)
    small = [
        send(pot, pot_all.at[pl.ds(4 * half, 4)], small_s.at[0], small_r.at[0], partner),
        send(notes.at[1 + half], notes.at[1 + half], small_s.at[1], small_r.at[1], partner),
        send(raw.at[1 + half, share], raw.at[1 + half, share], small_s.at[2], small_r.at[2], partner),
    ]
    small_in = [
        send(pot, pot_all.at[pl.ds(4 * other, 4)], small_s.at[0], small_r.at[0], partner),
        send(notes.at[1 + other], notes.at[1 + other], small_s.at[1], small_r.at[1], partner),
        send(raw.at[1 + other, share], raw.at[1 + other, share], small_s.at[2], small_r.at[2], partner),
    ]
    across = send(raw.at[1 + other, share], raw.at[1 + other, share], core_s, core_r, sibling)
    across_in = send(raw.at[1 + other, twin], raw.at[1 + other, twin], core_s, core_r, sibling)
    onward = [
        send(notes.at[2], notes.at[0], next_s.at[0], next_r.at[0], at_pair(1)),
        send(raw.at[2, share], raw.at[0, share], next_s.at[1], next_r.at[1], at_pair(1)),
    ]
    last = send(raw.at[0, share], raw.at[0, share], last_s, last_r, sibling)
    last_in = send(raw.at[0, twin], raw.at[0, twin], last_s, last_r, sibling)

    def piece_rows(c):
        return pl.ds(c * PIECE, PIECE)

    def cross(c):
        at = (slice(None), piece_rows(c))
        return send(give_cross.at[at], got_cross.at[at], x_s.at[c], x_r.at[c], partner)

    def keep(c):
        at = piece_rows(c)
        return send(give_keep.at[:, at], got1.at[other, :, at], own_s.at[c], halo_r.at[other, c],
                    at_pair(2 * half - 1))

    def forward(c):
        at = piece_rows(c)
        return send(got_cross.at[:, at], got1.at[half, :, at], fwd_s.at[c], halo_r.at[half, c],
                    at_pair(1 - 2 * half))

    def halo_in(side, c):
        at = piece_rows(c)
        return send(give_keep.at[:, at], got1.at[side, :, at], own_s.at[c], halo_r.at[side, c], at_pair(1))

    line = lax.broadcasted_iota(jnp.int32, (PROJ, WIDE), 0)
    column = lax.broadcasted_iota(jnp.int32, (PROJ, WIDE), 1)
    start, live = jnp.zeros_like(line), jnp.zeros_like(line)
    for a in range(PROJ // MAXPROJ):
        at_atom = (line >> 2) == a
        start = jnp.where(at_atom, planes[a] - dom * 4, start)
        live = jnp.where(at_atom, counts[a], live)
        scratch_notes[a * MAXPROJ : (a + 1) * MAXPROJ, 0:MAXPROJ] = coupling[a]
    same = (line >> 2) == (column >> 2)
    spread_out = jnp.zeros((PROJ, WIDE), jnp.float32)
    for j in range(MAXPROJ):
        value = jnp.broadcast_to(scratch_notes[:, j : j + 1], (PROJ, WIDE))
        spread_out = jnp.where(same & ((column & 3) == j), value, spread_out)
    square = jnp.concatenate([spread_out, jnp.zeros((WIDE - PROJ, WIDE), jnp.float32)], axis=0)
    symmetric = 0.5 * (spread_out + square.T[:PROJ])
    symmetric = jnp.where(((line & 3) < live) & ((column & 3) < live), symmetric, 0.0)
    wanted = jnp.full((PROJ, WIDE), -WIDE, jnp.int32)
    for reach in range(REACH):
        for k in range(SPAN):
            wanted = jnp.where(column == FLAGS + reach * SPAN + k, reach - k, wanted)
    flag_rows = jnp.where(wanted == start, 1.0, 0.0)
    notes[1 + half] = jnp.where(column < FLAGS, symmetric, flag_rows)
    for a in range(PROJ // MAXPROJ):
        raw[1 + half, a * MAXPROJ : (a + 1) * MAXPROJ, :] = proj[a]
    pot_all[pl.ds(4 * half, 4)] = pot[...]
    for copy in loads:
        copy.wait()

    def pack_piece(c, carry):
        for n in range(PIECE):
            r = c * PIECE + n
            for j in range(2):
                near, far = second[j, r], second[j + 2, r]
                give_cross[j, r] = jnp.where(kept, swap(near), far)
                give_keep[j, r] = jnp.where(kept, near, swap(far))
        return carry

    def start_piece(c):
        cross(c).start()
        keep(c).start()

    lax.fori_loop(0, WINDOW, pack_piece, 0)
    pl.semaphore_wait(barrier, GROUP + FAR - 2)
    for copy in small:
        copy.start()
    for c in range(WINDOW):
        start_piece(c)
    lax.fori_loop(WINDOW, PIECES, pack_piece, 0)

    for copy in small_in:
        copy.wait_recv()
    across.start()
    for copy in onward[:1]:
        copy.start()

    def placed(group, reach):
        total = jnp.zeros((PROJ, CELLS), jnp.float32)
        for k in range(SPAN):
            flag = notes[group, :, FLAGS + reach * SPAN + k : FLAGS + reach * SPAN + k + 1]
            total = total + flag * raw[group, :, k * CELLS : (k + 1) * CELLS]
        return total

    def store_pair(p, groups, reach, slot):
        beta = jnp.concatenate([placed(group, reach) for group in groups], axis=0)
        high_part, low_part = split(beta)
        both = jnp.concatenate([high_part, low_part], axis=0)
        for n in range(STRIPS):
            left[p, n, slot * 128 : (slot + 1) * 128, :] = both[:, n * AREA : (n + 1) * AREA]
        high32 = high_part.astype(jnp.float32)
        wide = jnp.concatenate([high32, low_part.astype(jnp.float32)], axis=0)
        turned = wide.T.astype(jnp.bfloat16)
        right[p, :, slot * 256 : slot * 256 + 128] = turned
        right[p, :, slot * 256 + 128 : slot * 256 + 192] = turned[:, :64]
        right[p, :, slot * 256 + 192 : slot * 256 + 256] = jnp.zeros((CELLS, 64), jnp.bfloat16)

    diagonal = lax.broadcasted_iota(jnp.int32, (DEPTH, DEPTH), 0) == lax.broadcasted_iota(
        jnp.int32, (DEPTH, DEPTH), 1)
    constant = -1.5 * center_weight - 7.0

    def spread(n, carry):
        p, r = n // ROWS, lax.rem(n, ROWS)
        columns = []
        for extra in (0, 4):
            line = jnp.broadcast_to(pot_all[p + extra, pl.ds(r, 1), :], (DEPTH, DEPTH))
            columns.append(jnp.sum(jnp.where(diagonal, line, 0.0), axis=1, keepdims=True))
        shift_pot[p, r] = jnp.where(lower, columns[0], columns[1]) + constant
        return carry

    def receive_piece(c):
        cross(c).wait_recv()
        forward(c).start()
        cross(c).wait_send()
        keep(c).wait_send()
        if c + WINDOW < PIECES:
            start_piece(c + WINDOW)

        def one(n, carry):
            r = c * PIECE + n
            for j in range(2):
                arrived = got_cross[j, r]
                e1[4 + j, r] = jnp.where(kept, second[j, r], arrived)
                e1[6 + j, r] = jnp.where(kept, second[j + 2, r], swap(arrived))
            return carry

        lax.fori_loop(0, PIECE, one, 0)

    for p in (2, 3):
        left[p, :, 128:256, :] = jnp.zeros((STRIPS, 128, AREA), jnp.bfloat16)
        right[p, :, 256:512] = jnp.zeros((CELLS, 256), jnp.bfloat16)
    def spread_rows(n):
        lax.fori_loop(n * 4 * ROWS // PIECES, (n + 1) * 4 * ROWS // PIECES, spread, 0)

    def add_strip(field, strip):
        def part(p, total):
            cells = field[4 + p, pl.ds(strip * STRIP, STRIP)].reshape(AREA, WIDE)
            both = jnp.concatenate(split(cells), axis=1)
            return total + lax.dot_general(
                left[p, strip], both, (((1,), (0,)), ((), ())), preferred_element_type=jnp.float32)

        corr_sum[...] = lax.fori_loop(0, 4, part, corr_sum[...])

    def share_sums(phase):
        total = corr_sum[:, :WIDE] + corr_sum[:, WIDE:]
        corr_sum[...] = jnp.zeros_like(corr_sum)
        near, tail = total[0:64] + total[64:128], total[128:192] + total[192:256]
        corr[phase, 0] = tail[:PROJ]
        corr[phase, 1] = near[PROJ:]
        corr[phase, 2] = near[:PROJ] + swap(tail[PROJ:])
        down = send(corr.at[phase, 0], corr_in.at[phase, 1], corr_s.at[phase, 0], corr_r.at[phase, 1], at_pair(-1))
        up = send(corr.at[phase, 1], corr_in.at[phase, 0], corr_s.at[phase, 1], corr_r.at[phase, 0], at_pair(1))
        down.start()
        up.start()
        return [down, up]

    def weigh(phase, copies):
        for copy in copies:
            copy.wait_recv()
        before = corr[phase, 0] + swap(corr_in[phase, 0])
        after = corr[phase, 1] + swap(corr_in[phase, 1])
        before, own, after = (
            dot_f32(notes[group, :, :PROJ], value, ((1,), (0,)))
            for group, value in ((0, before), (1, corr[phase, 2]), (2, after))
        )
        in_low = lax.broadcasted_iota(jnp.int32, (PROJ, WIDE), 1) < WIDE // 2
        zero = jnp.zeros((64, WIDE), jnp.bfloat16)
        parts = []
        for low_value, high_value in ((own, after), (before, swap(own))):
            value = jnp.concatenate(
                [jnp.where(in_low, low_value, 0.0), jnp.where(in_low, 0.0, high_value)], axis=0)
            high_part, low_part = split(value)
            parts += [high_part, high_part, low_part, zero]
        weights[...] = jnp.concatenate(parts, axis=0)

    def open_rows(field, got, base, count):
        def one(n, carry):
            r = base + n
            for j in range(2):
                near, far = field[4 + j, r], field[6 + j, r]
                up, down = got[0, j, r], got[1, j, r]
                field[j, r] = swap(jnp.where(lower, near, up))
                field[2 + j, r] = jnp.where(lower, up, swap(far))
                field[8 + j, r] = swap(jnp.where(lower, down, near))
                field[10 + j, r] = jnp.where(lower, swap(far), down)
            return carry

        lax.fori_loop(0, count, one, 0)

    def apply(field, base, count, scale, write):
        def plane(p, carry):
            product = lax.dot_general(
                right[p, base * DEPTH : (base + count) * DEPTH, :], weights[...],
                (((1,), (0,)), ((), ())), preferred_element_type=jnp.float32)
            nonlocal_plane[:count] = product.reshape(count, DEPTH, WIDE)

            def row(n, inner):
                r = base + n
                centre = field[p + 4, r]
                total = centre * shift_pot[p, r] + nonlocal_plane[n]
                for k in range(1, 5):
                    pair_x = field[p + 4 + k, r] + field[p + 4 - k, r]
                    pair_y = field[p + 4, lax.rem(r + k, ROWS)] + field[p + 4, lax.rem(r + ROWS - k, ROWS)]
                    pair_z = pltpu.roll(centre, k, 0) + pltpu.roll(centre, DEPTH - k, 0)
                    total = total + (-0.5 * side_weights[k - 1]) * ((pair_x + pair_y) + pair_z)
                write(p, r, total * scale)
                return inner

            lax.fori_loop(0, count, row, 0)
            return carry

        lax.fori_loop(0, 4, plane, 0)

    def open_first(strip):
        for side in range(2):
            for n in range(STRIP // PIECE):
                halo_in(side, strip * (STRIP // PIECE) + n).wait_recv()
        open_rows(e1, got1, strip * STRIP, STRIP)

    spread_rows(0)
    across_in.wait_recv()
    onward[1].start()
    receive_piece(0)
    store_pair(0, (1, 2), 0, 0)
    store_pair(1, (1, 2), 1, 0)
    spread_rows(1)
    receive_piece(1)
    store_pair(2, (1, 2), 2, 0)
    store_pair(3, (1, 2), 3, 0)
    spread_rows(2)
    receive_piece(2)
    for copy in onward:
        copy.wait_recv()
    last.start()
    spread_rows(3)
    spread_rows(4)
    receive_piece(3)
    last_in.wait_recv()
    store_pair(0, (0, 1), 4, 1)
    store_pair(1, (0, 1), 5, 1)
    corr_sum[...] = jnp.zeros_like(corr_sum)
    add_strip(e1, 0)
    receive_piece(4)
    spread_rows(5)
    add_strip(e1, 1)
    receive_piece(5)
    spread_rows(6)
    open_first(0)
    receive_piece(6)
    spread_rows(7)
    add_strip(e1, 2)
    receive_piece(7)
    add_strip(e1, 3)
    copies1 = share_sums(0)
    for strip in range(1, STRIPS):
        open_first(strip)
    for c in range(PIECES):
        forward(c).wait_send()
    weigh(0, copies1)

    def write_first(p, r, value):
        e2[p + 4, r] = value

    def up2(c):
        at = piece_rows(c)
        return send(give_cross.at[:, at], got2.at[0, :, at], y2_s.at[0, c], y2_r.at[0, c], at_pair(1))

    def down2(c):
        at = piece_rows(c)
        return send(give_keep.at[:, at], got2.at[1, :, at], y2_s.at[1, c], y2_r.at[1, c], at_pair(-1))

    def first_strip(strip):
        apply(e1, strip * STRIP, STRIP, 1.0 / 6.0, write_first)

        def pack(n, inner):
            r = strip * STRIP + n
            for j in range(2):
                near, turned = e2[4 + j, r], swap(e2[6 + j, r])
                give_cross[j, r] = jnp.where(lower, turned, near)
                give_keep[j, r] = jnp.where(lower, near, turned)
            return inner

        lax.fori_loop(0, STRIP, pack, 0)
        for c in range(2 * strip, 2 * strip + 2):
            if c < WINDOW:
                up2(c).start()
                down2(c).start()
        add_strip(e2, strip)

    for strip in range(STRIPS):
        first_strip(strip)
    copies2 = share_sums(1)
    weigh(1, copies2)

    def write_second(p, r, value):
        second[p, r] = value - e1[p + 4, r]

    def give(index, part):
        src = second.at[index // 2, pl.ds(lax.rem(index, 2) * 16 + part * PIECE, PIECE)]
        return send(src, slab.at[rank, pl.ds(part * PIECE, PIECE)], out_s.at[index, part], out_r.at[rank, part],
                    member(index))

    def own_part(part):
        src = second.at[rank // 2, pl.ds(lax.rem(rank, 2) * 16 + part * PIECE, PIECE)]
        return pltpu.make_async_copy(src, slab.at[rank, pl.ds(part * PIECE, PIECE)], self_s.at[part])

    def second_piece(c):
        for copy in (up2(c), down2(c)):
            copy.wait_recv()
            copy.wait_send()
        if c + WINDOW < PIECES:
            up2(c + WINDOW).start()
            down2(c + WINDOW).start()
        open_rows(e2, got2, c * PIECE, PIECE)
        apply(e2, c * PIECE, PIECE, 1.0 / 3.0, write_second)
        row_half, part = c // 4, c % 4
        for n in range(4):
            index = 2 * lax.rem(n + rank // 2 + 2, 4) + row_half
            pl.when(index != rank)(lambda index=index: give(index, part).start())
        pl.when(lax.rem(rank, 2) == row_half)(own_part(part).start)

    for c in range(PIECES):
        second_piece(c)

    blocks = tri_blocks(NORB)
    pack[...] = jnp.zeros_like(pack)

    def repack(n, carry):
        cells = pl.ds(pl.multiple_of(n * DEPTH, 16), DEPTH)
        more = pl.ds(pl.multiple_of(CELLS // 2 + n * DEPTH, 16), DEPTH)
        for b in range(4):
            at = slice(b * WIDE, (b + 1) * WIDE)
            here, there = slab[b, n], slab[4 + b, n]
            high_cells[cells, at], low_cells[cells, at] = split(jnp.where(lower, here, swap(there)))
            high_cells[more, at], low_cells[more, at] = split(jnp.where(lower, swap(here), there))
        return carry

    def add_gram(part):
        contract = (((0,), (0,)), ((), ()))

        def chunk(side, carry):
            cells = pl.ds(pl.multiple_of(side * (CELLS // 2) + part * AREA, 16), AREA)
            for i in range(NORB // B):
                own, wide = slice(i * B, (i + 1) * B), slice(0, (i + 1) * B)
                row = lax.dot_general(
                    high_cells[cells, own], high_cells[cells, wide], contract, preferred_element_type=jnp.float32)
                row += lax.dot_general(
                    high_cells[cells, own], low_cells[cells, wide], contract, preferred_element_type=jnp.float32)
                row += lax.dot_general(
                    low_cells[cells, own], high_cells[cells, wide], contract, preferred_element_type=jnp.float32)
                for j in range(i + 1):
                    n = blocks.index((i, j))
                    pack[n * B : (n + 1) * B, :] += row[:, j * B : (j + 1) * B]
            return carry

        lax.fori_loop(0, 2, chunk, 0)

    for section in range(2):
        for part in (2 * section, 2 * section + 1):
            for n in range(1, GROUP):
                index = lax.rem(rank + n, GROUP)
                send(second.at[0, pl.ds(0, PIECE)], slab.at[index, pl.ds(part * PIECE, PIECE)],
                     out_s.at[index, part], out_r.at[index, part], member(index)).wait_recv()
            own_part(part).wait()
            lax.fori_loop(part * PIECE, (part + 1) * PIECE, repack, 0)
        add_gram(section)

    for copy in small + [across, last] + onward + copies1 + copies2:
        copy.wait_send()
    for n in range(1, GROUP):
        for part in range(4):
            give(lax.rem(rank + n, GROUP), part).wait_send()
    finish_part(factor, gram_ref, filtered_ref, high_cells, low_cells, pack, *rest[:5], second, *rest[5:])


def run(orbitals, potential, projectors, coupling, atom_plane, projector_count, factor):
    dma = pltpu.SemaphoreType.DMA
    f32, bf16 = jnp.float32, jnp.bfloat16
    smem = pl.BlockSpec(memory_space=pltpu.SMEM)
    vmem, hbm = pl.BlockSpec(memory_space=pltpu.VMEM), pl.BlockSpec(memory_space=pl.ANY)
    block = (ROWS, DEPTH, WIDE)
    packed = len(tri_blocks(NORB)) * B
    share = packed // NEAR
    return pl.pallas_call(
        functools.partial(whole_kernel, factor),
        out_shape=[jax.ShapeDtypeStruct((NORB, NORB), f32), jax.ShapeDtypeStruct((4,) + block, f32)],
        in_specs=[hbm, vmem, vmem, vmem, smem, smem],
        out_specs=[vmem, hbm],
        scratch_shapes=[
            pltpu.VMEM((12,) + block, f32),
            pltpu.VMEM((12,) + block, f32),
            pltpu.VMEM((4,) + block, f32),
            pltpu.VMEM((4,) + block, f32),
            pltpu.VMEM((STRIP, DEPTH, WIDE), f32),
            pltpu.VMEM((4, STRIPS, 256, AREA), bf16),
            pltpu.VMEM((4, CELLS, 512), bf16),
            pltpu.VMEM((3, PROJ, SPAN * CELLS), f32),
            pltpu.VMEM((3, PROJ, 128), f32),
            pltpu.VMEM((PROJ, MAXPROJ), f32),
            pltpu.VMEM((8, ROWS, DEPTH), f32),
            pltpu.VMEM((256, 2 * WIDE), f32),
            pltpu.VMEM((2, 3, PROJ, WIDE), f32),
            pltpu.VMEM((2, 2, PROJ, WIDE), f32),
            pltpu.VMEM((512, WIDE), bf16),
            pltpu.VMEM((2,) + block, f32),
            pltpu.VMEM((2,) + block, f32),
            pltpu.VMEM((2,) + block, f32),
            pltpu.VMEM((2, 2) + block, f32),
            pltpu.VMEM((2, 2) + block, f32),
            pltpu.VMEM((GROUP, ROWS // 2, DEPTH, WIDE), f32),
            dma((4,)), dma((PIECES,)), dma((PIECES,)), dma((PIECES,)), dma((PIECES,)), dma((2, PIECES)),
            dma((3,)), dma((3,)), dma(()), dma(()), dma((2,)), dma((2,)), dma(()), dma(()),
            dma((2, 2)), dma((2, 2)), dma((2, PIECES)), dma((2, PIECES)),
            dma((GROUP, 4)), dma((GROUP, 4)), dma((4,)),
            pltpu.VMEM((CELLS, NORB), bf16),
            pltpu.VMEM((CELLS, NORB), bf16),
            pltpu.VMEM((packed, B), f32),
            pltpu.VMEM((NEAR, share, B), f32),
            pltpu.VMEM((share, B), f32),
            pltpu.VMEM((FAR, share // SUMMERS, B), f32),
            pltpu.VMEM((packed, B), f32),
            pltpu.VMEM((NORB, NORB), f32),
            dma((NEAR,)), dma((NEAR,)), dma((FAR,)), dma((FAR,)),
            dma((FAR,)), dma((FAR,)), dma((NEAR,)), dma((NEAR,)),
            dma(()), dma((4, 2)), dma((NEAR,)),
        ],
        compiler_params=pltpu.CompilerParams(collective_id=2, has_side_effects=True, vmem_limit_bytes=62 * 2**20),
    )(orbitals, potential, projectors, coupling, atom_plane, projector_count)


def settle_kernel(gram, filtered, gram_out, filtered_out, sems):
    copies = [pltpu.make_async_copy(filtered.at[p], filtered_out.at[p], sems.at[p]) for p in range(4)]
    copies.append(pltpu.make_async_copy(gram, gram_out, sems.at[4]))
    for copy in copies:
        copy.start()
    for copy in copies:
        copy.wait()


def settle(gram, filtered):
    hbm = pl.BlockSpec(memory_space=pl.ANY)
    return pl.pallas_call(
        settle_kernel,
        out_shape=[jax.ShapeDtypeStruct(x.shape, x.dtype) for x in (gram, filtered)],
        in_specs=[hbm, hbm],
        out_specs=[hbm, hbm],
        scratch_shapes=[pltpu.SemaphoreType.DMA((5,))],
        compiler_params=pltpu.CompilerParams(vmem_limit_bytes=8 * 2**20),
    )(gram, filtered)


def shards(orbitals, potential, projectors, coupling, atom_plane, projector_count):
    planes, side_y, side_z, _ = orbitals.shape
    total_cells = planes * side_y * side_z * lax.axis_size("dom")
    gram, filtered = run(
        orbitals, potential, projectors, coupling, atom_plane, projector_count, 1.0 / total_cells)
    gram, filtered = settle(gram, filtered)
    return (filtered, gram)


def solution(mesh):
    placed = (
        P("dom", None, None, "band"),
        P("dom", None, None),
        P("dom", None, None),
        P("dom", None, None),
        P("dom"),
        P("dom"),
    )
    return jax.shard_map(
        shards,
        mesh=mesh,
        in_specs=placed,
        out_specs=(P("dom", None, None, "band"), P()),
        check_vma=False,
    )
```

```python
import functools

import jax
import jax.numpy as jnp
from jax import lax
from jax.experimental import pallas as pl
from jax.experimental.pallas import tpu as pltpu
from jax.sharding import PartitionSpec as P

NORB = 512
HALO = 4
SPAN = 3
MAXPROJ = 4
B = 128

center_weight = -205.0 / 72.0
side_weights = (8.0 / 5.0, -1.0 / 5.0, 8.0 / 315.0, -1.0 / 560.0)
HIGH = lax.Precision.HIGHEST


HIGHEST = lax.Precision.HIGHEST


def dot_f32(a, b, dims):
    return lax.dot_general(a, b, (dims, ((), ())), precision=HIGHEST, preferred_element_type=jnp.float32)


def block_inverse(tiles):
    count = len(tiles)
    tiles = list(tiles)
    shape = tiles[0].shape
    lane = lax.broadcasted_iota(jnp.int32, shape, 1)
    sub = lax.broadcasted_iota(jnp.int32, shape, 0)
    done = []
    for j in range(count):
        base = 8 * j
        cols = [
            [jnp.broadcast_to(tiles[t][:, base + k : base + k + 1], shape) for k in range(8)]
            for t in range(j, count)
        ]
        inside = (lane >= base) & (lane < base + 8)
        unit = jnp.where(lane == sub + base, 1.0, 0.0)
        own = jnp.where(inside, unit, tiles[j])
        rows = [jnp.broadcast_to(own[k : k + 1, :], shape) for k in range(8)]
        splat = [
            [jnp.broadcast_to(cols[0][k][i : i + 1, :], shape) if i >= k else None for k in range(8)]
            for i in range(8)
        ]
        rest = [jnp.where(inside, 0.0, tiles[t]) for t in range(j + 1, count)]
        result = jnp.zeros(shape, jnp.float32)
        for k in range(8):
            scale = lax.rsqrt(splat[k][k])
            rows[k] = rows[k] * scale
            for i in range(k + 1, 8):
                splat[i][k] = splat[i][k] * scale
            for i in range(k + 1, 8):
                for m in range(k + 1, i + 1):
                    splat[i][m] = splat[i][m] - splat[i][k] * splat[m][k]
                rows[i] = rows[i] - splat[i][k] * rows[k]
            for t in range(len(rest)):
                below = cols[t + 1]
                below[k] = below[k] * scale
                for m in range(k + 1, 8):
                    below[m] = below[m] - below[k] * splat[m][k]
                rest[t] = rest[t] - below[k] * rows[k]
            result = jnp.where(sub == k, rows[k], result)
        done.append(jnp.where(lane <= sub + base, result, 0.0))
        tiles[j + 1 :] = rest
    return done


def factor_steps(work, begin, complete, done):
    size = work.shape[0]

    def step(k, carry):
        at = pl.ds(pl.multiple_of(k * B, B), B)
        pl.when(k == 0)(begin)
        tiles = [work[pl.ds(pl.multiple_of(k * B + 8 * t, 8), 8), at] for t in range(B // 8)]
        corner = jnp.concatenate(block_inverse(tiles), axis=0)
        pl.when(k == 0)(complete)
        row_id = lax.broadcasted_iota(jnp.int32, (size, B), 0)
        column = jnp.where(row_id >= (k + 1) * B, work[:, at], 0.0)
        unit = lax.broadcasted_iota(jnp.int32, (B, B), 0) == lax.broadcasted_iota(jnp.int32, (B, B), 1)
        work[at, at] = jnp.where(unit, 1.0, 0.0)
        scaled = dot_f32(corner, work[at, :], ((1,), (0,)))
        work[at, :] = scaled

        def hand_on(n, inner):
            block = k - n
            rows = work[pl.ds(pl.multiple_of(block * B, B), B), :]
            row_at = lax.broadcasted_iota(jnp.int32, (B, size), 0) + block * B
            done(block, jnp.where(lax.broadcasted_iota(jnp.int32, (B, size), 1) <= row_at, rows, 0.0))
            return inner

        lax.fori_loop(0, jnp.where(k == 1, 0, jnp.where(k == 2, 2, 1)), hand_on, 0)
        below = dot_f32(column, corner, ((1,), (1,)))
        block = work[:, at]
        work[:, at] = jnp.where(row_id >= (k + 1) * B, 0.0, block)
        work[...] = work[...] - dot_f32(below, scaled, ((1,), (0,)))
        return carry

    lax.fori_loop(0, size // B, step, 0)


MESH = pl.DeviceIdType.MESH
NEAR = 8
FAR = 16
SUMMERS = 10


def tri_blocks(size):
    return [(i, j) for i in range(size // B) for j in range(i + 1)]


def finish_part(
    factor, gram_ref, filtered_ref,
    high, low, pack, near, mine, far, total, work, parts, near_s, near_r, far_s, far_r, out_s, out_r, end_s, end_r,
    local_s, home_s, home_r,
):
    band, dom = lax.axis_index("band"), lax.axis_index("dom")
    pair, half = dom // 2, dom % 2
    rank = half * 4 + band
    blocks = tri_blocks(work.shape[0])
    share = len(blocks) * B // NEAR
    piece = share // SUMMERS

    def near_peer(step):
        other = (rank + step) % NEAR
        return other, (other % 4, pair * 2 + other // 4)

    def far_peer(step):
        other = (pair + step) % FAR
        return other, (band, other * 2 + half)

    def rows(index, count):
        return pl.ds(pl.multiple_of(index * count, 8), count)

    def near_copy(step):
        other, device = near_peer(step)
        return pltpu.make_async_remote_copy(
            src_ref=pack.at[rows(other, share)], dst_ref=near.at[rank],
            send_sem=near_s.at[step], recv_sem=near_r.at[rank], device_id=device, device_id_type=MESH)

    def near_arrival(step):
        other, device = near_peer(step)
        return pltpu.make_async_remote_copy(
            src_ref=pack.at[rows(other, share)], dst_ref=near.at[other],
            send_sem=near_s.at[step], recv_sem=near_r.at[other], device_id=device, device_id_type=MESH)

    for step in range(1, NEAR):
        near_copy(step).start()
    near[rank] = pack[rows(rank, share), :]
    for step in range(1, NEAR):
        near_arrival(step).wait_recv()
    acc = near[0]
    for n in range(1, NEAR):
        acc = acc + near[n]
    mine[...] = acc

    def far_copy(step, slot):
        other, device = far_peer(step)
        return other, pltpu.make_async_remote_copy(
            src_ref=mine.at[rows(other % SUMMERS, piece)], dst_ref=far.at[pair if slot is None else other],
            send_sem=far_s.at[step], recv_sem=far_r.at[pair if slot is None else other],
            device_id=device, device_id_type=MESH)

    for step in range(1, FAR):
        other, copy = far_copy(step, None)
        pl.when(other < SUMMERS)(copy.start)

    place = rank * share

    def out_rows(index):
        return pl.ds(pl.multiple_of(place + (index % SUMMERS) * piece, 8), piece)

    def out_copy(step):
        other, device = far_peer(step)
        return pltpu.make_async_remote_copy(
            src_ref=total.at[out_rows(pair)], dst_ref=total.at[out_rows(pair)],
            send_sem=out_s.at[step], recv_sem=out_r.at[pair], device_id=device, device_id_type=MESH)

    def out_arrival(step):
        other, device = far_peer(step)
        return other, pltpu.make_async_remote_copy(
            src_ref=total.at[out_rows(other)], dst_ref=total.at[out_rows(other)],
            send_sem=out_s.at[step], recv_sem=out_r.at[other], device_id=device, device_id_type=MESH)

    @pl.when(pair < SUMMERS)
    def _():
        far[pair] = mine[rows(pair % SUMMERS, piece), :]
        for step in range(1, FAR):
            far_copy(step, 1)[1].wait_recv()
        acc = far[0]
        for n in range(1, FAR):
            acc = acc + far[n]
        total[out_rows(pair), :] = acc * factor
        for step in range(1, FAR):
            out_copy(step).start()

    for step in range(1, FAR):
        other, copy = out_arrival(step)
        pl.when(other < SUMMERS)(copy.wait_recv)

    def end_copy(step, slot):
        other, device = near_peer(step)
        at = rows(rank if slot is None else other, share)
        return pltpu.make_async_remote_copy(
            src_ref=total.at[at], dst_ref=total.at[at],
            send_sem=end_s.at[step], recv_sem=end_r.at[rank if slot is None else other],
            device_id=device, device_id_type=MESH)

    for step in range(1, NEAR):
        end_copy(step, None).start()

    def share_in(index):
        at = rows(index, share)
        return pltpu.make_async_remote_copy(
            src_ref=total.at[at], dst_ref=total.at[at], send_sem=end_s.at[1], recv_sem=end_r.at[index],
            device_id=near_peer(1)[1], device_id_type=MESH)

    def begin():
        pl.when(rank != 0)(share_in(0).wait_recv)
        work[:B, :B] = total[:B, :]

    def complete():
        for index in range(1, NEAR):
            pl.when(rank != index)(share_in(index).wait_recv)
        for n, (i, j) in enumerate(blocks):
            block = total[n * B : (n + 1) * B, :]
            gram_ref[i * B : (i + 1) * B, j * B : (j + 1) * B] = block
            if i != j:
                gram_ref[j * B : (j + 1) * B, i * B : (i + 1) * B] = block.T
        work[...] = gram_ref[...]

    def target(index):
        return filtered_ref.at[index // 2, pl.ds(pl.multiple_of(lax.rem(index, 2) * 16, 8), ROWS // 2)]

    def move(k, to_half):
        return pltpu.make_async_remote_copy(
            src_ref=parts.at[k, rows(to_half, ROWS // 2)], dst_ref=target(rank), send_sem=home_s.at[k, to_half],
            recv_sem=home_r.at[rank], device_id=(k, pair * 2 + to_half), device_id_type=MESH)

    local = pltpu.make_async_copy(parts.at[band, rows(half, ROWS // 2)], target(rank), local_s)
    across = (((1,), (1,)), ((), ()))
    cells = high.shape[0] // 2

    def rotate(k, inverse_rows):
        high_rot, low_rot = split(inverse_rows)
        both = jnp.concatenate([high_rot, low_rot], axis=0)
        for to_half in range(2):
            at = slice(to_half * cells, (to_half + 1) * cells)
            wide = lax.dot_general(high[at, :], both, across, preferred_element_type=jnp.float32)
            more = lax.dot_general(low[at, :], high_rot, across, preferred_element_type=jnp.float32)
            value = wide[:, :B] + (wide[:, B:] + more)
            parts[k, rows(to_half, ROWS // 2)] = value.reshape(ROWS // 2, DEPTH, B)
            here = (k == band) & (to_half == half)
            pl.when(jnp.logical_not(here))(lambda to_half=to_half: move(k, to_half).start())
            pl.when(here)(local.start)

    factor_steps(work, begin, complete, rotate)
    for step in range(1, NEAR):
        other, device = near_peer(step)
        pltpu.make_async_remote_copy(
            src_ref=parts.at[0, rows(0, ROWS // 2)], dst_ref=target(other), send_sem=home_s.at[0, 0], recv_sem=home_r.at[other],
            device_id=device, device_id_type=MESH).wait_recv()
    local.wait()
    for k in range(4):
        for to_half in range(2):
            here = (k == band) & (to_half == half)
            pl.when(jnp.logical_not(here))(lambda k=k, to_half=to_half: move(k, to_half).wait_send())

    for step in range(1, NEAR):
        near_copy(step).wait_send()
        end_copy(step, None).wait_send()
    for step in range(1, FAR):
        other, copy = far_copy(step, None)
        pl.when(other < SUMMERS)(copy.wait_send)

    @pl.when(pair < SUMMERS)
    def _():
        for step in range(1, FAR):
            out_copy(step).wait_send()


ROWS = 32
DEPTH = 48
WIDE = 128
CELLS = ROWS * DEPTH
PROJ = 32
REACH = 6
FLAGS = PROJ
GROUP = 8
STRIP = 8
STRIPS = ROWS // STRIP
PIECE = 4
PIECES = ROWS // PIECE
WINDOW = 3
AREA = STRIP * DEPTH


def split(value):
    high = value.astype(jnp.bfloat16)
    return high, (value - high.astype(jnp.float32)).astype(jnp.bfloat16)


def swap(value):
    return pltpu.roll(value, WIDE // 2, value.ndim - 1)


def whole_kernel(
    factor, orb, pot, proj, coupling, planes, counts, gram_ref, filtered_ref,
    e1, e2, second, shift_pot, nonlocal_plane, left, right, raw, notes, scratch_notes, pot_all, corr_sum, corr, corr_in, weights,
    give_cross, give_keep, got_cross, got1, got2, slab,
    local_s, x_s, x_r, own_s, fwd_s, halo_r, small_s, small_r, core_s, core_r, next_s, next_r, last_s, last_r,
    corr_s, corr_r, y2_s, y2_r, out_s, out_r, self_s,
    high_cells, low_cells, pack, *rest,
):
    band, dom = lax.axis_index("band"), lax.axis_index("dom")
    pair, half = dom // 2, dom % 2
    other = 1 - half
    core = lax.rem(band, 2)
    rank = half * 4 + band
    pairs = lax.axis_size("dom") // 2
    partner = (band, pair * 2 + other)
    sibling = (band + 1 - 2 * core, dom)

    def at_pair(step):
        return (band, lax.rem(pair + step + pairs, pairs) * 2 + half)

    def send(src, dst, ssem, rsem, device):
        return pltpu.make_async_remote_copy(
            src_ref=src, dst_ref=dst, send_sem=ssem, recv_sem=rsem, device_id=device, device_id_type=MESH)

    def member(index):
        return (lax.rem(index, 4), pair * 2 + index // 4)

    barrier = pltpu.get_barrier_semaphore()
    for n in range(1, GROUP):
        pl.semaphore_signal(barrier, inc=1, device_id=member(lax.rem(rank + n, GROUP)), device_id_type=MESH)
    for n in range(1, FAR):
        pl.semaphore_signal(barrier, inc=1, device_id=at_pair(n), device_id_type=MESH)

    loads = [pltpu.make_async_copy(orb.at[p], second.at[p], local_s.at[p]) for p in range(4)]
    for copy in loads:
        copy.start()
    lane = lax.broadcasted_iota(jnp.int32, (DEPTH, WIDE), 1)
    lower = lane < WIDE // 2
    kept = (lane // (WIDE // 2)) == half

    share = pl.ds(pl.multiple_of(core * (PROJ // 2), 16), PROJ // 2)
    twin = pl.ds(pl.multiple_of((1 - core) * (PROJ // 2), 16), PROJ // 2)
    small = [
        send(pot, pot_all.at[pl.ds(4 * half, 4)], small_s.at[0], small_r.at[0], partner),
        send(notes.at[1 + half], notes.at[1 + half], small_s.at[1], small_r.at[1], partner),
        send(raw.at[1 + half, share], raw.at[1 + half, share], small_s.at[2], small_r.at[2], partner),
    ]
    small_in = [
        send(pot, pot_all.at[pl.ds(4 * other, 4)], small_s.at[0], small_r.at[0], partner),
        send(notes.at[1 + other], notes.at[1 + other], small_s.at[1], small_r.at[1], partner),
        send(raw.at[1 + other, share], raw.at[1 + other, share], small_s.at[2], small_r.at[2], partner),
    ]
    across = send(raw.at[1 + other, share], raw.at[1 + other, share], core_s, core_r, sibling)
    across_in = send(raw.at[1 + other, twin], raw.at[1 + other, twin], core_s, core_r, sibling)
    onward = [
        send(notes.at[2], notes.at[0], next_s.at[0], next_r.at[0], at_pair(1)),
        send(raw.at[2, share], raw.at[0, share], next_s.at[1], next_r.at[1], at_pair(1)),
    ]
    last = send(raw.at[0, share], raw.at[0, share], last_s, last_r, sibling)
    last_in = send(raw.at[0, twin], raw.at[0, twin], last_s, last_r, sibling)

    def piece_rows(c):
        return pl.ds(c * PIECE, PIECE)

    def cross(c):
        at = (slice(None), piece_rows(c))
        return send(give_cross.at[at], got_cross.at[at], x_s.at[c], x_r.at[c], partner)

    def keep(c):
        at = piece_rows(c)
        return send(give_keep.at[:, at], got1.at[other, :, at], own_s.at[c], halo_r.at[other, c],
                    at_pair(2 * half - 1))

    def forward(c):
        at = piece_rows(c)
        return send(got_cross.at[:, at], got1.at[half, :, at], fwd_s.at[c], halo_r.at[half, c],
                    at_pair(1 - 2 * half))

    def halo_in(side, c):
        at = piece_rows(c)
        return send(give_keep.at[:, at], got1.at[side, :, at], own_s.at[c], halo_r.at[side, c], at_pair(1))

    line = lax.broadcasted_iota(jnp.int32, (PROJ, WIDE), 0)
    column = lax.broadcasted_iota(jnp.int32, (PROJ, WIDE), 1)
    start, live = jnp.zeros_like(line), jnp.zeros_like(line)
    for a in range(PROJ // MAXPROJ):
        at_atom = (line >> 2) == a
        start = jnp.where(at_atom, planes[a] - dom * 4, start)
        live = jnp.where(at_atom, counts[a], live)
        scratch_notes[a * MAXPROJ : (a + 1) * MAXPROJ, 0:MAXPROJ] = coupling[a]
    same = (line >> 2) == (column >> 2)
    spread_out = jnp.zeros((PROJ, WIDE), jnp.float32)
    for j in range(MAXPROJ):
        value = jnp.broadcast_to(scratch_notes[:, j : j + 1], (PROJ, WIDE))
        spread_out = jnp.where(same & ((column & 3) == j), value, spread_out)
    square = jnp.concatenate([spread_out, jnp.zeros((WIDE - PROJ, WIDE), jnp.float32)], axis=0)
    symmetric = 0.5 * (spread_out + square.T[:PROJ])
    symmetric = jnp.where(((line & 3) < live) & ((column & 3) < live), symmetric, 0.0)
    wanted = jnp.full((PROJ, WIDE), -WIDE, jnp.int32)
    for reach in range(REACH):
        for k in range(SPAN):
            wanted = jnp.where(column == FLAGS + reach * SPAN + k, reach - k, wanted)
    flag_rows = jnp.where(wanted == start, 1.0, 0.0)
    notes[1 + half] = jnp.where(column < FLAGS, symmetric, flag_rows)
    for a in range(PROJ // MAXPROJ):
        raw[1 + half, a * MAXPROJ : (a + 1) * MAXPROJ, :] = proj[a]
    pot_all[pl.ds(4 * half, 4)] = pot[...]
    for copy in loads:
        copy.wait()

    def pack_piece(c, carry):
        for n in range(PIECE):
            r = c * PIECE + n
            for j in range(2):
                near, far = second[j, r], second[j + 2, r]
                give_cross[j, r] = jnp.where(kept, swap(near), far)
                give_keep[j, r] = jnp.where(kept, near, swap(far))
        return carry

    def start_piece(c):
        cross(c).start()
        keep(c).start()

    lax.fori_loop(0, WINDOW, pack_piece, 0)
    pl.semaphore_wait(barrier, GROUP + FAR - 2)
    for copy in small:
        copy.start()
    for c in range(WINDOW):
        start_piece(c)
    lax.fori_loop(WINDOW, PIECES, pack_piece, 0)

    for copy in small_in:
        copy.wait_recv()
    across.start()
    for copy in onward[:1]:
        copy.start()

    def placed(group, reach):
        total = jnp.zeros((PROJ, CELLS), jnp.float32)
        for k in range(SPAN):
            flag = notes[group, :, FLAGS + reach * SPAN + k : FLAGS + reach * SPAN + k + 1]
            total = total + flag * raw[group, :, k * CELLS : (k + 1) * CELLS]
        return total

    def store_pair(p, groups, reach, slot):
        beta = jnp.concatenate([placed(group, reach) for group in groups], axis=0)
        high_part, low_part = split(beta)
        both = jnp.concatenate([high_part, low_part], axis=0)
        for n in range(STRIPS):
            left[p, n, slot * 128 : (slot + 1) * 128, :] = both[:, n * AREA : (n + 1) * AREA]
        high32 = high_part.astype(jnp.float32)
        wide = jnp.concatenate([high32, low_part.astype(jnp.float32)], axis=0)
        turned = wide.T.astype(jnp.bfloat16)
        right[p, :, slot * 256 : slot * 256 + 128] = turned
        right[p, :, slot * 256 + 128 : slot * 256 + 192] = turned[:, :64]
        right[p, :, slot * 256 + 192 : slot * 256 + 256] = jnp.zeros((CELLS, 64), jnp.bfloat16)

    diagonal = lax.broadcasted_iota(jnp.int32, (DEPTH, DEPTH), 0) == lax.broadcasted_iota(
        jnp.int32, (DEPTH, DEPTH), 1)
    constant = -1.5 * center_weight - 7.0

    def spread(n, carry):
        p, r = n // ROWS, lax.rem(n, ROWS)
        columns = []
        for extra in (0, 4):
            line = jnp.broadcast_to(pot_all[p + extra, pl.ds(r, 1), :], (DEPTH, DEPTH))
            columns.append(jnp.sum(jnp.where(diagonal, line, 0.0), axis=1, keepdims=True))
        shift_pot[p, r] = jnp.where(lower, columns[0], columns[1]) + constant
        return carry

    def receive_piece(c):
        cross(c).wait_recv()
        forward(c).start()
        cross(c).wait_send()
        keep(c).wait_send()
        if c + WINDOW < PIECES:
            start_piece(c + WINDOW)

        def one(n, carry):
            r = c * PIECE + n
            for j in range(2):
                arrived = got_cross[j, r]
                e1[4 + j, r] = jnp.where(kept, second[j, r], arrived)
                e1[6 + j, r] = jnp.where(kept, second[j + 2, r], swap(arrived))
            return carry

        lax.fori_loop(0, PIECE, one, 0)

    for p in (2, 3):
        left[p, :, 128:256, :] = jnp.zeros((STRIPS, 128, AREA), jnp.bfloat16)
        right[p, :, 256:512] = jnp.zeros((CELLS, 256), jnp.bfloat16)
    def spread_rows(n):
        lax.fori_loop(n * 4 * ROWS // PIECES, (n + 1) * 4 * ROWS // PIECES, spread, 0)

    def add_strip(field, strip):
        def part(p, total):
            cells = field[4 + p, pl.ds(strip * STRIP, STRIP)].reshape(AREA, WIDE)
            both = jnp.concatenate(split(cells), axis=1)
            return total + lax.dot_general(
                left[p, strip], both, (((1,), (0,)), ((), ())), preferred_element_type=jnp.float32)

        corr_sum[...] = lax.fori_loop(0, 4, part, corr_sum[...])

    def share_sums(phase):
        total = corr_sum[:, :WIDE] + corr_sum[:, WIDE:]
        corr_sum[...] = jnp.zeros_like(corr_sum)
        near, tail = total[0:64] + total[64:128], total[128:192] + total[192:256]
        corr[phase, 0] = tail[:PROJ]
        corr[phase, 1] = near[PROJ:]
        corr[phase, 2] = near[:PROJ] + swap(tail[PROJ:])
        down = send(corr.at[phase, 0], corr_in.at[phase, 1], corr_s.at[phase, 0], corr_r.at[phase, 1], at_pair(-1))
        up = send(corr.at[phase, 1], corr_in.at[phase, 0], corr_s.at[phase, 1], corr_r.at[phase, 0], at_pair(1))
        down.start()
        up.start()
        return [down, up]

    def weigh(phase, copies):
        for copy in copies:
            copy.wait_recv()
        before = corr[phase, 0] + swap(corr_in[phase, 0])
        after = corr[phase, 1] + swap(corr_in[phase, 1])
        before, own, after = (
            dot_f32(notes[group, :, :PROJ], value, ((1,), (0,)))
            for group, value in ((0, before), (1, corr[phase, 2]), (2, after))
        )
        in_low = lax.broadcasted_iota(jnp.int32, (PROJ, WIDE), 1) < WIDE // 2
        zero = jnp.zeros((64, WIDE), jnp.bfloat16)
        parts = []
        for low_value, high_value in ((own, after), (before, swap(own))):
            value = jnp.concatenate(
                [jnp.where(in_low, low_value, 0.0), jnp.where(in_low, 0.0, high_value)], axis=0)
            high_part, low_part = split(value)
            parts += [high_part, high_part, low_part, zero]
        weights[...] = jnp.concatenate(parts, axis=0)

    def open_rows(field, got, base, count):
        def one(n, carry):
            r = base + n
            for j in range(2):
                near, far = field[4 + j, r], field[6 + j, r]
                up, down = got[0, j, r], got[1, j, r]
                field[j, r] = swap(jnp.where(lower, near, up))
                field[2 + j, r] = jnp.where(lower, up, swap(far))
                field[8 + j, r] = swap(jnp.where(lower, down, near))
                field[10 + j, r] = jnp.where(lower, swap(far), down)
            return carry

        lax.fori_loop(0, count, one, 0)

    def apply(field, base, count, scale, write):
        def plane(p, carry):
            product = lax.dot_general(
                right[p, base * DEPTH : (base + count) * DEPTH, :], weights[...],
                (((1,), (0,)), ((), ())), preferred_element_type=jnp.float32)
            nonlocal_plane[:count] = product.reshape(count, DEPTH, WIDE)

            def row(n, inner):
                r = base + n
                centre = field[p + 4, r]
                total = centre * shift_pot[p, r] + nonlocal_plane[n]
                for k in range(1, 5):
                    pair_x = field[p + 4 + k, r] + field[p + 4 - k, r]
                    pair_y = field[p + 4, lax.rem(r + k, ROWS)] + field[p + 4, lax.rem(r + ROWS - k, ROWS)]
                    pair_z = pltpu.roll(centre, k, 0) + pltpu.roll(centre, DEPTH - k, 0)
                    total = total + (-0.5 * side_weights[k - 1]) * ((pair_x + pair_y) + pair_z)
                write(p, r, total * scale)
                return inner

            lax.fori_loop(0, count, row, 0)
            return carry

        lax.fori_loop(0, 4, plane, 0)

    def open_first(strip):
        for side in range(2):
            for n in range(STRIP // PIECE):
                halo_in(side, strip * (STRIP // PIECE) + n).wait_recv()
        open_rows(e1, got1, strip * STRIP, STRIP)

    spread_rows(0)
    across_in.wait_recv()
    onward[1].start()
    receive_piece(0)
    store_pair(0, (1, 2), 0, 0)
    store_pair(1, (1, 2), 1, 0)
    spread_rows(1)
    receive_piece(1)
    store_pair(2, (1, 2), 2, 0)
    store_pair(3, (1, 2), 3, 0)
    spread_rows(2)
    receive_piece(2)
    for copy in onward:
        copy.wait_recv()
    last.start()
    spread_rows(3)
    spread_rows(4)
    receive_piece(3)
    last_in.wait_recv()
    store_pair(0, (0, 1), 4, 1)
    store_pair(1, (0, 1), 5, 1)
    corr_sum[...] = jnp.zeros_like(corr_sum)
    add_strip(e1, 0)
    receive_piece(4)
    spread_rows(5)
    add_strip(e1, 1)
    receive_piece(5)
    spread_rows(6)
    open_first(0)
    receive_piece(6)
    spread_rows(7)
    add_strip(e1, 2)
    receive_piece(7)
    add_strip(e1, 3)
    copies1 = share_sums(0)
    for strip in range(1, STRIPS):
        open_first(strip)
    for c in range(PIECES):
        forward(c).wait_send()
    weigh(0, copies1)

    def write_first(p, r, value):
        e2[p + 4, r] = value

    def up2(c):
        at = piece_rows(c)
        return send(give_cross.at[:, at], got2.at[0, :, at], y2_s.at[0, c], y2_r.at[0, c], at_pair(1))

    def down2(c):
        at = piece_rows(c)
        return send(give_keep.at[:, at], got2.at[1, :, at], y2_s.at[1, c], y2_r.at[1, c], at_pair(-1))

    def first_strip(strip):
        apply(e1, strip * STRIP, STRIP, 1.0 / 6.0, write_first)

        def pack(n, inner):
            r = strip * STRIP + n
            for j in range(2):
                near, turned = e2[4 + j, r], swap(e2[6 + j, r])
                give_cross[j, r] = jnp.where(lower, turned, near)
                give_keep[j, r] = jnp.where(lower, near, turned)
            return inner

        lax.fori_loop(0, STRIP, pack, 0)
        for c in range(2 * strip, 2 * strip + 2):
            if c < WINDOW:
                up2(c).start()
                down2(c).start()
        add_strip(e2, strip)

    for strip in range(STRIPS):
        first_strip(strip)
    copies2 = share_sums(1)
    weigh(1, copies2)

    def write_second(p, r, value):
        second[p, r] = value - e1[p + 4, r]

    def give(index, part):
        src = second.at[index // 2, pl.ds(lax.rem(index, 2) * 16 + part * PIECE, PIECE)]
        return send(src, slab.at[rank, pl.ds(part * PIECE, PIECE)], out_s.at[index, part], out_r.at[rank, part],
                    member(index))

    def own_part(part):
        src = second.at[rank // 2, pl.ds(lax.rem(rank, 2) * 16 + part * PIECE, PIECE)]
        return pltpu.make_async_copy(src, slab.at[rank, pl.ds(part * PIECE, PIECE)], self_s.at[part])

    def second_piece(c):
        for copy in (up2(c), down2(c)):
            copy.wait_recv()
            copy.wait_send()
        if c + WINDOW < PIECES:
            up2(c + WINDOW).start()
            down2(c + WINDOW).start()
        open_rows(e2, got2, c * PIECE, PIECE)
        apply(e2, c * PIECE, PIECE, 1.0 / 3.0, write_second)
        row_half, part = c // 4, c % 4
        for n in range(4):
            index = 2 * lax.rem(n + rank // 2 + 2, 4) + row_half
            pl.when(index != rank)(lambda index=index: give(index, part).start())
        pl.when(lax.rem(rank, 2) == row_half)(own_part(part).start)

    for c in range(PIECES):
        second_piece(c)

    blocks = tri_blocks(NORB)
    pack[...] = jnp.zeros_like(pack)

    def repack(n, carry):
        cells = pl.ds(pl.multiple_of(n * DEPTH, 16), DEPTH)
        more = pl.ds(pl.multiple_of(CELLS // 2 + n * DEPTH, 16), DEPTH)
        for b in range(4):
            at = slice(b * WIDE, (b + 1) * WIDE)
            here, there = slab[b, n], slab[4 + b, n]
            high_cells[cells, at], low_cells[cells, at] = split(jnp.where(lower, here, swap(there)))
            high_cells[more, at], low_cells[more, at] = split(jnp.where(lower, swap(here), there))
        return carry

    def add_gram(part):
        contract = (((0,), (0,)), ((), ()))

        def chunk(side, carry):
            cells = pl.ds(pl.multiple_of(side * (CELLS // 2) + part * AREA, 16), AREA)
            for i in range(NORB // B):
                own, wide = slice(i * B, (i + 1) * B), slice(0, (i + 1) * B)
                row = lax.dot_general(
                    high_cells[cells, own], high_cells[cells, wide], contract, preferred_element_type=jnp.float32)
                row += lax.dot_general(
                    high_cells[cells, own], low_cells[cells, wide], contract, preferred_element_type=jnp.float32)
                row += lax.dot_general(
                    low_cells[cells, own], high_cells[cells, wide], contract, preferred_element_type=jnp.float32)
                for j in range(i + 1):
                    n = blocks.index((i, j))
                    pack[n * B : (n + 1) * B, :] += row[:, j * B : (j + 1) * B]
            return carry

        lax.fori_loop(0, 2, chunk, 0)

    for section in range(2):
        for part in (2 * section, 2 * section + 1):
            for n in range(1, GROUP):
                index = lax.rem(rank + n, GROUP)
                send(second.at[0, pl.ds(0, PIECE)], slab.at[index, pl.ds(part * PIECE, PIECE)],
                     out_s.at[index, part], out_r.at[index, part], member(index)).wait_recv()
            own_part(part).wait()
            lax.fori_loop(part * PIECE, (part + 1) * PIECE, repack, 0)
        add_gram(section)

    for copy in small + [across, last] + onward + copies1 + copies2:
        copy.wait_send()
    for n in range(1, GROUP):
        for part in range(4):
            give(lax.rem(rank + n, GROUP), part).wait_send()
    finish_part(factor, gram_ref, filtered_ref, high_cells, low_cells, pack, *rest[:5], second, *rest[5:])


def run(orbitals, potential, projectors, coupling, atom_plane, projector_count, factor):
    dma = pltpu.SemaphoreType.DMA
    f32, bf16 = jnp.float32, jnp.bfloat16
    smem = pl.BlockSpec(memory_space=pltpu.SMEM)
    vmem, hbm = pl.BlockSpec(memory_space=pltpu.VMEM), pl.BlockSpec(memory_space=pl.ANY)
    block = (ROWS, DEPTH, WIDE)
    packed = len(tri_blocks(NORB)) * B
    share = packed // NEAR
    return pl.pallas_call(
        functools.partial(whole_kernel, factor),
        out_shape=[jax.ShapeDtypeStruct((NORB, NORB), f32), jax.ShapeDtypeStruct((4,) + block, f32)],
        in_specs=[hbm, vmem, vmem, vmem, smem, smem],
        out_specs=[vmem, hbm],
        scratch_shapes=[
            pltpu.VMEM((12,) + block, f32),
            pltpu.VMEM((12,) + block, f32),
            pltpu.VMEM((4,) + block, f32),
            pltpu.VMEM((4,) + block, f32),
            pltpu.VMEM((STRIP, DEPTH, WIDE), f32),
            pltpu.VMEM((4, STRIPS, 256, AREA), bf16),
            pltpu.VMEM((4, CELLS, 512), bf16),
            pltpu.VMEM((3, PROJ, SPAN * CELLS), f32),
            pltpu.VMEM((3, PROJ, 128), f32),
            pltpu.VMEM((PROJ, MAXPROJ), f32),
            pltpu.VMEM((8, ROWS, DEPTH), f32),
            pltpu.VMEM((256, 2 * WIDE), f32),
            pltpu.VMEM((2, 3, PROJ, WIDE), f32),
            pltpu.VMEM((2, 2, PROJ, WIDE), f32),
            pltpu.VMEM((512, WIDE), bf16),
            pltpu.VMEM((2,) + block, f32),
            pltpu.VMEM((2,) + block, f32),
            pltpu.VMEM((2,) + block, f32),
            pltpu.VMEM((2, 2) + block, f32),
            pltpu.VMEM((2, 2) + block, f32),
            pltpu.VMEM((GROUP, ROWS // 2, DEPTH, WIDE), f32),
            dma((4,)), dma((PIECES,)), dma((PIECES,)), dma((PIECES,)), dma((PIECES,)), dma((2, PIECES)),
            dma((3,)), dma((3,)), dma(()), dma(()), dma((2,)), dma((2,)), dma(()), dma(()),
            dma((2, 2)), dma((2, 2)), dma((2, PIECES)), dma((2, PIECES)),
            dma((GROUP, 4)), dma((GROUP, 4)), dma((4,)),
            pltpu.VMEM((CELLS, NORB), bf16),
            pltpu.VMEM((CELLS, NORB), bf16),
            pltpu.VMEM((packed, B), f32),
            pltpu.VMEM((NEAR, share, B), f32),
            pltpu.VMEM((share, B), f32),
            pltpu.VMEM((FAR, share // SUMMERS, B), f32),
            pltpu.VMEM((packed, B), f32),
            pltpu.VMEM((NORB, NORB), f32),
            dma((NEAR,)), dma((NEAR,)), dma((FAR,)), dma((FAR,)),
            dma((FAR,)), dma((FAR,)), dma((NEAR,)), dma((NEAR,)),
            dma(()), dma((4, 2)), dma((NEAR,)),
        ],
        compiler_params=pltpu.CompilerParams(collective_id=2, has_side_effects=True, vmem_limit_bytes=62 * 2**20),
    )(orbitals, potential, projectors, coupling, atom_plane, projector_count)


def settle_kernel(gram, filtered, gram_out, filtered_out, sems):
    copies = [pltpu.make_async_copy(filtered.at[p], filtered_out.at[p], sems.at[p]) for p in range(4)]
    copies.append(pltpu.make_async_copy(gram, gram_out, sems.at[4]))
    for copy in copies:
        copy.start()
    for copy in copies:
        copy.wait()


def settle(gram, filtered):
    hbm = pl.BlockSpec(memory_space=pl.ANY)
    return pl.pallas_call(
        settle_kernel,
        out_shape=[jax.ShapeDtypeStruct(x.shape, x.dtype) for x in (gram, filtered)],
        in_specs=[hbm, hbm],
        out_specs=[hbm, hbm],
        scratch_shapes=[pltpu.SemaphoreType.DMA((5,))],
        compiler_params=pltpu.CompilerParams(vmem_limit_bytes=8 * 2**20),
    )(gram, filtered)


def shards(orbitals, potential, projectors, coupling, atom_plane, projector_count):
    planes, side_y, side_z, _ = orbitals.shape
    total_cells = planes * side_y * side_z * lax.axis_size("dom")
    gram, filtered = run(
        orbitals, potential, projectors, coupling, atom_plane, projector_count, 1.0 / total_cells)
    gram, filtered = settle(gram, filtered)
    return (filtered, gram)


def solution(mesh):
    placed = (
        P("dom", None, None, "band"),
        P("dom", None, None),
        P("dom", None, None),
        P("dom", None, None),
        P("dom"),
        P("dom"),
    )
    return jax.shard_map(
        shards,
        mesh=mesh,
        in_specs=placed,
        out_specs=(P("dom", None, None, "band"), P()),
        check_vma=False,
    )
```

```python
import functools

import jax
import jax.numpy as jnp
from jax import lax
from jax.experimental import pallas as pl
from jax.experimental.pallas import tpu as pltpu
from jax.sharding import PartitionSpec as P

NORB = 512
HALO = 4
SPAN = 3
MAXPROJ = 4
B = 128

center_weight = -205.0 / 72.0
side_weights = (8.0 / 5.0, -1.0 / 5.0, 8.0 / 315.0, -1.0 / 560.0)
HIGH = lax.Precision.HIGHEST


HIGHEST = lax.Precision.HIGHEST


def dot_f32(a, b, dims):
    return lax.dot_general(a, b, (dims, ((), ())), precision=HIGHEST, preferred_element_type=jnp.float32)


def block_inverse(tiles):
    count = len(tiles)
    tiles = list(tiles)
    shape = tiles[0].shape
    lane = lax.broadcasted_iota(jnp.int32, shape, 1)
    sub = lax.broadcasted_iota(jnp.int32, shape, 0)
    done = []
    for j in range(count):
        base = 8 * j
        cols = [
            [jnp.broadcast_to(tiles[t][:, base + k : base + k + 1], shape) for k in range(8)]
            for t in range(j, count)
        ]
        inside = (lane >= base) & (lane < base + 8)
        unit = jnp.where(lane == sub + base, 1.0, 0.0)
        own = jnp.where(inside, unit, tiles[j])
        rows = [jnp.broadcast_to(own[k : k + 1, :], shape) for k in range(8)]
        splat = [
            [jnp.broadcast_to(cols[0][k][i : i + 1, :], shape) if i >= k else None for k in range(8)]
            for i in range(8)
        ]
        rest = [jnp.where(inside, 0.0, tiles[t]) for t in range(j + 1, count)]
        result = jnp.zeros(shape, jnp.float32)
        for k in range(8):
            scale = lax.rsqrt(splat[k][k])
            rows[k] = rows[k] * scale
            for i in range(k + 1, 8):
                splat[i][k] = splat[i][k] * scale
            for i in range(k + 1, 8):
                for m in range(k + 1, i + 1):
                    splat[i][m] = splat[i][m] - splat[i][k] * splat[m][k]
                rows[i] = rows[i] - splat[i][k] * rows[k]
            for t in range(len(rest)):
                below = cols[t + 1]
                below[k] = below[k] * scale
                for m in range(k + 1, 8):
                    below[m] = below[m] - below[k] * splat[m][k]
                rest[t] = rest[t] - below[k] * rows[k]
            result = jnp.where(sub == k, rows[k], result)
        done.append(jnp.where(lane <= sub + base, result, 0.0))
        tiles[j + 1 :] = rest
    return done


def factor_steps(work, begin, complete, done):
    size = work.shape[0]

    def step(k, carry):
        at = pl.ds(pl.multiple_of(k * B, B), B)
        pl.when(k == 0)(begin)
        tiles = [work[pl.ds(pl.multiple_of(k * B + 8 * t, 8), 8), at] for t in range(B // 8)]
        corner = jnp.concatenate(block_inverse(tiles), axis=0)
        pl.when(k == 0)(complete)
        row_id = lax.broadcasted_iota(jnp.int32, (size, B), 0)
        column = jnp.where(row_id >= (k + 1) * B, work[:, at], 0.0)
        unit = lax.broadcasted_iota(jnp.int32, (B, B), 0) == lax.broadcasted_iota(jnp.int32, (B, B), 1)
        work[at, at] = jnp.where(unit, 1.0, 0.0)
        scaled = dot_f32(corner, work[at, :], ((1,), (0,)))
        work[at, :] = scaled

        def hand_on(n, inner):
            block = k - n
            rows = work[pl.ds(pl.multiple_of(block * B, B), B), :]
            row_at = lax.broadcasted_iota(jnp.int32, (B, size), 0) + block * B
            done(block, jnp.where(lax.broadcasted_iota(jnp.int32, (B, size), 1) <= row_at, rows, 0.0))
            return inner

        lax.fori_loop(0, jnp.where(k == 1, 0, jnp.where(k == 2, 2, 1)), hand_on, 0)
        below = dot_f32(column, corner, ((1,), (1,)))
        block = work[:, at]
        work[:, at] = jnp.where(row_id >= (k + 1) * B, 0.0, block)
        work[...] = work[...] - dot_f32(below, scaled, ((1,), (0,)))
        return carry

    lax.fori_loop(0, size // B, step, 0)


MESH = pl.DeviceIdType.MESH
NEAR = 8
FAR = 16
SUMMERS = 10


def tri_blocks(size):
    return [(i, j) for i in range(size // B) for j in range(i + 1)]


def finish_part(
    factor, gram_ref, filtered_ref,
    high, low, pack, near, mine, far, total, work, parts, near_s, near_r, far_s, far_r, out_s, out_r, end_s, end_r,
    local_s, home_s, home_r,
):
    band, dom = lax.axis_index("band"), lax.axis_index("dom")
    pair, half = dom // 2, dom % 2
    rank = half * 4 + band
    blocks = tri_blocks(work.shape[0])
    share = len(blocks) * B // NEAR
    piece = share // SUMMERS

    def near_peer(step):
        other = (rank + step) % NEAR
        return other, (other % 4, pair * 2 + other // 4)

    def far_peer(step):
        other = (pair + step) % FAR
        return other, (band, other * 2 + half)

    def rows(index, count):
        return pl.ds(pl.multiple_of(index * count, 8), count)

    def near_copy(step):
        other, device = near_peer(step)
        return pltpu.make_async_remote_copy(
            src_ref=pack.at[rows(other, share)], dst_ref=near.at[rank],
            send_sem=near_s.at[step], recv_sem=near_r.at[rank], device_id=device, device_id_type=MESH)

    def near_arrival(step):
        other, device = near_peer(step)
        return pltpu.make_async_remote_copy(
            src_ref=pack.at[rows(other, share)], dst_ref=near.at[other],
            send_sem=near_s.at[step], recv_sem=near_r.at[other], device_id=device, device_id_type=MESH)

    for step in range(1, NEAR):
        near_copy(step).start()
    near[rank] = pack[rows(rank, share), :]
    for step in range(1, NEAR):
        near_arrival(step).wait_recv()
    acc = near[0]
    for n in range(1, NEAR):
        acc = acc + near[n]
    mine[...] = acc

    def far_copy(step, slot):
        other, device = far_peer(step)
        return other, pltpu.make_async_remote_copy(
            src_ref=mine.at[rows(other % SUMMERS, piece)], dst_ref=far.at[pair if slot is None else other],
            send_sem=far_s.at[step], recv_sem=far_r.at[pair if slot is None else other],
            device_id=device, device_id_type=MESH)

    for step in range(1, FAR):
        other, copy = far_copy(step, None)
        pl.when(other < SUMMERS)(copy.start)

    place = rank * share

    def out_rows(index):
        return pl.ds(pl.multiple_of(place + (index % SUMMERS) * piece, 8), piece)

    def out_copy(step):
        other, device = far_peer(step)
        return pltpu.make_async_remote_copy(
            src_ref=total.at[out_rows(pair)], dst_ref=total.at[out_rows(pair)],
            send_sem=out_s.at[step], recv_sem=out_r.at[pair], device_id=device, device_id_type=MESH)

    def out_arrival(step):
        other, device = far_peer(step)
        return other, pltpu.make_async_remote_copy(
            src_ref=total.at[out_rows(other)], dst_ref=total.at[out_rows(other)],
            send_sem=out_s.at[step], recv_sem=out_r.at[other], device_id=device, device_id_type=MESH)

    @pl.when(pair < SUMMERS)
    def _():
        far[pair] = mine[rows(pair % SUMMERS, piece), :]
        for step in range(1, FAR):
            far_copy(step, 1)[1].wait_recv()
        acc = far[0]
        for n in range(1, FAR):
            acc = acc + far[n]
        total[out_rows(pair), :] = acc * factor
        for step in range(1, FAR):
            out_copy(step).start()

    for step in range(1, FAR):
        other, copy = out_arrival(step)
        pl.when(other < SUMMERS)(copy.wait_recv)

    def end_copy(step, slot):
        other, device = near_peer(step)
        at = rows(rank if slot is None else other, share)
        return pltpu.make_async_remote_copy(
            src_ref=total.at[at], dst_ref=total.at[at],
            send_sem=end_s.at[step], recv_sem=end_r.at[rank if slot is None else other],
            device_id=device, device_id_type=MESH)

    for step in range(1, NEAR):
        end_copy(step, None).start()

    def share_in(index):
        at = rows(index, share)
        return pltpu.make_async_remote_copy(
            src_ref=total.at[at], dst_ref=total.at[at], send_sem=end_s.at[1], recv_sem=end_r.at[index],
            device_id=near_peer(1)[1], device_id_type=MESH)

    def begin():
        pl.when(rank != 0)(share_in(0).wait_recv)
        work[:B, :B] = total[:B, :]

    def complete():
        for index in range(1, NEAR):
            pl.when(rank != index)(share_in(index).wait_recv)
        for n, (i, j) in enumerate(blocks):
            block = total[n * B : (n + 1) * B, :]
            gram_ref[i * B : (i + 1) * B, j * B : (j + 1) * B] = block
            if i != j:
                gram_ref[j * B : (j + 1) * B, i * B : (i + 1) * B] = block.T
        work[...] = gram_ref[...]

    def target(index):
        return filtered_ref.at[index // 2, pl.ds(pl.multiple_of(lax.rem(index, 2) * 16, 8), ROWS // 2)]

    def move(k, to_half):
        return pltpu.make_async_remote_copy(
            src_ref=parts.at[k, rows(to_half, ROWS // 2)], dst_ref=target(rank), send_sem=home_s.at[k, to_half],
            recv_sem=home_r.at[rank], device_id=(k, pair * 2 + to_half), device_id_type=MESH)

    local = pltpu.make_async_copy(parts.at[band, rows(half, ROWS // 2)], target(rank), local_s)
    across = (((1,), (1,)), ((), ()))
    cells = high.shape[0] // 2

    def rotate(k, inverse_rows):
        high_rot, low_rot = split(inverse_rows)
        both = jnp.concatenate([high_rot, low_rot], axis=0)
        for to_half in range(2):
            at = slice(to_half * cells, (to_half + 1) * cells)
            wide = lax.dot_general(high[at, :], both, across, preferred_element_type=jnp.float32)
            more = lax.dot_general(low[at, :], high_rot, across, preferred_element_type=jnp.float32)
            value = wide[:, :B] + (wide[:, B:] + more)
            parts[k, rows(to_half, ROWS // 2)] = value.reshape(ROWS // 2, DEPTH, B)
            here = (k == band) & (to_half == half)
            pl.when(jnp.logical_not(here))(lambda to_half=to_half: move(k, to_half).start())
            pl.when(here)(local.start)

    factor_steps(work, begin, complete, rotate)
    for step in range(1, NEAR):
        other, device = near_peer(step)
        pltpu.make_async_remote_copy(
            src_ref=parts.at[0, rows(0, ROWS // 2)], dst_ref=target(other), send_sem=home_s.at[0, 0], recv_sem=home_r.at[other],
            device_id=device, device_id_type=MESH).wait_recv()
    local.wait()
    for k in range(4):
        for to_half in range(2):
            here = (k == band) & (to_half == half)
            pl.when(jnp.logical_not(here))(lambda k=k, to_half=to_half: move(k, to_half).wait_send())

    for step in range(1, NEAR):
        near_copy(step).wait_send()
        end_copy(step, None).wait_send()
    for step in range(1, FAR):
        other, copy = far_copy(step, None)
        pl.when(other < SUMMERS)(copy.wait_send)

    @pl.when(pair < SUMMERS)
    def _():
        for step in range(1, FAR):
            out_copy(step).wait_send()


ROWS = 32
DEPTH = 48
WIDE = 128
CELLS = ROWS * DEPTH
PROJ = 32
REACH = 6
FLAGS = PROJ
GROUP = 8
STRIP = 8
STRIPS = ROWS // STRIP
PIECE = 4
PIECES = ROWS // PIECE
WINDOW = 3
AREA = STRIP * DEPTH


def split(value):
    high = value.astype(jnp.bfloat16)
    return high, (value - high.astype(jnp.float32)).astype(jnp.bfloat16)


def swap(value):
    return pltpu.roll(value, WIDE // 2, value.ndim - 1)


def whole_kernel(
    factor, orb, pot, proj, coupling, planes, counts, gram_ref, filtered_ref,
    e1, e2, second, shift_pot, nonlocal_plane, left, right, raw, notes, scratch_notes, pot_all, corr_sum, corr, corr_in, weights,
    give_cross, give_keep, got_cross, got1, got2, slab,
    local_s, x_s, x_r, own_s, fwd_s, halo_r, small_s, small_r, core_s, core_r, next_s, next_r, last_s, last_r,
    corr_s, corr_r, y2_s, y2_r, out_s, out_r, self_s,
    high_cells, low_cells, pack, *rest,
):
    band, dom = lax.axis_index("band"), lax.axis_index("dom")
    pair, half = dom // 2, dom % 2
    other = 1 - half
    core = lax.rem(band, 2)
    rank = half * 4 + band
    pairs = lax.axis_size("dom") // 2
    partner = (band, pair * 2 + other)
    sibling = (band + 1 - 2 * core, dom)

    def at_pair(step):
        return (band, lax.rem(pair + step + pairs, pairs) * 2 + half)

    def send(src, dst, ssem, rsem, device):
        return pltpu.make_async_remote_copy(
            src_ref=src, dst_ref=dst, send_sem=ssem, recv_sem=rsem, device_id=device, device_id_type=MESH)

    def member(index):
        return (lax.rem(index, 4), pair * 2 + index // 4)

    barrier = pltpu.get_barrier_semaphore()
    for n in range(1, GROUP):
        pl.semaphore_signal(barrier, inc=1, device_id=member(lax.rem(rank + n, GROUP)), device_id_type=MESH)
    for n in range(1, FAR):
        pl.semaphore_signal(barrier, inc=1, device_id=at_pair(n), device_id_type=MESH)

    loads = [pltpu.make_async_copy(orb.at[p], second.at[p], local_s.at[p]) for p in range(4)]
    for copy in loads:
        copy.start()
    lane = lax.broadcasted_iota(jnp.int32, (DEPTH, WIDE), 1)
    lower = lane < WIDE // 2
    kept = (lane // (WIDE // 2)) == half

    share = pl.ds(pl.multiple_of(core * (PROJ // 2), 16), PROJ // 2)
    twin = pl.ds(pl.multiple_of((1 - core) * (PROJ // 2), 16), PROJ // 2)
    small = [
        send(pot, pot_all.at[pl.ds(4 * half, 4)], small_s.at[0], small_r.at[0], partner),
        send(notes.at[1 + half], notes.at[1 + half], small_s.at[1], small_r.at[1], partner),
        send(raw.at[1 + half, share], raw.at[1 + half, share], small_s.at[2], small_r.at[2], partner),
    ]
    small_in = [
        send(pot, pot_all.at[pl.ds(4 * other, 4)], small_s.at[0], small_r.at[0], partner),
        send(notes.at[1 + other], notes.at[1 + other], small_s.at[1], small_r.at[1], partner),
        send(raw.at[1 + other, share], raw.at[1 + other, share], small_s.at[2], small_r.at[2], partner),
    ]
    across = send(raw.at[1 + other, share], raw.at[1 + other, share], core_s, core_r, sibling)
    across_in = send(raw.at[1 + other, twin], raw.at[1 + other, twin], core_s, core_r, sibling)
    onward = [
        send(notes.at[2], notes.at[0], next_s.at[0], next_r.at[0], at_pair(1)),
        send(raw.at[2, share], raw.at[0, share], next_s.at[1], next_r.at[1], at_pair(1)),
    ]
    last = send(raw.at[0, share], raw.at[0, share], last_s, last_r, sibling)
    last_in = send(raw.at[0, twin], raw.at[0, twin], last_s, last_r, sibling)

    def piece_rows(c):
        return pl.ds(c * PIECE, PIECE)

    def cross(c):
        at = (slice(None), piece_rows(c))
        return send(give_cross.at[at], got_cross.at[at], x_s.at[c], x_r.at[c], partner)

    def keep(c):
        at = piece_rows(c)
        return send(give_keep.at[:, at], got1.at[other, :, at], own_s.at[c], halo_r.at[other, c],
                    at_pair(2 * half - 1))

    def forward(c):
        at = piece_rows(c)
        return send(got_cross.at[:, at], got1.at[half, :, at], fwd_s.at[c], halo_r.at[half, c],
                    at_pair(1 - 2 * half))

    def halo_in(side, c):
        at = piece_rows(c)
        return send(give_keep.at[:, at], got1.at[side, :, at], own_s.at[c], halo_r.at[side, c], at_pair(1))

    line = lax.broadcasted_iota(jnp.int32, (PROJ, WIDE), 0)
    column = lax.broadcasted_iota(jnp.int32, (PROJ, WIDE), 1)
    start, live = jnp.zeros_like(line), jnp.zeros_like(line)
    for a in range(PROJ // MAXPROJ):
        at_atom = (line >> 2) == a
        start = jnp.where(at_atom, planes[a] - dom * 4, start)
        live = jnp.where(at_atom, counts[a], live)
        scratch_notes[a * MAXPROJ : (a + 1) * MAXPROJ, 0:MAXPROJ] = coupling[a]
    same = (line >> 2) == (column >> 2)
    spread_out = jnp.zeros((PROJ, WIDE), jnp.float32)
    for j in range(MAXPROJ):
        value = jnp.broadcast_to(scratch_notes[:, j : j + 1], (PROJ, WIDE))
        spread_out = jnp.where(same & ((column & 3) == j), value, spread_out)
    square = jnp.concatenate([spread_out, jnp.zeros((WIDE - PROJ, WIDE), jnp.float32)], axis=0)
    symmetric = 0.5 * (spread_out + square.T[:PROJ])
    symmetric = jnp.where(((line & 3) < live) & ((column & 3) < live), symmetric, 0.0)
    wanted = jnp.full((PROJ, WIDE), -WIDE, jnp.int32)
    for reach in range(REACH):
        for k in range(SPAN):
            wanted = jnp.where(column == FLAGS + reach * SPAN + k, reach - k, wanted)
    flag_rows = jnp.where(wanted == start, 1.0, 0.0)
    notes[1 + half] = jnp.where(column < FLAGS, symmetric, flag_rows)
    for a in range(PROJ // MAXPROJ):
        raw[1 + half, a * MAXPROJ : (a + 1) * MAXPROJ, :] = proj[a]
    pot_all[pl.ds(4 * half, 4)] = pot[...]
    for copy in loads:
        copy.wait()

    def pack_piece(c, carry):
        for n in range(PIECE):
            r = c * PIECE + n
            for j in range(2):
                near, far = second[j, r], second[j + 2, r]
                give_cross[j, r] = jnp.where(kept, swap(near), far)
                give_keep[j, r] = jnp.where(kept, near, swap(far))
        return carry

    def start_piece(c):
        cross(c).start()
        keep(c).start()

    pl.semaphore_wait(barrier, GROUP + FAR - 2)
    for copy in small:
        copy.start()
    for c in range(WINDOW):
        pack_piece(c, 0)
        start_piece(c)
    lax.fori_loop(WINDOW, PIECES, pack_piece, 0)

    for copy in small_in:
        copy.wait_recv()
    across.start()
    for copy in onward[:1]:
        copy.start()

    def placed(group, reach):
        total = jnp.zeros((PROJ, CELLS), jnp.float32)
        for k in range(SPAN):
            flag = notes[group, :, FLAGS + reach * SPAN + k : FLAGS + reach * SPAN + k + 1]
            total = total + flag * raw[group, :, k * CELLS : (k + 1) * CELLS]
        return total

    def store_pair(p, groups, reach, slot):
        beta = jnp.concatenate([placed(group, reach) for group in groups], axis=0)
        high_part, low_part = split(beta)
        both = jnp.concatenate([high_part, low_part], axis=0)
        for n in range(STRIPS):
            left[p, n, slot * 128 : (slot + 1) * 128, :] = both[:, n * AREA : (n + 1) * AREA]
        high32 = high_part.astype(jnp.float32)
        wide = jnp.concatenate([high32, low_part.astype(jnp.float32)], axis=0)
        turned = wide.T.astype(jnp.bfloat16)
        right[p, :, slot * 256 : slot * 256 + 128] = turned
        right[p, :, slot * 256 + 128 : slot * 256 + 192] = turned[:, :64]
        right[p, :, slot * 256 + 192 : slot * 256 + 256] = jnp.zeros((CELLS, 64), jnp.bfloat16)

    diagonal = lax.broadcasted_iota(jnp.int32, (DEPTH, DEPTH), 0) == lax.broadcasted_iota(
        jnp.int32, (DEPTH, DEPTH), 1)
    constant = -1.5 * center_weight - 7.0

    def spread(n, carry):
        p, r = n // ROWS, lax.rem(n, ROWS)
        columns = []
        for extra in (0, 4):
            line = jnp.broadcast_to(pot_all[p + extra, pl.ds(r, 1), :], (DEPTH, DEPTH))
            columns.append(jnp.sum(jnp.where(diagonal, line, 0.0), axis=1, keepdims=True))
        shift_pot[p, r] = jnp.where(lower, columns[0], columns[1]) + constant
        return carry

    def receive_piece(c):
        cross(c).wait_recv()
        forward(c).start()
        cross(c).wait_send()
        keep(c).wait_send()
        if c + WINDOW < PIECES:
            start_piece(c + WINDOW)

        def one(n, carry):
            r = c * PIECE + n
            for j in range(2):
                arrived = got_cross[j, r]
                e1[4 + j, r] = jnp.where(kept, second[j, r], arrived)
                e1[6 + j, r] = jnp.where(kept, second[j + 2, r], swap(arrived))
            return carry

        lax.fori_loop(0, PIECE, one, 0)

    for p in (2, 3):
        left[p, :, 128:256, :] = jnp.zeros((STRIPS, 128, AREA), jnp.bfloat16)
        right[p, :, 256:512] = jnp.zeros((CELLS, 256), jnp.bfloat16)
    def spread_rows(n):
        lax.fori_loop(n * 4 * ROWS // PIECES, (n + 1) * 4 * ROWS // PIECES, spread, 0)

    def add_strip(field, strip):
        def part(p, total):
            cells = field[4 + p, pl.ds(strip * STRIP, STRIP)].reshape(AREA, WIDE)
            both = jnp.concatenate(split(cells), axis=1)
            return total + lax.dot_general(
                left[p, strip], both, (((1,), (0,)), ((), ())), preferred_element_type=jnp.float32)

        corr_sum[...] = lax.fori_loop(0, 4, part, corr_sum[...])

    def share_sums(phase):
        total = corr_sum[:, :WIDE] + corr_sum[:, WIDE:]
        corr_sum[...] = jnp.zeros_like(corr_sum)
        near, tail = total[0:64] + total[64:128], total[128:192] + total[192:256]
        corr[phase, 0] = tail[:PROJ]
        corr[phase, 1] = near[PROJ:]
        corr[phase, 2] = near[:PROJ] + swap(tail[PROJ:])
        down = send(corr.at[phase, 0], corr_in.at[phase, 1], corr_s.at[phase, 0], corr_r.at[phase, 1], at_pair(-1))
        up = send(corr.at[phase, 1], corr_in.at[phase, 0], corr_s.at[phase, 1], corr_r.at[phase, 0], at_pair(1))
        down.start()
        up.start()
        return [down, up]

    def weigh(phase, copies):
        for copy in copies:
            copy.wait_recv()
        before = corr[phase, 0] + swap(corr_in[phase, 0])
        after = corr[phase, 1] + swap(corr_in[phase, 1])
        before, own, after = (
            dot_f32(notes[group, :, :PROJ], value, ((1,), (0,)))
            for group, value in ((0, before), (1, corr[phase, 2]), (2, after))
        )
        in_low = lax.broadcasted_iota(jnp.int32, (PROJ, WIDE), 1) < WIDE // 2
        zero = jnp.zeros((64, WIDE), jnp.bfloat16)
        parts = []
        for low_value, high_value in ((own, after), (before, swap(own))):
            value = jnp.concatenate(
                [jnp.where(in_low, low_value, 0.0), jnp.where(in_low, 0.0, high_value)], axis=0)
            high_part, low_part = split(value)
            parts += [high_part, high_part, low_part, zero]
        weights[...] = jnp.concatenate(parts, axis=0)

    def open_rows(field, got, base, count):
        def one(n, carry):
            r = base + n
            for j in range(2):
                near, far = field[4 + j, r], field[6 + j, r]
                up, down = got[0, j, r], got[1, j, r]
                field[j, r] = swap(jnp.where(lower, near, up))
                field[2 + j, r] = jnp.where(lower, up, swap(far))
                field[8 + j, r] = swap(jnp.where(lower, down, near))
                field[10 + j, r] = jnp.where(lower, swap(far), down)
            return carry

        lax.fori_loop(0, count, one, 0)

    def apply(field, base, count, scale, write):
        def plane(p, carry):
            product = lax.dot_general(
                right[p, base * DEPTH : (base + count) * DEPTH, :], weights[...],
                (((1,), (0,)), ((), ())), preferred_element_type=jnp.float32)
            nonlocal_plane[:count] = product.reshape(count, DEPTH, WIDE)

            def row(n, inner):
                r = base + n
                centre = field[p + 4, r]
                total = centre * shift_pot[p, r] + nonlocal_plane[n]
                for k in range(1, 5):
                    pair_x = field[p + 4 + k, r] + field[p + 4 - k, r]
                    pair_y = field[p + 4, lax.rem(r + k, ROWS)] + field[p + 4, lax.rem(r + ROWS - k, ROWS)]
                    pair_z = pltpu.roll(centre, k, 0) + pltpu.roll(centre, DEPTH - k, 0)
                    total = total + (-0.5 * side_weights[k - 1]) * ((pair_x + pair_y) + pair_z)
                write(p, r, total * scale)
                return inner

            lax.fori_loop(0, count, row, 0)
            return carry

        lax.fori_loop(0, 4, plane, 0)

    def open_first(strip):
        for side in range(2):
            for n in range(STRIP // PIECE):
                halo_in(side, strip * (STRIP // PIECE) + n).wait_recv()
        open_rows(e1, got1, strip * STRIP, STRIP)

    spread_rows(0)
    across_in.wait_recv()
    onward[1].start()
    receive_piece(0)
    store_pair(0, (1, 2), 0, 0)
    store_pair(1, (1, 2), 1, 0)
    spread_rows(1)
    receive_piece(1)
    store_pair(2, (1, 2), 2, 0)
    store_pair(3, (1, 2), 3, 0)
    spread_rows(2)
    receive_piece(2)
    for copy in onward:
        copy.wait_recv()
    last.start()
    spread_rows(3)
    spread_rows(4)
    receive_piece(3)
    last_in.wait_recv()
    store_pair(0, (0, 1), 4, 1)
    store_pair(1, (0, 1), 5, 1)
    corr_sum[...] = jnp.zeros_like(corr_sum)
    add_strip(e1, 0)
    receive_piece(4)
    spread_rows(5)
    add_strip(e1, 1)
    receive_piece(5)
    spread_rows(6)
    open_first(0)
    receive_piece(6)
    spread_rows(7)
    add_strip(e1, 2)
    receive_piece(7)
    add_strip(e1, 3)
    copies1 = share_sums(0)
    for strip in range(1, STRIPS):
        open_first(strip)
    for c in range(PIECES):
        forward(c).wait_send()
    weigh(0, copies1)

    def write_first(p, r, value):
        e2[p + 4, r] = value

    def up2(c):
        at = piece_rows(c)
        return send(give_cross.at[:, at], got2.at[0, :, at], y2_s.at[0, c], y2_r.at[0, c], at_pair(1))

    def down2(c):
        at = piece_rows(c)
        return send(give_keep.at[:, at], got2.at[1, :, at], y2_s.at[1, c], y2_r.at[1, c], at_pair(-1))

    def first_strip(strip):
        apply(e1, strip * STRIP, STRIP, 1.0 / 6.0, write_first)

        def pack(n, inner):
            r = strip * STRIP + n
            for j in range(2):
                near, turned = e2[4 + j, r], swap(e2[6 + j, r])
                give_cross[j, r] = jnp.where(lower, turned, near)
                give_keep[j, r] = jnp.where(lower, near, turned)
            return inner

        lax.fori_loop(0, STRIP, pack, 0)
        for c in range(2 * strip, 2 * strip + 2):
            if c < WINDOW:
                up2(c).start()
                down2(c).start()
        add_strip(e2, strip)

    for strip in range(STRIPS):
        first_strip(strip)
    copies2 = share_sums(1)
    weigh(1, copies2)

    def write_second(p, r, value):
        second[p, r] = value - e1[p + 4, r]

    def give(index, part):
        src = second.at[index // 2, pl.ds(lax.rem(index, 2) * 16 + part * PIECE, PIECE)]
        return send(src, slab.at[rank, pl.ds(part * PIECE, PIECE)], out_s.at[index, part], out_r.at[rank, part],
                    member(index))

    def own_part(part):
        src = second.at[rank // 2, pl.ds(lax.rem(rank, 2) * 16 + part * PIECE, PIECE)]
        return pltpu.make_async_copy(src, slab.at[rank, pl.ds(part * PIECE, PIECE)], self_s.at[part])

    def second_piece(c):
        for copy in (up2(c), down2(c)):
            copy.wait_recv()
            copy.wait_send()
        if c + WINDOW < PIECES:
            up2(c + WINDOW).start()
            down2(c + WINDOW).start()
        open_rows(e2, got2, c * PIECE, PIECE)
        apply(e2, c * PIECE, PIECE, 1.0 / 3.0, write_second)
        row_half, part = c // 4, c % 4
        for n in range(4):
            index = 2 * lax.rem(n + rank // 2 + 2, 4) + row_half
            pl.when(index != rank)(lambda index=index: give(index, part).start())
        pl.when(lax.rem(rank, 2) == row_half)(own_part(part).start)

    for c in range(PIECES):
        second_piece(c)

    blocks = tri_blocks(NORB)
    pack[...] = jnp.zeros_like(pack)

    def repack(n, carry):
        cells = pl.ds(pl.multiple_of(n * DEPTH, 16), DEPTH)
        more = pl.ds(pl.multiple_of(CELLS // 2 + n * DEPTH, 16), DEPTH)
        for b in range(4):
            at = slice(b * WIDE, (b + 1) * WIDE)
            here, there = slab[b, n], slab[4 + b, n]
            high_cells[cells, at], low_cells[cells, at] = split(jnp.where(lower, here, swap(there)))
            high_cells[more, at], low_cells[more, at] = split(jnp.where(lower, swap(here), there))
        return carry

    def add_gram(part):
        contract = (((0,), (0,)), ((), ()))

        def chunk(side, carry):
            cells = pl.ds(pl.multiple_of(side * (CELLS // 2) + part * AREA, 16), AREA)
            for i in range(NORB // B):
                own, wide = slice(i * B, (i + 1) * B), slice(0, (i + 1) * B)
                row = lax.dot_general(
                    high_cells[cells, own], high_cells[cells, wide], contract, preferred_element_type=jnp.float32)
                row += lax.dot_general(
                    high_cells[cells, own], low_cells[cells, wide], contract, preferred_element_type=jnp.float32)
                row += lax.dot_general(
                    low_cells[cells, own], high_cells[cells, wide], contract, preferred_element_type=jnp.float32)
                for j in range(i + 1):
                    n = blocks.index((i, j))
                    pack[n * B : (n + 1) * B, :] += row[:, j * B : (j + 1) * B]
            return carry

        lax.fori_loop(0, 2, chunk, 0)

    for section in range(2):
        for part in (2 * section, 2 * section + 1):
            for n in range(1, GROUP):
                index = lax.rem(rank + n, GROUP)
                send(second.at[0, pl.ds(0, PIECE)], slab.at[index, pl.ds(part * PIECE, PIECE)],
                     out_s.at[index, part], out_r.at[index, part], member(index)).wait_recv()
            own_part(part).wait()
            lax.fori_loop(part * PIECE, (part + 1) * PIECE, repack, 0)
        add_gram(section)

    for copy in small + [across, last] + onward + copies1 + copies2:
        copy.wait_send()
    for n in range(1, GROUP):
        for part in range(4):
            give(lax.rem(rank + n, GROUP), part).wait_send()
    finish_part(factor, gram_ref, filtered_ref, high_cells, low_cells, pack, *rest[:5], second, *rest[5:])


def run(orbitals, potential, projectors, coupling, atom_plane, projector_count, factor):
    dma = pltpu.SemaphoreType.DMA
    f32, bf16 = jnp.float32, jnp.bfloat16
    smem = pl.BlockSpec(memory_space=pltpu.SMEM)
    vmem, hbm = pl.BlockSpec(memory_space=pltpu.VMEM), pl.BlockSpec(memory_space=pl.ANY)
    block = (ROWS, DEPTH, WIDE)
    packed = len(tri_blocks(NORB)) * B
    share = packed // NEAR
    return pl.pallas_call(
        functools.partial(whole_kernel, factor),
        out_shape=[jax.ShapeDtypeStruct((NORB, NORB), f32), jax.ShapeDtypeStruct((4,) + block, f32)],
        in_specs=[hbm, vmem, vmem, vmem, smem, smem],
        out_specs=[vmem, hbm],
        scratch_shapes=[
            pltpu.VMEM((12,) + block, f32),
            pltpu.VMEM((12,) + block, f32),
            pltpu.VMEM((4,) + block, f32),
            pltpu.VMEM((4,) + block, f32),
            pltpu.VMEM((STRIP, DEPTH, WIDE), f32),
            pltpu.VMEM((4, STRIPS, 256, AREA), bf16),
            pltpu.VMEM((4, CELLS, 512), bf16),
            pltpu.VMEM((3, PROJ, SPAN * CELLS), f32),
            pltpu.VMEM((3, PROJ, 128), f32),
            pltpu.VMEM((PROJ, MAXPROJ), f32),
            pltpu.VMEM((8, ROWS, DEPTH), f32),
            pltpu.VMEM((256, 2 * WIDE), f32),
            pltpu.VMEM((2, 3, PROJ, WIDE), f32),
            pltpu.VMEM((2, 2, PROJ, WIDE), f32),
            pltpu.VMEM((512, WIDE), bf16),
            pltpu.VMEM((2,) + block, f32),
            pltpu.VMEM((2,) + block, f32),
            pltpu.VMEM((2,) + block, f32),
            pltpu.VMEM((2, 2) + block, f32),
            pltpu.VMEM((2, 2) + block, f32),
            pltpu.VMEM((GROUP, ROWS // 2, DEPTH, WIDE), f32),
            dma((4,)), dma((PIECES,)), dma((PIECES,)), dma((PIECES,)), dma((PIECES,)), dma((2, PIECES)),
            dma((3,)), dma((3,)), dma(()), dma(()), dma((2,)), dma((2,)), dma(()), dma(()),
            dma((2, 2)), dma((2, 2)), dma((2, PIECES)), dma((2, PIECES)),
            dma((GROUP, 4)), dma((GROUP, 4)), dma((4,)),
            pltpu.VMEM((CELLS, NORB), bf16),
            pltpu.VMEM((CELLS, NORB), bf16),
            pltpu.VMEM((packed, B), f32),
            pltpu.VMEM((NEAR, share, B), f32),
            pltpu.VMEM((share, B), f32),
            pltpu.VMEM((FAR, share // SUMMERS, B), f32),
            pltpu.VMEM((packed, B), f32),
            pltpu.VMEM((NORB, NORB), f32),
            dma((NEAR,)), dma((NEAR,)), dma((FAR,)), dma((FAR,)),
            dma((FAR,)), dma((FAR,)), dma((NEAR,)), dma((NEAR,)),
            dma(()), dma((4, 2)), dma((NEAR,)),
        ],
        compiler_params=pltpu.CompilerParams(collective_id=2, has_side_effects=True, vmem_limit_bytes=62 * 2**20),
    )(orbitals, potential, projectors, coupling, atom_plane, projector_count)


def settle_kernel(gram, filtered, gram_out, filtered_out, sems):
    copies = [pltpu.make_async_copy(filtered.at[p], filtered_out.at[p], sems.at[p]) for p in range(4)]
    copies.append(pltpu.make_async_copy(gram, gram_out, sems.at[4]))
    for copy in copies:
        copy.start()
    for copy in copies:
        copy.wait()


def settle(gram, filtered):
    hbm = pl.BlockSpec(memory_space=pl.ANY)
    return pl.pallas_call(
        settle_kernel,
        out_shape=[jax.ShapeDtypeStruct(x.shape, x.dtype) for x in (gram, filtered)],
        in_specs=[hbm, hbm],
        out_specs=[hbm, hbm],
        scratch_shapes=[pltpu.SemaphoreType.DMA((5,))],
        compiler_params=pltpu.CompilerParams(vmem_limit_bytes=8 * 2**20),
    )(gram, filtered)


def shards(orbitals, potential, projectors, coupling, atom_plane, projector_count):
    planes, side_y, side_z, _ = orbitals.shape
    total_cells = planes * side_y * side_z * lax.axis_size("dom")
    gram, filtered = run(
        orbitals, potential, projectors, coupling, atom_plane, projector_count, 1.0 / total_cells)
    gram, filtered = settle(gram, filtered)
    return (filtered, gram)


def solution(mesh):
    placed = (
        P("dom", None, None, "band"),
        P("dom", None, None),
        P("dom", None, None),
        P("dom", None, None),
        P("dom"),
        P("dom"),
    )
    return jax.shard_map(
        shards,
        mesh=mesh,
        in_specs=placed,
        out_specs=(P("dom", None, None, "band"), P()),
        check_vma=False,
    )
```
